128 devices in a mesh: rows: 4 (over z_lo, core), blk: 32 (over x, y, z_hi).
Axes of the slice: x: 4, y: 4, z: 4 (z_hi: 2, z_lo: 2; z = z_hi * 2 + z_lo), core: 2. Of those that a mesh axis runs over, the one named last changes fastest.
Arguments:
- tokens: bfloat16 [8, 2048, 1024], P('rows', 'blk'), may hold values from -6 to 6
- lengths: int32 [8], P('rows'), may hold values from 128 to 2048, as said below
- routes: int32 [8, 2048, 8], P('rows', 'blk'), may hold values from 0 to 31, all different within a row; in each aligned block of 64 rows (0 to 63, 64 to 127, ..., all dimensions but the last counted through in order) at most 24 rows name the same one
- gates: float32 [8, 2048, 8], P('rows', 'blk'), may hold values from 0.05 to 0.25
- gain_attn: float32 [1024], replicated, may hold values from 0.5 to 1.5
- w_qkv: bfloat16 [1024, 2048], replicated, may hold values from -0.1875 to 0.1875
- w_out: bfloat16 [1024, 1024], replicated, may hold values from -0.75 to 0.75
- gain_moe: float32 [1024], replicated, may hold values from 0.5 to 1.5
- w_gate_up: bfloat16 [32, 1024, 1024], P('blk'), may hold values from -0.1875 to 0.1875
- w_down: bfloat16 [32, 512, 1024], P('blk'), may hold values from -1 to 1
- cotangent: bfloat16 [8, 2048, 1024], P('rows', 'blk'), may hold values from -6 to 6
Outputs:
- mixed_out: bfloat16 [8, 2048, 1024], P('rows', 'blk')
- grad_tokens: float32 [8, 2048, 1024], P('rows', 'blk')
- grad_gain_attn: float32 [1024], replicated
- grad_qkv: float32 [1024, 2048], replicated
- grad_out: float32 [1024, 1024], replicated
- grad_gain_moe: float32 [1024], replicated
- grad_gate_up: float32 [32, 1024, 1024], P('blk')
- grad_down: float32 [32, 512, 1024], P('blk')
The draws below stay inside these ranges and needn't reach their ends.
Inputs may be any that keep to these rules, and one draw needn't show every extreme that they name: `routes`: within each aligned block of 64 tokens of one sequence, no expert is named by more than 24 tokens; a token names 8 different experts. `lengths`: in each group of 2 consecutive sequences one, drawn from the seed, has length 2048; the others are shorter.
All inputs are finite; a program needn't handle non-finite values.
Results may differ from the reference program's by a relative error of at most 0.02.
Values may be sent and summed in bfloat16 or wider, within the bound.
No kernel may reach another device: no remote copies, remote signals or barrier semaphores. Data moves between devices by JAX's collectives and lax.ppermute only.
A program may use at most 128 MiB of HBM per device.

```python
import math
import jax
import jax.numpy as jnp
import numpy as np
from jax import lax

D = 1024
HEADS = 16
KV_HEADS = 8
HEAD = 64
FF_EXP = 512
TOP = 8
SEQ_GRP = 2
LEN = 2048
TOK = 64
SEQS = 8
EXPERTS = 32
MOST = 24
N_BLK = 32


def draw_lengths(key, part):
    key = jax.random.fold_in(key, 7)
    key_pick, key_short = jax.random.split(key)
    group_count = SEQS // SEQ_GRP
    picked = jax.random.randint(key_pick, (group_count,), 0, SEQ_GRP)
    shorter = jax.random.randint(key_short, (group_count, SEQ_GRP), LEN // 16, LEN)
    is_full = jnp.arange(SEQ_GRP)[None, :] == picked[:, None]
    return jnp.where(is_full, LEN, shorter).reshape(SEQS).astype(jnp.int32)


def shard_levels(key, extent, pieces, smallest, high):
    def one(position, shards_of):
        steps = jax.random.uniform(jax.random.fold_in(jax.random.fold_in(key, 6), position), (shards_of,), jnp.float32, smallest / len(pieces), high / len(pieces))
        return jnp.repeat(jnp.exp(steps), extent[position] // shards_of).reshape((-1,) + (1,) * (len(extent) - position - 1))

    gain = one(*pieces[0])
    for cut in pieces[1:]:
        gain = gain * one(*cut)
    return gain


def assign_block(key, own, number, rows, number_of, top, bound, lean):
    order = jax.random.permutation(key, number_of)
    crowded, common = load_shares(number_of, rows * top, bound, lean, True), load_shares(number_of, rows * top, bound, lean, False)
    places = jnp.arange(number_of)

    def named(sizes, offset_by):
        used = int((sizes > 0).sum())
        fixed = max(1, used // 4)
        shifted = fixed + (places - fixed + offset_by * (used - fixed)) % max(1, number_of - fixed)
        return jnp.zeros((number_of,), jnp.int32).at[order[jnp.where(places < fixed, places, shifted)]].set(jnp.asarray(sizes, jnp.int32))

    sizes = jnp.where(number % 4 == 0, named(crowded, number // 4), named(common, number - number // 4 - 1))
    mixed = jax.random.permutation(jax.random.fold_in(own, 3), number_of)
    donor, sink = mixed[0:number_of // 2 * 2:2], mixed[1:number_of // 2 * 2:2]
    room = jnp.minimum(sizes[donor] - 1, bound - sizes[sink]) // 2
    room = jnp.where((donor == order[0]) | (sink == order[0]) | (sizes[sink] == 0), 0, jnp.maximum(room, 0))
    shifted = jax.random.randint(jax.random.fold_in(own, 4), (number_of // 2,), 0, 1 << 20) % (room + 1)
    sizes = sizes.at[donor].add(-shifted).at[sink].add(shifted)
    members = jnp.searchsorted(jnp.cumsum(sizes), jnp.arange(rows * top), side="right").astype(jnp.int32)
    listing = members.reshape(top, rows).T
    listing = listing[jax.random.permutation(jax.random.fold_in(own, 1), rows)]
    offset_by = jax.random.randint(jax.random.fold_in(own, 2), (rows, 1), 0, top)
    return jnp.take_along_axis(listing, (jnp.arange(top)[None, :] + offset_by) % top, axis=1)


def load_shares(count, total, limit, lean, full):
    weights = [(1 << 20) // math.isqrt(grade ** lean) + 1 for grade in range(1, count + 1)]
    largest = limit if full else min(limit, max(-(-total // count), total * weights[0] // sum(weights)))
    least = 1 if total - largest >= count - 1 else 0
    counts, rest = [largest] + [least] * (count - 1), total - largest - least * (count - 1)
    while rest > 0:
        candidates = [i for i in range(1, count) if counts[i] < largest] or [i for i in range(1, count) if counts[i] < limit]
        mass, budget = sum([weights[i] for i in candidates]), rest
        for i in candidates:
            addition = min(limit - counts[i], max(1, budget * weights[i] // mass), rest)
            counts[i] = counts[i] + addition
            rest = rest - addition
    return np.array(counts)


def noise(rng, dims, deviation, bound, cuts=(), kind=jnp.bfloat16):
    level = shard_levels(rng, dims, cuts, -0.22, 0.18) if cuts else 1.0
    array = jax.random.normal(rng, dims, jnp.float32) * deviation * level
    return jnp.minimum(jnp.maximum(array, -bound), bound).astype(kind)


def setup_inputs(seed: int = 0) -> dict:
    keys = jax.random.split(jax.random.key(seed), 12)
    tokens = noise(keys[0], (SEQS, LEN, D), 1.0, 6.0, ((0, 4), (1, 32)))
    lengths = draw_lengths(jax.random.fold_in(keys[11], 71), 0)
    routes_keys = jax.random.split(jax.random.fold_in(keys[2], 1), SEQS * LEN // TOK)
    routes_turns = jax.random.permutation(jax.random.fold_in(keys[2], 3), SEQS * LEN // TOK)
    routes = jax.vmap(lambda own, number: assign_block(jax.random.fold_in(keys[2], 2), own, number, TOK, EXPERTS, TOP, MOST, 1))(routes_keys, routes_turns).reshape((SEQS, LEN, TOP))
    gates = jnp.clip(jnp.exp(math.log(0.25) - 1.609438 * jax.random.uniform(keys[3], (SEQS, LEN, TOP), jnp.float32) ** shard_levels(keys[3], (SEQS, LEN, TOP), ((0, 4), (1, 32)), -0.2, 0.2)), 0.05, 0.25)
    gain_attn = jnp.clip(1.0 + 0.1 * jax.random.normal(keys[4], (D,), jnp.float32), 0.5, 1.5)
    w_qkv = noise(keys[5], (D, HEADS * HEAD + 2 * KV_HEADS * HEAD), D ** -0.5, 0.1875)
    w_out = noise(keys[6], (HEADS * HEAD, D), (D // 16) ** -0.5, 0.75)
    gain_moe = jnp.clip(1.0 + 0.1 * jax.random.normal(keys[7], (D,), jnp.float32), 0.5, 1.5)
    w_gate_up = noise(keys[8], (EXPERTS, D, 2 * FF_EXP), D ** -0.5, 0.1875, ((0, 32),))
    w_down = noise(keys[9], (EXPERTS, FF_EXP, D), (FF_EXP // 16) ** -0.5, 1.0, ((0, 32),))
    cotangent = noise(keys[10], (SEQS, LEN, D), 1.0, 6.0, ((0, 4), (1, 32)))
    return dict(tokens=tokens, lengths=lengths, routes=routes, gates=gates, gain_attn=gain_attn, w_qkv=w_qkv, w_out=w_out, gain_moe=gain_moe, w_gate_up=w_gate_up, w_down=w_down, cotangent=cotangent)


EPS = 1e-06
ROPE_BASE = 10000.0

@jax.custom_vjp
def low(v):
    return lax.optimization_barrier(v.astype(jnp.bfloat16)).astype(jnp.float32)

@jax.custom_vjp
def low_back(v):
    return v

def low_keep(v):
    return (low(v), None)

def low_pass(kept, grad):
    return (grad,)

def back_keep(v):
    return (v, None)

def back_low(kept, grad):
    return (low(grad),)
low.defvjp(low_keep, low_pass)
low_back.defvjp(back_keep, back_low)

def product(left, right):
    return jnp.dot(left, right, precision=lax.Precision.HIGHEST, preferred_element_type=jnp.float32)

def norm_rows(vectors, gain_vec):
    return vectors * lax.rsqrt(lax.optimization_barrier(jnp.mean(vectors * vectors, axis=-1, keepdims=True)) + EPS) * gain_vec

def rotate(vectors, positions):
    half_head = HEAD // 2
    frequency = ROPE_BASE ** (-jnp.arange(half_head, dtype=jnp.float32) / half_head)
    angles = positions.astype(jnp.float32)[:, None] * frequency[None, :]
    cosine = jnp.cos(angles)[:, None, :]
    sine_table = jnp.sin(angles)[:, None, :]
    front_half = vectors[..., :half_head]
    back_half = vectors[..., half_head:]
    return jnp.concatenate([front_half * cosine - back_half * sine_table, back_half * cosine + front_half * sine_table], -1)

def attention(queries, key_rows, value_rows, seq_length):
    groups = HEADS // KV_HEADS
    block_rows = min(512, LEN)
    query_blocks = queries.reshape(LEN // block_rows, block_rows, KV_HEADS, groups, HEAD)
    starts = jnp.arange(LEN // block_rows, dtype=jnp.int32) * block_rows
    key_pos = jnp.arange(LEN, dtype=jnp.int32)

    def one_block(operands):
        query_part, start = operands
        query_pos = start + jnp.arange(block_rows, dtype=jnp.int32)
        scores = jnp.einsum('tkgd,jkd->kgtj', query_part, key_rows, precision=lax.Precision.HIGHEST) * HEAD ** (-0.5)
        allowed = (key_pos[None, :] <= query_pos[:, None]) & (key_pos[None, :] < seq_length)
        scores = low_back(jnp.where(allowed, scores, -1e+30))
        soft_weights = low(jax.nn.softmax(scores, axis=-1))
        attended = jnp.einsum('kgtj,jkd->tkgd', soft_weights, value_rows, precision=lax.Precision.HIGHEST)
        return attended.reshape(block_rows, HEADS * HEAD)
    result = lax.map(jax.checkpoint(one_block), (query_blocks, starts))
    return result.reshape(LEN, HEADS * HEAD)

def experts_apply(normed_moe, seq_routes, seq_gates, w_gu, w_dn):
    flat_routes = seq_routes.reshape(-1)
    ordering = jnp.argsort(flat_routes, stable=True).astype(jnp.int32)
    expert_ids = jnp.arange(EXPERTS, dtype=jnp.int32)
    expert_load = lax.optimization_barrier(jnp.sum((flat_routes[:, None] == expert_ids[None, :]).astype(jnp.int32), axis=0))
    offsets = jnp.cumsum(expert_load) - expert_load
    slot_count = N_BLK * MOST
    slot_ids = jnp.arange(slot_count, dtype=jnp.int32)
    is_live = slot_ids[None, :] < expert_load[:, None]
    positions = jnp.minimum(offsets[:, None] + slot_ids[None, :], LEN * TOP - 1)
    sources = ordering[positions]
    token_ids = sources // TOP
    slot_gate = jnp.where(is_live, seq_gates.reshape(-1)[sources], 0.0)
    gathered = low_back(normed_moe[token_ids])
    pre_act = low_back(jnp.einsum('ecd,edf->ecf', gathered, w_gu, precision=lax.Precision.HIGHEST))
    gate_part = pre_act[..., :FF_EXP]
    up_part = pre_act[..., FF_EXP:]
    hidden = low(jax.nn.silu(gate_part) * up_part)
    expert_out = low_back(low(jnp.einsum('ecf,efd->ecd', hidden, w_dn, precision=lax.Precision.HIGHEST)))
    weighted = (slot_gate[..., None] * expert_out).reshape(-1, D)
    return jnp.zeros((LEN, D), jnp.float32).at[token_ids.reshape(-1)].add(weighted)

def layer_seq(seq_tokens, seq_length, seq_routes, seq_gates, weights_all):
    gain_a, wqkv, wout, gain_m, wgu, wdn = weights_all
    positions = jnp.arange(LEN, dtype=jnp.int32)
    q_width = HEADS * HEAD
    kv_width = KV_HEADS * HEAD
    normed = low(norm_rows(seq_tokens, gain_a))
    projected = low_back(product(normed, wqkv))
    queries = low(rotate(projected[:, :q_width].reshape(LEN, HEADS, HEAD), positions))
    key_rows = low(rotate(projected[:, q_width:q_width + kv_width].reshape(LEN, KV_HEADS, HEAD), positions))
    value_rows = low(projected[:, q_width + kv_width:].reshape(LEN, KV_HEADS, HEAD))
    attended = low_back(low(attention(queries, key_rows, value_rows, seq_length)))
    residual = seq_tokens + low_back(product(attended, wout))
    normed_moe = low(norm_rows(residual, gain_m))
    return residual + experts_apply(normed_moe, seq_routes, seq_gates, wgu, wdn)

def reference(tokens, lengths, routes, gates, gain_attn, w_qkv, w_out, gain_moe, w_gate_up, w_down, cotangent):
    weights_all = (gain_attn, w_qkv.astype(jnp.float32), w_out.astype(jnp.float32), gain_moe, w_gate_up.astype(jnp.float32), w_down.astype(jnp.float32))

    def layer_all(inputs, weights_now):

        def per_sequence(carried, operands):
            seq_tokens, seq_length, seq_routes, seq_gates = operands
            return (carried, layer_seq(seq_tokens, seq_length, seq_routes, seq_gates, weights_now))
        carried, outputs = lax.scan(jax.checkpoint(per_sequence), jnp.zeros((), jnp.float32), (inputs, lengths, routes, gates))
        return outputs
    outputs, pullback = jax.vjp(layer_all, tokens.astype(jnp.float32), weights_all)
    grad_inputs, grad_weights = pullback(cotangent.astype(jnp.float32))
    return (outputs.astype(jnp.bfloat16), grad_inputs, grad_weights[0], grad_weights[1], grad_weights[2], grad_weights[3], grad_weights[4], grad_weights[5])
```

```python
import jax
import jax.numpy as jnp
import numpy as np
from jax import lax
from jax.experimental import pallas as pl
from jax.experimental.pallas import tpu as pltpu
from jax.sharding import Mesh
from jax.sharding import PartitionSpec as P

HEADS = 16
KV_HEADS = 8
HEAD = 64
FF_EXP = 512
TOP = 8
MOST = 24
EPS = 1e-06
ROPE_BASE = 10000.0
SCALE = HEAD ** (-0.5)

ROWS = ("zl", "core")
BLK = ("x", "y", "zh")
CHIPS = ("zl", "x", "y", "zh")
AXES = ("zl", "core", "x", "y", "zh")
SWAP = [(0, 1), (1, 0)]
EXPERT_GROUPS = [
    [(parity ^ zh) * 32 + xy * 2 + zh for xy in range(16) for zh in range(2)] for parity in range(2)
]
Z_PAIRS = [(i, 3 - i) for i in range(4)]
F32 = jnp.float32
BF16 = jnp.bfloat16
NT = (((1,), (1,)), ((), ()))
TN = (((0,), (0,)), ((), ()))


def dot(left, right, dims=(((1,), (0,)), ((), ()))):
    return lax.dot_general(left, right, dims, preferred_element_type=F32)


def call(
    kernel,
    grid,
    in_specs,
    out_specs,
    out_shape,
    scratch=(),
    mb=24,
    flops=0,
    moved=0,
    deps=(),
    scalars=0,
    aliases=None,
):
    count = len(in_specs) + scalars

    def body(*refs):
        kernel(*refs[:count], *refs[count + len(deps) :])

    built = pl.pallas_call(
        body,
        grid_spec=pltpu.PrefetchScalarGridSpec(
            num_scalar_prefetch=scalars,
            grid=grid,
            in_specs=[*in_specs, *[pl.BlockSpec(memory_space=pl.ANY)] * len(deps)],
            out_specs=out_specs,
            scratch_shapes=list(scratch),
        ),
        out_shape=out_shape,
        input_output_aliases=aliases or {},
        compiler_params=pltpu.CompilerParams(vmem_limit_bytes=mb * 1024 * 1024),
        cost_estimate=pl.CostEstimate(flops=flops, bytes_accessed=moved, transcendentals=0),
    )
    return lambda *operands: built(*operands, *deps)


def after(x, *deps):
    any_space = pl.BlockSpec(memory_space=pl.ANY)
    return pl.pallas_call(
        lambda *refs: None,
        in_specs=[any_space] * (1 + len(deps)),
        out_specs=any_space,
        out_shape=sds(x.shape, x.dtype),
        input_output_aliases={0: 0},
    )(x, *deps)


def whole(*shape):
    return pl.BlockSpec(shape, lambda *_: (0,) * len(shape))


def sds(shape, dtype):
    return pltpu.HBM(shape, dtype)


def low_half(shape):
    return lax.broadcasted_iota(jnp.int32, shape, len(shape) - 1) < HEAD


def swap_halves(u):
    lane = lax.broadcasted_iota(jnp.int32, u.shape, 1)
    return jnp.where(lane % HEAD < HEAD // 2, pltpu.roll(u, 96, 1), pltpu.roll(u, 32, 1))


def pre_kernel(tok, gain, wq, wk, wv, cos, sin, h_ref, send):
    @pl.when(pl.program_id(0) == 0)
    def _():
        x = tok[...].astype(F32)
        inverse = lax.rsqrt(jnp.mean(x * x, axis=-1, keepdims=True) + EPS)
        h_ref[...] = (x * inverse * gain[...]).astype(BF16)

    h = h_ref[...]
    c = jnp.concatenate([cos[...], cos[...]], 0)
    s = jnp.concatenate([sin[...], sin[...]], 0)

    def rope(u):
        return u * c + swap_halves(u) * s

    q = dot(h, wq[...])
    k = rope(dot(h, wk[...]))
    v = dot(h, wv[...])
    low = low_half(k.shape)
    pairs = (
        jnp.where(low, k, pltpu.roll(v, HEAD, 1)).astype(BF16),
        jnp.where(low, pltpu.roll(k, HEAD, 1), v).astype(BF16),
    )
    for j in range(2):
        qj = (rope(q[:, j * 128 : (j + 1) * 128]).astype(BF16).astype(F32) * SCALE).astype(BF16)
        for t in range(2):
            for half in range(2):
                first = t * 64 + half * 32
                send[t, j, half, 0:32, :] = qj[first : first + 32]
                send[t, j, half, 32:96, :] = pairs[j][t * 64 : t * 64 + 64]


def pre(tok, gain, w_qkv, cos, sin):
    return call(
        pre_kernel,
        (4,),
        [
            whole(128, 1024),
            whole(1, 1024),
            pl.BlockSpec((1024, 256), lambda m: (0, m)),
            pl.BlockSpec((1024, 128), lambda m: (0, 8 + m)),
            pl.BlockSpec((1024, 128), lambda m: (0, 12 + m)),
            whole(64, 128),
            whole(64, 128),
        ],
        [whole(128, 1024), pl.BlockSpec((2, 2, 2, 96, 128), lambda m: (0, m, 0, 0, 0))],
        [sds((128, 1024), BF16), sds((2, 8, 2, 96, 128), BF16)],
        flops=2 * 128 * 1024 * 2048,
        moved=5 << 20,
    )(tok, gain, w_qkv, w_qkv, w_qkv, cos, sin)


def plan_kernel(routes, gates, dz, pos_ref, gate_ref, out):
    named = routes[...].astype(F32).T
    weights = gates[...].T
    experts = lax.broadcasted_iota(jnp.int32, (32, 128), 0).astype(F32)
    chosen = jnp.zeros((32, 128), F32)
    gate = jnp.zeros((32, 128), F32)
    for k in range(TOP):
        match = named[k : k + 1] == experts
        chosen = jnp.where(match, 1.0, chosen)
        gate = jnp.where(match, weights[k : k + 1], gate)
    row = lax.broadcasted_iota(jnp.int32, (128, 128), 0)
    before = jnp.where(row < lax.broadcasted_iota(jnp.int32, (128, 128), 1), 1.0, 0.0)
    rank = dot(chosen.astype(BF16), before.astype(BF16))
    pos = jnp.where(chosen > 0.0, rank, -1.0)
    pos_ref[...] = pos.astype(jnp.int32)
    gate_ref[...] = gate
    high = gate.astype(BF16).astype(F32)
    rest = gate - high
    out[0:128, :] = dz[...]
    for j in range(8):
        part = slice(4 * j, 4 * j + 4)
        tile = jnp.concatenate([pos[part], high[part], rest[part], jnp.zeros((4, 128), F32)], 0)
        out[128:144, j * 128 : (j + 1) * 128] = tile.astype(BF16)


def plan(routes, gates, dz, deps):
    return call(
        plan_kernel,
        (1,),
        [whole(128, 8), whole(128, 8), whole(128, 1024)],
        [whole(32, 128), whole(32, 128), whole(144, 1024)],
        [sds((32, 128), jnp.int32), sds((32, 128), F32), sds((144, 1024), BF16)],
        moved=1 << 20,
        deps=deps,
    )(routes, gates, dz)


def split_queries(q):
    qf = q.astype(F32)
    low = low_half(qf.shape)
    first = jnp.where(low, qf, 0.0)
    second = jnp.where(low, pltpu.roll(qf, HEAD, 1), 0.0)
    return jnp.concatenate([first, second], 0).astype(BF16)


def limits(tile, info):
    place = lax.broadcasted_iota(jnp.int32, (1, 512), 1) % 256
    position = (tile * 8 + place // 32) * 64 + info[1] * 32 + place % 32
    return jnp.minimum(position, info[0] - 1)


def load_pairs(x_ref, kv, kvt):
    kv[...] = x_ref[:, 32:96, :].reshape(2048, 128)
    for c in range(8):
        rows = slice(c * 256, (c + 1) * 256)
        kvt[:, rows] = kv[rows, :].astype(F32).T.astype(BF16)


def attend_kernel(info, x_ref, o_ref, ot_ref, lse_ref, kv, kvt):
    load_pairs(x_ref, kv, kvt)
    for tile in range(4):
        q2 = split_queries(x_ref[tile * 8 : (tile + 1) * 8, 0:32, :].reshape(256, 128))
        limit = limits(tile, info)

        def step(c, carry):
            top, total, acc = carry
            at = pl.ds(pl.multiple_of(c * 512, 512), 512)
            s = dot(kv[at, :], q2, NT)
            place = c * 512 + lax.broadcasted_iota(jnp.int32, (512, 1), 0)
            s = jnp.where(place <= limit, s, -1e30)
            new_top = jnp.maximum(top, jnp.max(s, axis=0, keepdims=True))
            shrink = jnp.exp(top - new_top)
            p = jnp.exp(s - new_top)
            total = total * shrink + jnp.sum(p, axis=0, keepdims=True)
            return new_top, total, acc * shrink + dot(kvt[64:128, at], p.astype(BF16))

        start = (jnp.full((1, 512), -1e30, F32), jnp.zeros((1, 512), F32), jnp.zeros((64, 512), F32))
        top, total, acc = lax.fori_loop(0, tile + 1, step, start)
        out = acc / total
        ot_ref[tile] = out
        lse_ref[tile] = jnp.broadcast_to(top + jnp.log(total), (8, 512))
        both = jnp.concatenate([out[:, :256], out[:, 256:]], 0).T
        o_ref[tile * 8 : (tile + 1) * 8] = both.astype(BF16).reshape(8, 32, 128)


def attend(info, arrived, deps):
    return call(
        attend_kernel,
        (1,),
        [pl.BlockSpec(memory_space=pltpu.SMEM), whole(32, 96, 128)],
        [whole(32, 32, 128), whole(4, 64, 512), whole(4, 8, 512)],
        [sds((32, 32, 128), BF16), sds((4, 64, 512), F32), sds((4, 8, 512), F32)],
        [pltpu.VMEM((2048, 128), BF16), pltpu.VMEM((128, 2048), BF16)],
        flops=4 * 2048 * 1280 * 128,
        moved=2 << 20,
        deps=deps,
    )(info, arrived)


def attend_back_kernel(info, x_ref, do_ref, ot_ref, lse_ref, out_ref, gain_ref, kv, kvt, total):
    load_pairs(x_ref, kv, kvt)
    total[...] = jnp.zeros_like(total)
    for tile in range(4):
        q2 = split_queries(x_ref[tile * 8 : (tile + 1) * 8, 0:32, :].reshape(256, 128))
        grad = do_ref[tile * 8 : (tile + 1) * 8, 0:32, :].reshape(256, 128).astype(F32)
        low = low_half(grad.shape)
        do2 = jnp.concatenate(
            [jnp.where(low, 0.0, pltpu.roll(grad, HEAD, 1)), jnp.where(low, 0.0, grad)], 0
        ).astype(BF16)
        grad_t = grad.T
        grad_t = jnp.concatenate([grad_t[:64], grad_t[64:]], 1)
        inner = jnp.sum(grad_t * ot_ref[tile], axis=0, keepdims=True)
        lse = lse_ref[tile][0:1]
        limit = limits(tile, info)

        def step(c, acc):
            at = pl.ds(pl.multiple_of(c * 256, 256), 256)
            part = kv[at, :]
            s = dot(part, q2, NT)
            place = c * 256 + lax.broadcasted_iota(jnp.int32, (256, 1), 0)
            p = jnp.exp(jnp.where(place <= limit, s, -1e30) - lse)
            ds = (p * (dot(part, do2, NT) - inner)).astype(BF16)
            total[at, :] += dot(ds, q2) + dot(p.astype(BF16), do2)
            return acc + dot(kvt[0:64, at], ds)

        acc = lax.fori_loop(0, 2 * tile + 2, step, jnp.zeros((64, 512), F32))
        dq = jnp.concatenate([acc[:, :256], acc[:, 256:]], 0).T
        out_ref[tile * 8 : (tile + 1) * 8, 0:32, :] = dq.astype(BF16).reshape(8, 32, 128)
    out_ref[:, 32:96, :] = total[...].astype(BF16).reshape(32, 64, 128)
    gains = jnp.sum(do_ref[:, 32:48, :].astype(F32), axis=0)
    gain_ref[...] = gains[:8] + gains[8:]


def attend_back(info, arrived, grad, ot, lse, deps):
    return call(
        attend_back_kernel,
        (1,),
        [
            pl.BlockSpec(memory_space=pltpu.SMEM),
            whole(32, 96, 128),
            whole(32, 48, 128),
            whole(4, 64, 512),
            whole(4, 8, 512),
        ],
        [whole(32, 96, 128), whole(8, 128)],
        [sds((32, 96, 128), BF16), sds((8, 128), F32)],
        [pltpu.VMEM((2048, 128), BF16), pltpu.VMEM((128, 2048), BF16), pltpu.VMEM((2048, 128), F32)],
        flops=10 * 2048 * 1280 * 128,
        moved=3 << 20,
        deps=deps,
    )(info, arrived, grad, ot, lse)


def placement(pos):
    slots = lax.broadcasted_iota(jnp.int32, (8, 48, 128), 1)
    return (pos[...][:, None, :] == slots).reshape(384, 128)


def gated(pos, gate):
    placed = placement(pos)
    weight = jnp.broadcast_to(gate[...][:, None, :], (8, 48, 128)).reshape(384, 128)
    weight = jnp.where(placed, weight, 0.0)
    high = weight.astype(BF16)
    return high, (weight - high.astype(F32)).astype(BF16)


PLACE = pl.BlockSpec((8, 128), lambda e: (e, 0))
SLOTS = pl.BlockSpec((8, 48, 1024), lambda e: (e, 0, 0))


def mid_kernel(recv, w_out, tok, gain, pos, o_ref, y_ref, out, h2):
    @pl.when(pl.program_id(0) == 0)
    def _():
        for s in range(2):
            for half in range(2):
                first = s * 64 + half * 32
                for m in range(8):
                    o_ref[first : first + 32, m * 128 : (m + 1) * 128] = recv[s, m, half]
        y = tok[...].astype(F32) + dot(o_ref[...], w_out[...])
        y_ref[...] = y
        inverse = lax.rsqrt(jnp.mean(y * y, axis=-1, keepdims=True) + EPS)
        h2[...] = (y * inverse * gain[...]).astype(BF16)

    placed = placement(pos).astype(F32).astype(BF16)
    out[...] = dot(placed, h2[...]).astype(BF16).reshape(8, 48, 1024)


def mid(recv, w_out, tok, gain, pos):
    return call(
        mid_kernel,
        (4,),
        [
            whole(2, 8, 2, 32, 128),
            whole(1024, 1024),
            whole(128, 1024),
            whole(1, 1024),
            PLACE,
        ],
        [whole(128, 1024), whole(128, 1024), SLOTS],
        [sds((128, 1024), BF16), sds((128, 1024), F32), sds((32, 48, 1024), BF16)],
        [pltpu.VMEM((128, 1024), BF16)],
        flops=2 * 128 * 1024 * 1024 + 2 * 1536 * 128 * 1024,
        moved=6 << 20,
    )(recv, w_out, tok, gain, pos)


def expert_kernel(x_ref, wgu, wdn, eo, slopes, hid_ref):
    activations = dot(x_ref[...], wgu[...])
    gate, up = activations[:, :FF_EXP], activations[:, FF_EXP:]
    sig = jax.nn.sigmoid(gate)
    act = gate * sig
    hid = (act * up).astype(BF16)
    hid_ref[...] = hid
    slopes[:, :FF_EXP] = (up * sig * (1.0 + gate * (1.0 - sig))).astype(BF16)
    slopes[:, FF_EXP:] = act.astype(BF16)
    eo[...] = dot(hid, wdn[...]).astype(BF16)


ROWS384 = pl.BlockSpec((384, 1024), lambda i: (i, 0))
HIDDEN = pl.BlockSpec((384, 512), lambda i: (i, 0))


def expert(x, wgu, wdn, deps):
    return call(
        expert_kernel,
        (4,),
        [ROWS384, whole(1024, 1024), whole(512, 1024)],
        [ROWS384, ROWS384, HIDDEN],
        [sds((1536, 1024), BF16), sds((1536, 1024), BF16), sds((1536, 512), BF16)],
        flops=2 * 1536 * 1024 * 1536,
        moved=14 << 20,
        deps=deps,
    )(x, wgu, wdn)


def expert_back_kernel(which, info, dz, slopes, wgu, wdn, dx2, da_ref, deo_ref):
    slots = lax.broadcasted_iota(jnp.int32, (48, 128), 0).astype(F32)
    rows16 = lax.broadcasted_iota(jnp.int32, (16, 128), 0)
    blank = jnp.zeros((48, 128), F32)
    mine = which[0] % 4
    for pair in range(4):
        parts, weights = [], []
        for j in range(2):
            tile = info[pair, j].astype(F32)

            def pick(k):
                return jnp.sum(jnp.where(rows16 == mine + 4 * k, tile, 0.0), axis=0, keepdims=True)

            hot = jnp.where(slots == pick(0), 1.0, 0.0)
            weights.append(jnp.sum(hot * (pick(1) + pick(2)), axis=1, keepdims=True))
            parts.append(jnp.concatenate([hot, blank] if j == 0 else [blank, hot], 1))
        rows = dot(jnp.concatenate(parts, 0).astype(BF16), dz[pair].reshape(256, 1024))
        rows = (rows * jnp.concatenate(weights, 0)).astype(BF16)
        for j in range(2):
            first = pl.multiple_of(pair * 96 + (which[1] ^ j) * 48, 48)
            deo_ref[pl.ds(first, 48), :] = rows[j * 48 : (j + 1) * 48]
    dhid = dot(deo_ref[...], wdn[...], NT)
    da_ref[:, :FF_EXP] = (dhid * slopes[:, :FF_EXP].astype(F32)).astype(BF16)
    da_ref[:, FF_EXP:] = (dhid * slopes[:, FF_EXP:].astype(F32)).astype(BF16)
    dx2[...] = dot(da_ref[...], wgu[...], NT).astype(BF16)


def expert_back(which, dz_all, slopes, wgu, wdn):
    dz_all = pltpu.with_memory_space_constraint(dz_all, pltpu.HBM)
    rows = pl.BlockSpec((384, 1024), lambda i, which: (i, 0))
    return call(
        expert_back_kernel,
        (4,),
        [
            pl.BlockSpec((4, 2, 16, 128), lambda i, which: (i, 0, 8, which[0] // 4)),
            pl.BlockSpec((4, 2, 128, 1024), lambda i, which: (i, 0, 0, 0)),
            rows,
            whole(1024, 1024),
            whole(512, 1024),
        ],
        [rows, rows, rows],
        [sds((1536, 1024), BF16)] * 3,
        flops=2 * 1536 * 1024 * 1792,
        moved=24 << 20,
        scalars=1,
    )(which, dz_all, dz_all, slopes, wgu, wdn)


def expert_grad_kernel(core, x_ref, da, hid, deo, own, other):
    step = pl.program_id(0)

    for first, out in ((0, own), (3, other)):

        @pl.when((step >= first) & (step < first + 2))
        def _():
            out[...] = dot(x_ref[...], da[...], TN).astype(BF16)

        @pl.when(step == first + 2)
        def _():
            out[...] = dot(hid[...], deo[...], TN).astype(BF16)


def expert_grad(core, x, da, hid, deo):
    def half(i, core):
        return jnp.where(i < 3, core[0], 1 - core[0])

    return call(
        expert_grad_kernel,
        (6,),
        [
            pl.BlockSpec((1536, 256), lambda i, c: (0, half(i, c) * 2 + jnp.minimum(i % 3, 1))),
            whole(1536, 1024),
            pl.BlockSpec((1536, 256), lambda i, c: (0, half(i, c))),
            whole(1536, 1024),
        ],
        [
            pl.BlockSpec((256, 1024), lambda i, c: (jnp.minimum(i, 2), 0)),
            pl.BlockSpec((256, 1024), lambda i, c: (jnp.maximum(i - 3, 0), 0)),
        ],
        [sds((768, 1024), BF16)] * 2,
        flops=2 * 1536 * 1024 * 1536,
        moved=16 << 20,
        scalars=1,
    )(core, x, da, hid, deo)


def final_expert_kernel(core, own, other, gate_up, down):
    step = pl.program_id(0)
    half = jnp.where(step < 4, step // 2, step - 4)

    def write(out):
        @pl.when(half == core[0])
        def _():
            out[...] = own[...].astype(F32)

        @pl.when(half != core[0])
        def _():
            out[...] = other[...].astype(F32)

    @pl.when(step < 4)
    def _():
        write(gate_up)

    @pl.when(step >= 4)
    def _():
        write(down)


def final_expert(core, own, other):
    part = pl.BlockSpec((256, 1024), lambda i: (jnp.where(i < 4, i % 2, 2), 0))
    return call(
        final_expert_kernel,
        (6,),
        [pl.BlockSpec(memory_space=pltpu.SMEM), part, part],
        [
            pl.BlockSpec((256, 1024), lambda i: (jnp.minimum(i, 3), 0)),
            pl.BlockSpec((256, 1024), lambda i: (jnp.maximum(i - 4, 0), 0)),
        ],
        [sds((1024, 1024), F32), sds((512, 1024), F32)],
        moved=9 << 20,
    )(core, own, other)


def norm_back(incoming, gain, vectors):
    inverse = lax.rsqrt(jnp.mean(vectors * vectors, axis=-1, keepdims=True) + EPS)
    scaled = vectors * inverse
    weighted = incoming * gain
    mean = jnp.mean(weighted * scaled, axis=-1, keepdims=True)
    return inverse * (weighted - scaled * mean), scaled


def mid_back_kernel(core, back, pos, y, gain, dz, w_out, dy_ref, own, other, send, acc):
    @pl.when(pl.program_id(0) == 0)
    def _():
        acc[...] = jnp.zeros_like(acc)

    placed = placement(pos).astype(F32).astype(BF16)
    acc[...] += dot(placed, back[...].reshape(384, 1024), TN)

    @pl.when(pl.program_id(0) == 3)
    def _():
        dh2 = acc[...]
        dv, scaled = norm_back(dh2, gain[...], y[...])
        gains = jnp.sum(dh2 * scaled, axis=0, keepdims=True)
        row = lax.broadcasted_iota(jnp.int32, (8, 128), 0)
        tile = jnp.zeros((8, 128), F32)
        for r in range(8):
            tile = jnp.where(row == r, gains[:, r * 128 : (r + 1) * 128], tile)
        high = tile.astype(BF16).astype(F32)
        extra = jnp.concatenate([high, tile - high], 0).astype(BF16)
        dy = dz[...].astype(F32) + dv
        dy_ref[...] = dy
        dbr = dy.astype(BF16)

        @pl.when(core[0] == 0)
        def _():
            own[...] = dbr[:, :512]
            other[...] = dbr[:, 512:]

        @pl.when(core[0] == 1)
        def _():
            own[...] = dbr[:, 512:]
            other[...] = dbr[:, :512]

        do = dot(dbr, w_out[...], NT).astype(BF16)
        for s in range(2):
            for half in range(2):
                first = s * 64 + half * 32
                for m in range(8):
                    send[s, m, half, 0:32, :] = do[first : first + 32, m * 128 : (m + 1) * 128]
                    send[s, m, half, 32:48, :] = extra


def mid_back(core, back, pos, y, gain, dz, w_out, deps):
    return call(
        mid_back_kernel,
        (4,),
        [
            pl.BlockSpec(memory_space=pltpu.SMEM),
            SLOTS,
            PLACE,
            whole(128, 1024),
            whole(1, 1024),
            whole(128, 1024),
            whole(1024, 1024),
        ],
        [whole(128, 1024), whole(128, 512), whole(128, 512), whole(2, 8, 2, 48, 128)],
        [
            sds((128, 1024), F32),
            sds((128, 512), BF16),
            sds((128, 512), BF16),
            sds((2, 8, 2, 48, 128), BF16),
        ],
        [pltpu.VMEM((128, 1024), F32)],
        flops=2 * 128 * 1024 * 1024 + 2 * 1536 * 128 * 1024,
        moved=6 << 20,
        deps=deps,
    )(core, back, pos, y, gain, dz, w_out)


def combine_kernel(back, pos, gate, y, out, acc):
    @pl.when(pl.program_id(0) == 0)
    def _():
        acc[...] = y[...]

    high, rest = gated(pos, gate)
    rows = back[...].reshape(384, 1024)
    acc[...] += dot(high, rows, TN) + dot(rest, rows, TN)

    @pl.when(pl.program_id(0) == 3)
    def _():
        out[...] = acc[...].astype(BF16)


def combine(back, pos, gate, y):
    return call(
        combine_kernel,
        (4,),
        [SLOTS, PLACE, PLACE, whole(128, 1024)],
        whole(128, 1024),
        sds((128, 1024), BF16),
        [pltpu.VMEM((128, 1024), F32)],
        flops=4 * 1536 * 128 * 1024,
        moved=4 << 20,
    )(back, pos, gate, y)


def unpack_kernel(core, recv, cos, sin, dproj, own, other):
    c, s = cos[...], sin[...]

    def rope_back(u):
        return u * c - swap_halves(u) * s

    for t in range(2):
        rows = slice(t * 64, t * 64 + 64)
        for mm in range(4):
            both = []
            for j in range(2):
                m = 2 * mm + j
                dq = jnp.concatenate([recv[t, m, 0, 0:32, :], recv[t, m, 1, 0:32, :]], 0)
                dproj[rows, m * 128 : (m + 1) * 128] = (rope_back(dq.astype(F32)) * SCALE).astype(
                    BF16
                )
                both.append(
                    recv[t, m, 0, 32:96, :].astype(F32) + recv[t, m, 1, 32:96, :].astype(F32)
                )
            low = low_half((64, 128))
            dk = jnp.where(low, both[0], pltpu.roll(both[1], HEAD, 1))
            dv = jnp.where(low, pltpu.roll(both[0], HEAD, 1), both[1])
            dproj[rows, 1024 + mm * 128 : 1152 + mm * 128] = rope_back(dk).astype(BF16)
            dproj[rows, 1536 + mm * 128 : 1664 + mm * 128] = dv.astype(BF16)

    @pl.when(core[0] == 0)
    def _():
        own[...] = dproj[:, :1024]
        other[...] = dproj[:, 1024:]

    @pl.when(core[0] == 1)
    def _():
        own[...] = dproj[:, 1024:]
        other[...] = dproj[:, :1024]


def unpack(core, recv, cos, sin, deps):
    return call(
        unpack_kernel,
        (1,),
        [
            pl.BlockSpec(memory_space=pltpu.SMEM),
            whole(2, 8, 2, 96, 128),
            whole(64, 128),
            whole(64, 128),
        ],
        [whole(128, 2048), whole(128, 1024), whole(128, 1024)],
        [sds((128, 2048), BF16), sds((128, 1024), BF16), sds((128, 1024), BF16)],
        moved=3 << 20,
        deps=deps,
    )(core, recv, cos, sin)


def last_kernel(dproj, w_qkv, tok, gain, dy, grad_tokens):
    dh = dot(dproj[...], w_qkv[...], NT)
    dv, _ = norm_back(dh, gain[...], tok[...].astype(F32))
    grad_tokens[...] = dy[...] + dv


def last(dproj, w_qkv, tok, gain, dy, deps):
    return call(
        last_kernel,
        (1,),
        [
            whole(128, 2048),
            whole(1024, 2048),
            whole(128, 1024),
            whole(1, 1024),
            whole(128, 1024),
        ],
        whole(128, 1024),
        sds((128, 1024), F32),
        flops=2 * 128 * 1024 * 2048,
        moved=6 << 20,
        deps=deps,
    )(dproj, w_qkv, tok, gain, dy)


def weight_grad_kernel(left, left2, right, right2, out):
    a = jnp.concatenate([left[...], left2[...]], 0)
    b = jnp.concatenate([right[...], right2[...]], 0)
    out[...] = dot(a, b, TN).astype(BF16)


def weight_grad(left, left2, right, right2, deps=()):
    width = right.shape[1]
    thin = pl.BlockSpec((128, 256), lambda i: (0, i))
    return call(
        weight_grad_kernel,
        (4,),
        [thin, thin, whole(128, width), whole(128, width)],
        pl.BlockSpec((256, width), lambda i: (i, 0)),
        sds((1024, width), BF16),
        flops=2 * 256 * 1024 * width,
        moved=3 << 20,
        deps=deps,
    )(left, left2, right, right2)


def add_pieces_kernel(pieces, out):
    total = jnp.sum(pieces[...].astype(F32), axis=0).astype(BF16)
    out[...] = jnp.broadcast_to(total[None], out.shape)


def add_pieces(pieces, deps=()):
    block = pl.BlockSpec((64, 16, 256), lambda i: (0, 0, i))
    return call(
        add_pieces_kernel,
        (pieces.shape[2] // 256,),
        [block],
        block,
        sds(pieces.shape, BF16),
        moved=4 << 20,
        deps=deps,
    )(pieces)


def final_out_kernel(core, own, other, out):
    @pl.when(core[0] == 0)
    def _():
        out[:, :512] = own[...].astype(F32)
        out[:, 512:] = other[...].astype(F32)

    @pl.when(core[0] == 1)
    def _():
        out[:, :512] = other[...].astype(F32)
        out[:, 512:] = own[...].astype(F32)


def final_out(core, own, other):
    half = pl.BlockSpec((256, 512), lambda i: (i, 0))
    return call(
        final_out_kernel,
        (4,),
        [pl.BlockSpec(memory_space=pltpu.SMEM), half, half],
        pl.BlockSpec((256, 1024), lambda i: (i, 0)),
        sds((1024, 1024), F32),
        moved=6 << 20,
    )(core, own, other)


def row_sums(product):
    total = jnp.sum(product, axis=-1, keepdims=True)
    total = jnp.broadcast_to(total, (256, 128))
    return jnp.concatenate([total[:128].T[0:1], total[128:].T[0:1]], 0)


def final_own_kernel(core, own, w_qkv, out, gain_ref):
    value = own[...].astype(F32)
    out[...] = value
    at = pl.ds(pl.program_id(0) * 2, 2)
    gain_ref[at, :] = row_sums(value * w_qkv[...].astype(F32))


def final_own(core, own, w_qkv):
    half = pl.BlockSpec((256, 1024), lambda i, core: (i, core[0]))
    return call(
        final_own_kernel,
        (4,),
        [pl.BlockSpec((256, 1024), lambda i, core: (i, 0)), half],
        [half, whole(8, 128)],
        [sds((1024, 2048), F32), sds((8, 128), F32)],
        moved=8 << 20,
        scalars=1,
    )(core, own, w_qkv)


def final_other_kernel(core, other, w_qkv, part, gain, _, out, gain_ref):
    value = other[...].astype(F32)
    out[...] = value
    at = pl.ds(pl.program_id(0) * 2, 2)
    gain_ref[at, :] = (part[at, :] + row_sums(value * w_qkv[...].astype(F32))) / gain[at, :]


def final_other(core, other, w_qkv, part, gain, out):
    half = pl.BlockSpec((256, 1024), lambda i, core: (i, 1 - core[0]))
    return call(
        final_other_kernel,
        (4,),
        [
            pl.BlockSpec((256, 1024), lambda i, core: (i, 0)),
            half,
            whole(8, 128),
            whole(8, 128),
            pl.BlockSpec(memory_space=pl.ANY),
        ],
        [half, whole(8, 128)],
        [sds((1024, 2048), F32), sds((8, 128), F32)],
        moved=8 << 20,
        scalars=1,
        aliases={5: 0},
    )(core, other, w_qkv, part, gain, out)


def exchange(x):
    return lax.all_to_all(x, BLK, 0, 0, tiled=True)


def add_rounded(a, b):
    return (a.astype(F32) + b.astype(F32)).astype(BF16)


def among_experts(x):
    return lax.all_to_all(x, CHIPS, 0, 0, tiled=True, axis_index_groups=EXPERT_GROUPS)


def among_chips(x):
    return lax.all_to_all(x, CHIPS, 0, 0, tiled=True)


def shards(
    tokens, lengths, routes, gates, gain_attn, w_qkv, w_out, gain_moe, w_gate_up, w_down, cotangent
):
    core = lax.axis_index("core")
    blk = lax.axis_index(BLK)
    tok = tokens.reshape(128, 1024)
    dz = cotangent.reshape(128, 1024)
    wgu = w_gate_up.reshape(1024, 1024)
    wdn = w_down.reshape(512, 1024)
    gain_a = gain_attn.reshape(1, 1024)
    gain_m = gain_moe.reshape(1, 1024)

    lane = np.arange(128)
    frequency = ROPE_BASE ** (-jnp.arange(32, dtype=F32) / 32)
    angles = (blk * 64 + jnp.arange(64, dtype=jnp.int32)).astype(F32)[:, None] * frequency[None, :]
    cos = jnp.tile(jnp.cos(angles), (1, 4))
    sin = jnp.tile(jnp.sin(angles), (1, 4)) * np.where(lane % 64 < 32, -1.0, 1.0).astype(np.float32)

    which = core.astype(jnp.int32).reshape(1)
    info = jnp.stack([jnp.where(blk < 16, lengths[0], lengths[1]), blk % 2]).astype(jnp.int32)

    def to_partner(part):
        return lax.ppermute(part, "core", SWAP)

    h, send = pre(tok, gain_a, w_qkv, cos, sin)
    arrived = exchange(send.reshape(32, 96, 128))
    h_other = to_partner(h)
    pos, gate, planned = plan(routes.reshape(128, 8), gates.reshape(128, 8), dz, [send])
    planned = jnp.stack([planned, lax.ppermute(planned, ("zl", "zh"), Z_PAIRS)])
    dz_all = lax.all_gather(planned, ("x", "y"))
    o_part, ot, lse = attend(info, arrived, [h_other, planned])
    o_recv = exchange(o_part).reshape(2, 8, 2, 32, 128)
    o, y, rows = mid(o_recv, w_out, tok, gain_m, pos)
    o_other = to_partner(o)
    x = among_experts(rows).reshape(1536, 1024)
    eo, slopes, hid = expert(x, wgu, wdn, [o_other])
    eo_back = among_experts(eo.reshape(32, 48, 1024))
    place = jnp.stack([blk, lax.axis_index("zh")]).astype(jnp.int32)
    dx2, da, deo = expert_back(place, dz_all, slopes, wgu, wdn)
    dx2_back = among_experts(after(dx2.reshape(32, 48, 1024), eo_back))
    experts_own, experts_send = expert_grad(which, x, da, hid, deo)
    experts_own = add_rounded(experts_own, to_partner(experts_send))
    mixed = combine(eo_back, pos, gate, y)
    dy, dbr_own, dbr_send, do = mid_back(
        which, dx2_back, pos, y, gain_m, dz, w_out, [experts_own, mixed]
    )
    experts_own = add_rounded(experts_own, lax.ppermute(experts_own, "zl", SWAP))

    do_recv = exchange(do.reshape(32, 48, 128))
    out_partial = weight_grad(o, o_other, dbr_own, to_partner(dbr_send), [experts_own])
    out_pieces = among_chips(out_partial.reshape(64, 16, 512))
    dqkv, gains = attend_back(info, arrived, do_recv, ot, lse, [out_partial])
    dqkv_recv = exchange(after(dqkv, out_pieces)).reshape(2, 8, 2, 96, 128)

    for axis in ROWS:
        gains = gains + lax.ppermute(gains, axis, SWAP)

    out_copies = add_pieces(out_pieces)
    dproj, dproj_own, dproj_send = unpack(which, dqkv_recv, cos, sin, [gains, out_copies])
    out_own = among_chips(out_copies).reshape(1024, 512)
    grad_out = final_out(which, out_own, to_partner(out_own))
    grad_gate_up, grad_down = final_expert(which, experts_own, to_partner(experts_own))

    partial = weight_grad(h, h_other, dproj_own, to_partner(dproj_send))
    grad_tokens = last(dproj, w_qkv, tok, gain_a, dy, [partial])
    pieces = among_chips(after(partial.reshape(64, 16, 1024), out_own))
    own = among_chips(add_pieces(pieces, [grad_out, grad_gate_up, grad_tokens])).reshape(1024, 1024)
    own_part, gain_part = final_own(which, own, w_qkv)
    grad_qkv, grad_gain_attn = final_other(
        which, to_partner(own), w_qkv, gain_part, gain_attn.reshape(8, 128), own_part
    )
    return (
        mixed.reshape(2, 64, 1024),
        grad_tokens.reshape(2, 64, 1024),
        grad_gain_attn.reshape(1024),
        grad_qkv,
        grad_out,
        gains.reshape(1024),
        grad_gate_up[None],
        grad_down[None],
    )


def solution(mesh):
    split = Mesh(mesh.devices.reshape(2, 2, 4, 4, 2), AXES)
    rows = P(ROWS, BLK, None)
    return jax.shard_map(
        shards,
        mesh=split,
        in_specs=(
            rows,
            P(ROWS),
            rows,
            rows,
            P(),
            P(),
            P(),
            P(),
            P(BLK, None, None),
            P(BLK, None, None),
            rows,
        ),
        out_specs=(
            rows,
            rows,
            P(),
            P(),
            P(),
            P(),
            P(BLK, None, None),
            P(BLK, None, None),
        ),
        check_vma=False,
    )
```

```python
import jax
import jax.numpy as jnp
import numpy as np
from jax import lax
from jax.experimental import pallas as pl
from jax.experimental.pallas import tpu as pltpu
from jax.sharding import Mesh
from jax.sharding import PartitionSpec as P

HEADS = 16
KV_HEADS = 8
HEAD = 64
FF_EXP = 512
TOP = 8
MOST = 24
EPS = 1e-06
ROPE_BASE = 10000.0
SCALE = HEAD ** (-0.5)

ROWS = ("zl", "core")
PLANE = ("xh", "xl", "y")
BLK = ("xh", "xl", "y", "zh")
CHIPS = ("zl", "xh", "xl", "y", "zh")
AXES = ("zl", "core", "xh", "xl", "y", "zh")
SAME_COLUMNS = ("zl", "core", "xh", "zh")
SWAP = [(0, 1), (1, 0)]
EXPERT_GROUPS = [
    [(parity ^ zh) * 32 + xy * 2 + zh for xy in range(16) for zh in range(2)] for parity in range(2)
]
Z_PAIRS = [(i, 3 - i) for i in range(4)]
F32 = jnp.float32
BF16 = jnp.bfloat16
NT = (((1,), (1,)), ((), ()))
TN = (((0,), (0,)), ((), ()))


def rope_tables():
    lane = np.arange(128) % HEAD
    frequency = (ROPE_BASE ** (-(lane % 32) / 32.0)).astype(np.float32)
    angles = np.arange(2048, dtype=np.float32)[:, None] * frequency[None, :]
    sign = np.where(lane < 32, -1.0, 1.0)
    cosine = np.cos(angles.astype(np.float64)).astype(np.float32)
    return cosine, (np.sin(angles.astype(np.float64)) * sign).astype(np.float32)


def dot(left, right, dims=(((1,), (0,)), ((), ()))):
    return lax.dot_general(left, right, dims, preferred_element_type=F32)


def call(
    kernel,
    grid,
    in_specs,
    out_specs,
    out_shape,
    scratch=(),
    mb=24,
    flops=0,
    moved=0,
    deps=(),
    scalars=0,
    aliases=None,
    moving=(),
):
    count = len(in_specs) + scalars

    def place(i, x):
        small = i < scalars or in_specs[i - scalars].memory_space == pltpu.SMEM
        return x if small or i in moving else hold(x)

    def body(*refs):
        kernel(*refs[:count], *refs[count + len(deps) :])

    built = pl.pallas_call(
        body,
        grid_spec=pltpu.PrefetchScalarGridSpec(
            num_scalar_prefetch=scalars,
            grid=grid,
            in_specs=[*in_specs, *[pl.BlockSpec(memory_space=pl.ANY)] * len(deps)],
            out_specs=out_specs,
            scratch_shapes=list(scratch),
        ),
        out_shape=out_shape,
        input_output_aliases=aliases or {},
        compiler_params=pltpu.CompilerParams(vmem_limit_bytes=mb * 1024 * 1024),
        cost_estimate=pl.CostEstimate(flops=flops, bytes_accessed=moved, transcendentals=0),
    )
    return lambda *operands: built(*[place(i, x) for i, x in enumerate(operands)], *deps)


def after(x, *deps):
    any_space = pl.BlockSpec(memory_space=pl.ANY)
    return pl.pallas_call(
        lambda *refs: None,
        in_specs=[any_space] * (1 + len(deps)),
        out_specs=any_space,
        out_shape=sds(x.shape, x.dtype),
        input_output_aliases={0: 0},
        compiler_params=pltpu.CompilerParams(vmem_limit_bytes=1024 * 1024),
    )(hold(x), *deps)


def hold(x):
    return pltpu.with_memory_space_constraint(x, pltpu.HBM)


def corner(x):
    return x[(0,) * (x.ndim - 2)][:8, :128]


def whole(*shape):
    return pl.BlockSpec(shape, lambda *_: (0,) * len(shape))


def sds(shape, dtype):
    return pltpu.HBM(shape, dtype)


def low_half(shape):
    return lax.broadcasted_iota(jnp.int32, shape, len(shape) - 1) < HEAD


def swap_halves(u):
    lane = lax.broadcasted_iota(jnp.int32, u.shape, 1)
    return jnp.where(lane % HEAD < HEAD // 2, pltpu.roll(u, 96, 1), pltpu.roll(u, 32, 1))


def pre_kernel(blk, tok, gain, wq, wk, wv, cos, sin, h_ref, send):
    @pl.when(pl.program_id(0) == 0)
    def _():
        x = tok[...].astype(F32)
        inverse = lax.rsqrt(jnp.mean(x * x, axis=-1, keepdims=True) + EPS)
        h_ref[...] = (x * inverse * gain[...]).astype(BF16)

    h = h_ref[...]
    c = jnp.concatenate([cos[...], cos[...]], 0)
    s = jnp.concatenate([sin[...], sin[...]], 0)

    def rope(u):
        return u * c + swap_halves(u) * s

    q = dot(h, wq[...])
    k = rope(dot(h, wk[...]))
    v = dot(h, wv[...])
    low = low_half(k.shape)
    pairs = (
        jnp.where(low, k, pltpu.roll(v, HEAD, 1)).astype(BF16),
        jnp.where(low, pltpu.roll(k, HEAD, 1), v).astype(BF16),
    )
    for j in range(2):
        qj = (rope(q[:, j * 128 : (j + 1) * 128]).astype(BF16).astype(F32) * SCALE).astype(BF16)
        for t in range(2):
            for half in range(2):
                first = t * 64 + half * 32
                send[half, j, t, 0:32, :] = qj[first : first + 32]
                send[half, j, t, 32:96, :] = pairs[j][t * 64 : t * 64 + 64]


def pre(blk, tok, gain, w_qkv, cos, sin, deps):
    places = pl.BlockSpec((64, 128), lambda m, blk: (blk[0], 0))
    return call(
        pre_kernel,
        (4,),
        [
            whole(128, 1024),
            whole(1, 1024),
            pl.BlockSpec((1024, 256), lambda m, blk: (0, m)),
            pl.BlockSpec((1024, 128), lambda m, blk: (0, 8 + m)),
            pl.BlockSpec((1024, 128), lambda m, blk: (0, 12 + m)),
            places,
            places,
        ],
        [whole(128, 1024), pl.BlockSpec((2, 2, 2, 96, 128), lambda m, blk: (0, m, 0, 0, 0))],
        [sds((128, 1024), BF16), sds((2, 8, 2, 96, 128), BF16)],
        flops=2 * 128 * 1024 * 2048,
        moved=5 << 20,
        scalars=1,
        deps=deps,
    )(blk, tok, gain, w_qkv, w_qkv, w_qkv, cos, sin)


def plan_kernel(routes, gates, dz, pos_ref, gate_ref, out):
    named = jnp.concatenate([routes[0], routes[1]], 1).astype(F32)
    weights = jnp.concatenate([gates[0], gates[1]], 1)
    experts = lax.broadcasted_iota(jnp.int32, (32, 128), 0).astype(F32)
    chosen = jnp.zeros((32, 128), F32)
    gate = jnp.zeros((32, 128), F32)
    for k in range(TOP):
        match = named[k : k + 1] == experts
        chosen = jnp.where(match, 1.0, chosen)
        gate = jnp.where(match, weights[k : k + 1], gate)
    row = lax.broadcasted_iota(jnp.int32, (128, 128), 0)
    before = jnp.where(row < lax.broadcasted_iota(jnp.int32, (128, 128), 1), 1.0, 0.0)
    rank = dot(chosen.astype(BF16), before.astype(BF16))
    pos = jnp.where(chosen > 0.0, rank, -1.0)
    pos_ref[...] = pos.astype(jnp.int32)
    gate_ref[...] = gate
    high = gate.astype(BF16).astype(F32)
    rest = gate - high
    out[0:128, :] = dz[...]
    for j in range(8):
        part = slice(4 * j, 4 * j + 4)
        tile = jnp.concatenate([pos[part], high[part], rest[part], jnp.zeros((4, 128), F32)], 0)
        out[128:144, j * 128 : (j + 1) * 128] = tile.astype(BF16)


def plan(routes, gates, dz):
    return call(
        plan_kernel,
        (1,),
        [whole(2, 8, 64), whole(2, 8, 64), whole(128, 1024)],
        [whole(32, 128), whole(32, 128), whole(144, 1024)],
        [sds((32, 128), jnp.int32), sds((32, 128), F32), sds((144, 1024), BF16)],
        moved=1 << 20,
    )(routes, gates, dz)


def split_queries(q):
    qf = q.astype(F32)
    low = low_half(qf.shape)
    first = jnp.where(low, qf, 0.0)
    second = jnp.where(low, pltpu.roll(qf, HEAD, 1), 0.0)
    return jnp.concatenate([first, second], 0).astype(BF16)


def limits(tile, info):
    place = lax.broadcasted_iota(jnp.int32, (1, 512), 1) % 256
    position = (tile * 8 + place // 32) * 64 + info[1] * 32 + place % 32
    return jnp.minimum(position, info[0] - 1)


def load_pairs(x_ref, kv, kvt):
    kv[...] = x_ref[:, 32:96, :].reshape(2048, 128)
    for c in range(8):
        rows = slice(c * 256, (c + 1) * 256)
        kvt[:, rows] = kv[rows, :].astype(F32).T.astype(BF16)


def attend_kernel(info, x_ref, o_ref, ot_ref, lse_ref, kv, kvt):
    load_pairs(x_ref, kv, kvt)
    for tile in range(4):
        q2 = split_queries(x_ref[tile * 8 : (tile + 1) * 8, 0:32, :].reshape(256, 128))
        limit = limits(tile, info)

        def step(c, carry):
            top, total, acc = carry
            at = pl.ds(pl.multiple_of(c * 512, 512), 512)
            s = dot(kv[at, :], q2, NT)
            place = c * 512 + lax.broadcasted_iota(jnp.int32, (512, 1), 0)
            s = jnp.where(place <= limit, s, -1e30)
            new_top = jnp.maximum(top, jnp.max(s, axis=0, keepdims=True))
            shrink = jnp.exp(top - new_top)
            p = jnp.exp(s - new_top)
            total = total * shrink + jnp.sum(p, axis=0, keepdims=True)
            return new_top, total, acc * shrink + dot(kvt[64:128, at], p.astype(BF16))

        start = (jnp.full((1, 512), -1e30, F32), jnp.zeros((1, 512), F32), jnp.zeros((64, 512), F32))
        top, total, acc = lax.fori_loop(0, tile + 1, step, start)
        out = acc / total
        ot_ref[tile] = out
        lse_ref[tile] = jnp.broadcast_to(top + jnp.log(total), (8, 512))
        both = jnp.concatenate([out[:, :256], out[:, 256:]], 0).T
        o_ref[tile * 8 : (tile + 1) * 8] = both.astype(BF16).reshape(8, 32, 128)


def attend(info, arrived, deps):
    return call(
        attend_kernel,
        (1,),
        [pl.BlockSpec(memory_space=pltpu.SMEM), whole(32, 96, 128)],
        [whole(32, 32, 128), whole(4, 64, 512), whole(4, 8, 512)],
        [sds((32, 32, 128), BF16), sds((4, 64, 512), F32), sds((4, 8, 512), F32)],
        [pltpu.VMEM((2048, 128), BF16), pltpu.VMEM((128, 2048), BF16)],
        flops=4 * 2048 * 1280 * 128,
        moved=2 << 20,
        deps=deps,
        moving=(1,),
    )(info, arrived)


def attend_back_kernel(
    info, x_ref, do_ref, ot_ref, lse_ref, cos, sin, out_ref, gain_ref, kv, kvt, total
):
    load_pairs(x_ref, kv, kvt)
    total[...] = jnp.zeros_like(total)
    for tile in range(4):
        q2 = split_queries(x_ref[tile * 8 : (tile + 1) * 8, 0:32, :].reshape(256, 128))
        grad = do_ref[tile * 8 : (tile + 1) * 8, 0:32, :].reshape(256, 128).astype(F32)
        low = low_half(grad.shape)
        do2 = jnp.concatenate(
            [jnp.where(low, 0.0, pltpu.roll(grad, HEAD, 1)), jnp.where(low, 0.0, grad)], 0
        ).astype(BF16)
        grad_t = grad.T
        grad_t = jnp.concatenate([grad_t[:64], grad_t[64:]], 1)
        inner = jnp.sum(grad_t * ot_ref[tile], axis=0, keepdims=True)
        lse = lse_ref[tile][0:1]
        limit = limits(tile, info)

        def step(c, acc):
            at = pl.ds(pl.multiple_of(c * 256, 256), 256)
            part = kv[at, :]
            s = dot(part, q2, NT)
            place = c * 256 + lax.broadcasted_iota(jnp.int32, (256, 1), 0)
            p = jnp.exp(jnp.where(place <= limit, s, -1e30) - lse)
            ds = (p * (dot(part, do2, NT) - inner)).astype(BF16)
            total[at, :] += dot(ds, q2) + dot(p.astype(BF16), do2)
            return acc + dot(kvt[0:64, at], ds)

        acc = lax.fori_loop(0, 2 * tile + 2, step, jnp.zeros((64, 512), F32))
        dq = jnp.concatenate([acc[:, :256], acc[:, 256:]], 0).T
        at = (slice(tile * 8, tile * 8 + 8), pl.ds(pl.multiple_of(info[1] * 32, 32), 32))
        c, s = cos[at].reshape(256, 128), sin[at].reshape(256, 128)
        dq = ((dq * c - swap_halves(dq) * s) * SCALE).astype(BF16)
        out_ref[tile * 8 : (tile + 1) * 8, 0:32, :] = dq.reshape(8, 32, 128)
    for tile in range(4):
        blocks = slice(tile * 8, tile * 8 + 8)
        part = total[tile * 512 : (tile + 1) * 512, :]
        turned = part * cos[blocks].reshape(512, 128) - swap_halves(part) * sin[
            blocks
        ].reshape(512, 128)
        part = jnp.where(low_half(part.shape), turned, part)
        out_ref[blocks, 32:96, :] = part.astype(BF16).reshape(8, 64, 128)
    gains = jnp.sum(do_ref[:, 32:48, :].astype(F32), axis=0)
    gain_ref[...] = gains[:8] + gains[8:]


def attend_back(info, arrived, grad, ot, lse, cos, sin, deps):
    return call(
        attend_back_kernel,
        (1,),
        [
            pl.BlockSpec(memory_space=pltpu.SMEM),
            whole(32, 96, 128),
            whole(32, 48, 128),
            whole(4, 64, 512),
            whole(4, 8, 512),
            whole(32, 64, 128),
            whole(32, 64, 128),
        ],
        [whole(32, 96, 128), whole(8, 128)],
        [sds((32, 96, 128), BF16), sds((8, 128), F32)],
        [pltpu.VMEM((2048, 128), BF16), pltpu.VMEM((128, 2048), BF16), pltpu.VMEM((2048, 128), F32)],
        flops=10 * 2048 * 1280 * 128,
        moved=3 << 20,
        deps=deps,
        moving=(1, 2,),
    )(info, arrived, grad, ot, lse, cos.reshape(32, 64, 128), sin.reshape(32, 64, 128))


def placement(pos):
    slots = lax.broadcasted_iota(jnp.int32, (8, 48, 128), 1)
    return (pos[...][:, None, :] == slots).reshape(384, 128)


def gated(pos, gate):
    placed = placement(pos)
    weight = jnp.broadcast_to(gate[...][:, None, :], (8, 48, 128)).reshape(384, 128)
    weight = jnp.where(placed, weight, 0.0)
    high = weight.astype(BF16)
    return high, (weight - high.astype(F32)).astype(BF16)


PLACE = pl.BlockSpec((8, 128), lambda e: (e, 0))
SLOTS = pl.BlockSpec((8, 48, 1024), lambda e: (e, 0, 0))


def mid_kernel(recv, w0, w1, w2, w3, tok, gain, pos, o_ref, y_ref, out, h2):
    @pl.when(pl.program_id(0) == 0)
    def _():
        for s in range(2):
            for half in range(2):
                first = s * 64 + half * 32
                for m in range(8):
                    o_ref[first : first + 32, m * 128 : (m + 1) * 128] = recv[half, m, s]
        o = o_ref[...]
        branch = jnp.concatenate([dot(o, w[...]) for w in (w0, w1, w2, w3)], 1)
        y = tok[...].astype(F32) + branch
        y_ref[...] = y
        inverse = lax.rsqrt(jnp.mean(y * y, axis=-1, keepdims=True) + EPS)
        h2[...] = (y * inverse * gain[...]).astype(BF16)

    placed = placement(pos).astype(F32).astype(BF16)
    out[...] = dot(placed, h2[...]).astype(BF16).reshape(8, 48, 1024)


def mid(recv, w_out, tok, gain, pos, deps):
    return call(
        mid_kernel,
        (4,),
        [
            whole(2, 8, 2, 32, 128),
            *[pl.BlockSpec((1024, 256), lambda e, j=j: (0, j)) for j in range(4)],
            whole(128, 1024),
            whole(1, 1024),
            PLACE,
        ],
        [whole(128, 1024), whole(128, 1024), SLOTS],
        [sds((128, 1024), BF16), sds((128, 1024), F32), sds((32, 48, 1024), BF16)],
        [pltpu.VMEM((128, 1024), BF16)],
        flops=2 * 128 * 1024 * 1024 + 2 * 1536 * 128 * 1024,
        moved=6 << 20,
        moving=(0,),
        deps=deps,
    )(recv, w_out, w_out, w_out, w_out, tok, gain, pos)


def expert_kernel(
    which, x_ref, info, dz, g0, g1, u0, u1, d0, d1, dx2, eo, da_ref, deo_ref, hid_ref
):
    slots = lax.broadcasted_iota(jnp.int32, (48, 128), 0).astype(F32)
    rows16 = lax.broadcasted_iota(jnp.int32, (16, 128), 0)
    blank = jnp.zeros((48, 128), F32)
    mine = which[0] % 4
    for pair in range(4):
        parts, weights = [], []
        for j in range(2):
            tile = info[pair, j].astype(F32)

            def pick(k):
                return jnp.sum(jnp.where(rows16 == mine + 4 * k, tile, 0.0), axis=0, keepdims=True)

            hot = jnp.where(slots == pick(0), 1.0, 0.0)
            weights.append(jnp.sum(hot * (pick(1) + pick(2)), axis=1, keepdims=True))
            parts.append(jnp.concatenate([hot, blank] if j == 0 else [blank, hot], 1))
        rows = dot(jnp.concatenate(parts, 0).astype(BF16), dz[pair].reshape(256, 1024))
        rows = (rows * jnp.concatenate(weights, 0)).astype(BF16)
        for j in range(2):
            first = pl.multiple_of(pair * 96 + (which[1] ^ j) * 48, 48)
            deo_ref[pl.ds(first, 48), :] = rows[j * 48 : (j + 1) * 48]
    x, deo = x_ref[...], deo_ref[...]
    total = None
    for part, (wg, wu) in enumerate(((g0, u0), (g1, u1))):
        at = slice(part * 256, part * 256 + 256)
        late = slice(part * 256 + FF_EXP, part * 256 + FF_EXP + 256)
        gate, up = dot(x, wg[...]), dot(x, wu[...])
        dhid = dot(deo[:, :512], d0[at, :], NT) + dot(deo[:, 512:], d1[at, :], NT)
        sig = jax.nn.sigmoid(gate)
        act = gate * sig
        hid_ref[:, at] = (act * up).astype(BF16)
        da_gate = (dhid * up * sig * (1.0 + gate * (1.0 - sig))).astype(BF16)
        da_up = (dhid * act).astype(BF16)
        da_ref[:, at] = da_gate
        da_ref[:, late] = da_up
        product = dot(da_gate, wg[...], NT) + dot(da_up, wu[...], NT)
        total = product if total is None else total + product
    dx2[...] = total.astype(BF16)
    hid = hid_ref[...]
    eo[:, 0:48, :512] = dot(hid, d0[...]).astype(BF16).reshape(8, 48, 512)
    eo[:, 0:48, 512:] = dot(hid, d1[...]).astype(BF16).reshape(8, 48, 512)


def expert(which, x, dz_all, wgu, wdn, deps):
    rows = pl.BlockSpec((384, 1024), lambda i, which: (i, 0))
    return call(
        expert_kernel,
        (4,),
        [
            rows,
            pl.BlockSpec((4, 2, 16, 128), lambda i, which: (i, 0, 8, which[0] // 4)),
            pl.BlockSpec((4, 2, 128, 1024), lambda i, which: (i, 0, 0, 0)),
            *[pl.BlockSpec((1024, 256), lambda i, which, j=j: (0, j)) for j in range(4)],
            *[pl.BlockSpec((512, 512), lambda i, which, j=j: (0, j)) for j in range(2)],
        ],
        [
            rows,
            pl.BlockSpec((8, 64, 1024), lambda i, which: (i, 0, 0)),
            rows,
            rows,
            pl.BlockSpec((384, 512), lambda i, which: (i, 0)),
        ],
        [
            sds((1536, 1024), BF16),
            sds((32, 64, 1024), BF16),
            sds((1536, 1024), BF16),
            sds((1536, 1024), BF16),
            sds((1536, 512), BF16),
        ],
        mb=32,
        flops=2 * 1536 * 1024 * 3328,
        moved=30 << 20,
        scalars=1,
        moving=(1,),
        deps=deps,
    )(which, x, dz_all, dz_all, wgu, wgu, wgu, wgu, wdn, wdn)


def expert_grad_kernel(core, x_ref, da, hid, deo, own, other):
    step = pl.program_id(0)

    for first, out in ((0, own), (3, other)):

        @pl.when((step >= first) & (step < first + 2))
        def _():
            out[...] = dot(x_ref[...], da[...], TN).astype(BF16)

        @pl.when(step == first + 2)
        def _():
            out[...] = dot(hid[...], deo[...], TN).astype(BF16)


def expert_grad(core, x, da, hid, deo):
    def half(i, core):
        return jnp.where(i < 3, core[0], 1 - core[0])

    return call(
        expert_grad_kernel,
        (6,),
        [
            pl.BlockSpec((1536, 256), lambda i, c: (0, half(i, c) * 2 + jnp.minimum(i % 3, 1))),
            whole(1536, 1024),
            pl.BlockSpec((1536, 256), lambda i, c: (0, half(i, c))),
            whole(1536, 1024),
        ],
        [
            pl.BlockSpec((256, 1024), lambda i, c: (jnp.minimum(i, 2), 0)),
            pl.BlockSpec((256, 1024), lambda i, c: (jnp.maximum(i - 3, 0), 0)),
        ],
        [sds((768, 1024), BF16)] * 2,
        flops=2 * 1536 * 1024 * 1536,
        moved=16 << 20,
        scalars=1,
        moving=(1,),
    )(core, x, da, hid, deo)


def final_expert_kernel(core, own, other, gate_up, down):
    step = pl.program_id(0)
    half = jnp.where(step < 4, step // 2, step - 4)

    def write(out):
        @pl.when(half == core[0])
        def _():
            out[...] = own[...].astype(F32)

        @pl.when(half != core[0])
        def _():
            out[...] = other[...].astype(F32)

    @pl.when(step < 4)
    def _():
        write(gate_up)

    @pl.when(step >= 4)
    def _():
        write(down)


def final_expert(core, own, other):
    part = pl.BlockSpec((256, 1024), lambda i: (jnp.where(i < 4, i % 2, 2), 0))
    return call(
        final_expert_kernel,
        (6,),
        [pl.BlockSpec(memory_space=pltpu.SMEM), part, part],
        [
            pl.BlockSpec((256, 1024), lambda i: (jnp.minimum(i, 3), 0)),
            pl.BlockSpec((256, 1024), lambda i: (jnp.maximum(i - 4, 0), 0)),
        ],
        [sds((1024, 1024), F32), sds((512, 1024), F32)],
        moved=9 << 20,
        moving=(1, 2,),
    )(core, own, other)


def norm_back(incoming, gain, vectors):
    inverse = lax.rsqrt(jnp.mean(vectors * vectors, axis=-1, keepdims=True) + EPS)
    scaled = vectors * inverse
    weighted = incoming * gain
    mean = jnp.mean(weighted * scaled, axis=-1, keepdims=True)
    return inverse * (weighted - scaled * mean), scaled


def mid_back_kernel(
    core, back, pos, y, gain, dz, w0, w1, w2, w3, dy_ref, own, other, send, acc
):
    @pl.when(pl.program_id(0) == 0)
    def _():
        acc[...] = jnp.zeros_like(acc)

    placed = placement(pos).astype(F32).astype(BF16)
    acc[...] += dot(placed, back[...].reshape(384, 1024), TN)

    @pl.when(pl.program_id(0) == 3)
    def _():
        dh2 = acc[...]
        dv, scaled = norm_back(dh2, gain[...], y[...])
        gains = jnp.sum(dh2 * scaled, axis=0, keepdims=True)
        row = lax.broadcasted_iota(jnp.int32, (8, 128), 0)
        tile = jnp.zeros((8, 128), F32)
        for r in range(8):
            tile = jnp.where(row == r, gains[:, r * 128 : (r + 1) * 128], tile)
        high = tile.astype(BF16).astype(F32)
        extra = jnp.concatenate([high, tile - high], 0).astype(BF16)
        dy = dz[...].astype(F32) + dv
        dy_ref[...] = dy
        dbr = dy.astype(BF16)

        @pl.when(core[0] == 0)
        def _():
            own[...] = dbr[:, :512]
            other[...] = dbr[:, 512:]

        @pl.when(core[0] == 1)
        def _():
            own[...] = dbr[:, 512:]
            other[...] = dbr[:, :512]

        do = jnp.concatenate([dot(dbr, w[...], NT) for w in (w0, w1, w2, w3)], 1).astype(BF16)
        for s in range(2):
            for half in range(2):
                first = s * 64 + half * 32
                for m in range(8):
                    send[half, m, s, 0:32, :] = do[first : first + 32, m * 128 : (m + 1) * 128]
                    send[half, m, s, 32:48, :] = extra


def mid_back(core, back, pos, y, gain, dz, w_out, deps):
    return call(
        mid_back_kernel,
        (4,),
        [
            pl.BlockSpec(memory_space=pltpu.SMEM),
            SLOTS,
            PLACE,
            whole(128, 1024),
            whole(1, 1024),
            whole(128, 1024),
            *[pl.BlockSpec((256, 1024), lambda e, j=j: (j, 0)) for j in range(4)],
        ],
        [whole(128, 1024), whole(128, 512), whole(128, 512), whole(2, 8, 2, 48, 128)],
        [
            sds((128, 1024), F32),
            sds((128, 512), BF16),
            sds((128, 512), BF16),
            sds((2, 8, 2, 48, 128), BF16),
        ],
        [pltpu.VMEM((128, 1024), F32)],
        flops=2 * 128 * 1024 * 1024 + 2 * 1536 * 128 * 1024,
        moved=6 << 20,
        deps=deps,
        moving=(1,),
    )(core, back, pos, y, gain, dz, w_out, w_out, w_out, w_out)


def combine_kernel(back, pos, gate, y, out, acc):
    @pl.when(pl.program_id(0) == 0)
    def _():
        acc[...] = y[...]

    high, rest = gated(pos, gate)
    rows = back[...].reshape(384, 1024)
    acc[...] += dot(high, rows, TN) + dot(rest, rows, TN)

    @pl.when(pl.program_id(0) == 3)
    def _():
        out[...] = acc[...].astype(BF16)


def combine(back, pos, gate, y):
    return call(
        combine_kernel,
        (4,),
        [SLOTS, PLACE, PLACE, whole(128, 1024)],
        whole(128, 1024),
        sds((128, 1024), BF16),
        [pltpu.VMEM((128, 1024), F32)],
        flops=4 * 1536 * 128 * 1024,
        moved=4 << 20,
        moving=(0,),
    )(back, pos, gate, y)


def last_kernel(recv, w_qkv, tok, gain, dy, grad_tokens, dproj):
    low = low_half((64, 128))
    for t in range(2):
        rows = slice(t * 64, t * 64 + 64)
        for mm in range(4):
            both = []
            for j in range(2):
                m = 2 * mm + j
                dq = jnp.concatenate([recv[0, m, t, 0:32, :], recv[1, m, t, 0:32, :]], 0)
                dproj[rows, m * 128 : (m + 1) * 128] = dq
                both.append(
                    recv[0, m, t, 32:96, :].astype(F32) + recv[1, m, t, 32:96, :].astype(F32)
                )
            dk = jnp.where(low, both[0], pltpu.roll(both[1], HEAD, 1))
            dv = jnp.where(low, pltpu.roll(both[0], HEAD, 1), both[1])
            dproj[rows, 1024 + mm * 128 : 1152 + mm * 128] = dk.astype(BF16)
            dproj[rows, 1536 + mm * 128 : 1664 + mm * 128] = dv.astype(BF16)
    dh = dot(dproj[...], w_qkv[...], NT)
    dv, _ = norm_back(dh, gain[...], tok[...].astype(F32))
    grad_tokens[...] = dy[...] + dv


def last(recv, w_qkv, tok, gain, dy, deps):
    return call(
        last_kernel,
        (1,),
        [
            whole(2, 8, 2, 96, 128),
            whole(1024, 2048),
            whole(128, 1024),
            whole(1, 1024),
            whole(128, 1024),
        ],
        whole(128, 1024),
        sds((128, 1024), F32),
        [pltpu.VMEM((128, 2048), BF16)],
        flops=2 * 128 * 1024 * 2048,
        moved=6 << 20,
        deps=deps,
        moving=(0,),
    )(recv, w_qkv, tok, gain, dy)


def qkv_grad_kernel(place, h_all, d_ref, gains, out, rows, acc):
    step = pl.program_id(0)
    for pair in range(4):
        for zh in range(2):
            first = (pair * 2 + zh) * 64
            rows[first : first + 64, :] = h_all[pair, place[1] ^ zh]
    dq = d_ref[:, 0:32, :]
    none = jnp.zeros_like(dq)
    dq = jnp.where(place[0] == 0, jnp.concatenate([dq, none], 1), jnp.concatenate([none, dq], 1))
    both = jnp.concatenate([dq.reshape(512, 128), d_ref[:, 32:96, :].reshape(512, 128)], 1)
    product = dot(rows[...], both, TN)

    @pl.when(step == 0)
    def _():
        acc[...] = product

    @pl.when((step > 0) & (step < 3))
    def _():
        acc[...] += product

    @pl.when(step == 3)
    def _():
        out[:, 0:64, :] = (acc[...] + product).astype(BF16).reshape(16, 64, 256)
        high = gains[...].astype(BF16).astype(F32)
        tile = jnp.concatenate([high, gains[...] - high], 1)
        tile = jnp.concatenate([tile, jnp.zeros_like(tile)], 0).astype(BF16)
        out[:, 64:80, :] = jnp.broadcast_to(tile[None], (16, 16, 256))


def qkv_grad(place, h_all, dqkv, gains):
    return call(
        qkv_grad_kernel,
        (4,),
        [
            pl.BlockSpec((4, 2, 64, 1024), lambda i, place: (i, 0, 0, 0)),
            pl.BlockSpec((8, 96, 128), lambda i, place: (i, 0, 0)),
            whole(8, 128),
        ],
        whole(16, 80, 256),
        sds((16, 80, 256), BF16),
        [pltpu.VMEM((512, 1024), BF16), pltpu.VMEM((1024, 256), F32)],
        flops=2 * 2048 * 1024 * 256,
        moved=6 << 20,
        scalars=1,
    )(place, h_all, dqkv, gains)


def out_grad_kernel(left, left2, right, right2, _, out):
    a = jnp.concatenate([left[...], left2[...]], 0)
    b = jnp.concatenate([right[...], right2[...]], 0)
    product = dot(a, b, TN).astype(BF16).reshape(8, 2, 16, 512)
    out[:, :, :512] = product[:, 0]
    out[:, :, 512:] = product[:, 1]


def out_grad(left, left2, right, right2, eo):
    thin = pl.BlockSpec((128, 256), lambda i: (0, i))
    return call(
        out_grad_kernel,
        (4,),
        [thin, thin, whole(128, 512), whole(128, 512), pl.BlockSpec(memory_space=pl.ANY)],
        pl.BlockSpec((8, 16, 1024), lambda i: (i, 3, 0)),
        sds((32, 64, 1024), BF16),
        flops=2 * 256 * 1024 * 512,
        moved=3 << 20,
        aliases={4: 0},
        moving=(1, 3),
    )(left, left2, right, right2, eo)


def out_sum_kernel(pieces, out):
    out[...] = jnp.sum(pieces[...].astype(F32), axis=0).astype(BF16)


def out_sum(pieces):
    return call(
        out_sum_kernel,
        (1,),
        [pl.BlockSpec((32, 16, 1024), lambda i: (0, 3, 0))],
        whole(16, 1024),
        sds((16, 1024), BF16),
        moved=1 << 20,
        moving=(0,),
    )(pieces)


def add_pieces_kernel(which, qkv, out_w, out_w2, out, gains):
    total = jnp.sum(qkv[:, 0:64, :].astype(F32), axis=0).astype(BF16)
    out[:, 0:64, :] = jnp.broadcast_to(total[None], (16, 64, 256))
    other = (out_w[...].astype(F32) + out_w2[...].astype(F32)).astype(BF16)
    other = jnp.where(which[0] == 0, other[:, :512], other[:, 512:])
    out[:, 64:80, :] = jnp.broadcast_to(other[None, :, :256], (16, 16, 256))
    out[:, 80:96, :] = jnp.broadcast_to(other[None, :, 256:], (16, 16, 256))
    parts = [qkv[row, 64:80, :].astype(F32)[:8] for row in (0, 4, 8, 12)]
    parts = [part[:, :128] + part[:, 128:] for part in parts]
    gains[...] = parts[0] + parts[1] + parts[2] + parts[3]


def add_pieces(which, qkv, out_w, out_w2, deps):
    return call(
        add_pieces_kernel,
        (4,),
        [
            pl.BlockSpec(memory_space=pltpu.SMEM),
            whole(16, 80, 256),
            whole(16, 1024),
            whole(16, 1024),
        ],
        [pl.BlockSpec((16, 96, 256), lambda i: (i, 0, 0)), whole(8, 128)],
        [sds((64, 96, 256), BF16), sds((8, 128), F32)],
        moved=5 << 20,
        moving=(1, 3),
        deps=deps,
    )(which, qkv, out_w, out_w2)


def row_sums(product):
    total = jnp.sum(product, axis=-1, keepdims=True)
    return jnp.broadcast_to(total, (128, 128)).T[0:1]


def final_kernel(which, part, w_qkv, gain, *refs):
    out, out_w, gain_ref = refs[-3:]
    step = pl.program_id(0)
    low = low_half((64, 128))
    for zh in range(2):
        rows = slice(zh * 64, zh * 64 + 64)
        for mm in range(4):
            both = []
            for j in range(2):
                m = 2 * mm + j
                out[rows, m * 128 : (m + 1) * 128] = part[0, 0, m, zh, 0:64, 0:128].astype(F32)
                both.append(part[0, 0, m, zh, 0:64, 128:256].astype(F32))
            out[rows, 1024 + mm * 128 : 1152 + mm * 128] = jnp.where(
                low, both[0], pltpu.roll(both[1], HEAD, 1)
            )
            out[rows, 1536 + mm * 128 : 1664 + mm * 128] = jnp.where(
                low, pltpu.roll(both[0], HEAD, 1), both[1]
            )
        for m in range(8):
            out_w[0, m, zh, 0, :, 0:256] = part[0, 0, m, zh, 64:80, :].astype(F32)
            out_w[0, m, zh, 0, :, 256:512] = part[0, 0, m, zh, 80:96, :].astype(F32)

    @pl.when(step == 0)
    def _():
        gain_ref[...] = gain[...] if len(refs) == 3 else refs[0][...]

    at = pl.ds(step // 2 * 4 + which[0] * 2 + step % 2, 1)
    sums = row_sums(out[...] * w_qkv[...].astype(F32))
    gain_ref[at, :] = sums / gain[at, :]


def final(which, part, w_qkv, gain, before=()):
    def rows(i, which):
        return (i // 2 * 4 + which[0] * 2 + i % 2, 0)

    wide = pl.BlockSpec((128, 2048), rows)
    any_space = pl.BlockSpec(memory_space=pl.ANY)
    return call(
        final_kernel,
        (4,),
        [
            pl.BlockSpec((1, 1, 8, 2, 96, 256), lambda i, which: (i // 2, i % 2, 0, 0, 0, 0)),
            wide,
            whole(8, 128),
            *([whole(8, 128), any_space, any_space] if before else []),
        ],
        [
            wide,
            pl.BlockSpec(
                (1, 8, 2, 1, 16, 512), lambda i, which: (i % 2, 0, 0, i // 2, 0, which[0])
            ),
            whole(8, 128),
        ],
        [sds((1024, 2048), F32), sds((2, 8, 2, 2, 16, 1024), F32), sds((8, 128), F32)],
        moved=16 << 20,
        scalars=1,
        aliases={5: 0, 6: 1} if before else None,
        moving=(1,),
    )(which, part.reshape(2, 2, 8, 2, 96, 256), w_qkv, gain, *before)


def exchange(x):
    return lax.all_to_all(x, BLK, 0, 0, tiled=True)


def add_rounded(a, b):
    return (a.astype(F32) + b.astype(F32)).astype(BF16)


def among_experts(x):
    return lax.all_to_all(x, CHIPS, 0, 0, tiled=True, axis_index_groups=EXPERT_GROUPS)


def among_chips(x):
    return lax.all_to_all(x, CHIPS, 0, 0, tiled=True)


def shards(
    tokens, lengths, routes, gates, gain_attn, w_qkv, w_out, gain_moe, w_gate_up, w_down, cotangent
):
    core = lax.axis_index("core")
    blk = lax.axis_index(BLK)
    xh, zh = lax.axis_index("xh"), lax.axis_index("zh")
    tok = tokens.reshape(128, 1024)
    dz = cotangent.reshape(128, 1024)
    wgu = w_gate_up.reshape(1024, 1024)
    wdn = w_down.reshape(512, 1024)
    gain_a = gain_attn.reshape(1, 1024)
    gain_m = gain_moe.reshape(1, 1024)

    cos, sin = map(jnp.asarray, rope_tables())
    zl = lax.axis_index("zl").astype(jnp.int32).reshape(1)
    which = core.astype(jnp.int32).reshape(1)
    info = jnp.stack([lax.dynamic_index_in_dim(lengths, zh, 0, False), xh]).astype(jnp.int32)

    def to_partner(part):
        return lax.ppermute(part, "core", SWAP)

    pos, gate, planned = plan(routes.transpose(0, 2, 1), gates.transpose(0, 2, 1), dz)
    h, send = pre(
        blk.astype(jnp.int32).reshape(1), tok, gain_a, w_qkv, cos, sin, [hold(planned)]
    )
    planned_far = lax.ppermute(planned, ("zl", "zh"), Z_PAIRS)
    planned = jnp.stack([after(planned, hold(send)), planned_far])
    dz_all = lax.all_gather(planned, PLANE).reshape(16, 2, 144, 1024)
    arrived = exchange(send.reshape(32, 96, 128))
    o_part, ot, lse = attend(info, arrived, [corner(planned)])
    h_both = h.reshape(2, 64, 1024)
    h_mine = lax.dynamic_index_in_dim(h_both, zh, 0, keepdims=False)
    h_far = lax.ppermute(lax.dynamic_index_in_dim(h_both, 1 - zh, 0, keepdims=False), "zh", SWAP)
    h_near = jnp.stack([after(h_mine, hold(o_part)), h_far])
    o_recv = exchange(o_part).reshape(2, 8, 2, 32, 128)
    o, y, rows = mid(o_recv, w_out, tok, gain_m, pos, [corner(h_near[1])])
    o_other = to_partner(o)
    x = among_experts(rows).reshape(1536, 1024)
    place = jnp.stack([blk, zh]).astype(jnp.int32)
    dx2, eo, da, deo, hid = expert(place, x, dz_all, wgu, wdn, [corner(o_other)])
    dx2_back = among_experts(dx2.reshape(32, 48, 1024))
    experts_own, experts_send = expert_grad(which, x, da, hid, deo)
    dy, dbr_own, dbr_send, do = mid_back(
        which, dx2_back, pos, y, gain_m, dz, w_out, [hold(experts_send)]
    )
    experts_own = add_rounded(experts_own, to_partner(experts_send))
    experts_far = lax.ppermute(experts_own, "zl", SWAP)
    h_near = after(h_near, hold(experts_send))
    h_all = lax.all_gather(h_near, PLANE).reshape(16, 2, 64, 1024)


    do_recv = exchange(do.reshape(32, 48, 128))
    eo = out_grad(o, o_other, dbr_own, to_partner(dbr_send), eo)
    eo_back = among_experts(after(eo, do_recv))
    mixed = combine(eo_back, pos, gate, y)
    out_part = out_sum(eo_back)
    out_far = lax.ppermute(out_part, "zl", SWAP)
    dqkv, gains = attend_back(info, arrived, do_recv, ot, lse, cos, sin, [])
    experts_own = add_rounded(after(experts_own, hold(dqkv)), experts_far)

    place = jnp.stack([xh, zh]).astype(jnp.int32)
    dqkv_recv = exchange(after(dqkv, eo_back)).reshape(2, 8, 2, 96, 128)
    qkv_partial = after(qkv_grad(place, h_all, dqkv, gains), dqkv_recv, corner(experts_own))
    qkv_pieces = lax.all_to_all(qkv_partial, SAME_COLUMNS, 0, 0, tiled=True)
    experts_other = to_partner(experts_own)
    grad_gate_up, grad_down = final_expert(which, experts_own, experts_other)
    copies, gains = add_pieces(
        zl, qkv_pieces, out_part, out_far, []
    )
    grad_tokens = last(dqkv_recv, w_qkv, tok, gain_a, dy, [])
    own = after(among_chips(copies), hold(mixed), hold(grad_gate_up), hold(grad_tokens))
    rows = final(which, own, w_qkv, gain_attn.reshape(8, 128))
    grad_qkv, grad_out, grad_gain_attn = final(
        1 - which, to_partner(own), w_qkv, gain_attn.reshape(8, 128), (rows[2], rows[0], rows[1])
    )

    return (
        mixed.reshape(2, 64, 1024),
        grad_tokens.reshape(2, 64, 1024),
        grad_gain_attn.reshape(1024),
        grad_qkv,
        grad_out.reshape(1024, 1024),
        gains.reshape(1024),
        grad_gate_up[None],
        grad_down[None],
    )


def solution(mesh):
    split = Mesh(mesh.devices.reshape(2, 2, 2, 2, 4, 2), AXES)
    rows = P(ROWS, BLK, None)
    return jax.shard_map(
        shards,
        mesh=split,
        in_specs=(
            rows,
            P(ROWS),
            rows,
            rows,
            P(),
            P(),
            P(),
            P(),
            P(BLK, None, None),
            P(BLK, None, None),
            rows,
        ),
        out_specs=(
            rows,
            rows,
            P(),
            P(),
            P(),
            P(),
            P(BLK, None, None),
            P(BLK, None, None),
        ),
        check_vma=False,
    )
```

```python
import jax
import jax.numpy as jnp
import numpy as np
from jax import lax
from jax.experimental import pallas as pl
from jax.experimental.pallas import tpu as pltpu
from jax.sharding import Mesh
from jax.sharding import PartitionSpec as P

HEADS = 16
KV_HEADS = 8
HEAD = 64
FF_EXP = 512
TOP = 8
MOST = 24
EPS = 1e-06
ROPE_BASE = 10000.0
SCALE = HEAD ** (-0.5)

ROWS = ("zl", "core")
PLANE = ("xh", "xl", "y")
BLK = ("xh", "xl", "y", "zh")
CHIPS = ("zl", "xh", "xl", "y", "zh")
AXES = ("zl", "core", "xh", "xl", "y", "zh")
SAME_COLUMNS = ("zl", "core", "xh", "zh")
SWAP = [(0, 1), (1, 0)]
EXPERT_GROUPS = [
    [(parity ^ zh) * 32 + xy * 2 + zh for xy in range(16) for zh in range(2)] for parity in range(2)
]
Z_PAIRS = [(i, 3 - i) for i in range(4)]
F32 = jnp.float32
BF16 = jnp.bfloat16
NT = (((1,), (1,)), ((), ()))
TN = (((0,), (0,)), ((), ()))


def rope_tables():
    lane = np.arange(128) % HEAD
    frequency = (ROPE_BASE ** (-(lane % 32) / 32.0)).astype(np.float32)
    angles = np.arange(2048, dtype=np.float32)[:, None] * frequency[None, :]
    sign = np.where(lane < 32, -1.0, 1.0)
    cosine = np.cos(angles.astype(np.float64)).astype(np.float32)
    return cosine, (np.sin(angles.astype(np.float64)) * sign).astype(np.float32)


def dot(left, right, dims=(((1,), (0,)), ((), ()))):
    return lax.dot_general(left, right, dims, preferred_element_type=F32)


def call(
    kernel,
    grid,
    in_specs,
    out_specs,
    out_shape,
    scratch=(),
    mb=24,
    flops=0,
    moved=0,
    deps=(),
    scalars=0,
    aliases=None,
    moving=(),
):
    count = len(in_specs) + scalars

    def place(i, x):
        small = i < scalars or in_specs[i - scalars].memory_space == pltpu.SMEM
        return x if small or i in moving else hold(x)

    def body(*refs):
        kernel(*refs[:count], *refs[count + len(deps) :])

    built = pl.pallas_call(
        body,
        grid_spec=pltpu.PrefetchScalarGridSpec(
            num_scalar_prefetch=scalars,
            grid=grid,
            in_specs=[*in_specs, *[pl.BlockSpec(memory_space=pl.ANY)] * len(deps)],
            out_specs=out_specs,
            scratch_shapes=list(scratch),
        ),
        out_shape=out_shape,
        input_output_aliases=aliases or {},
        compiler_params=pltpu.CompilerParams(vmem_limit_bytes=mb * 1024 * 1024),
        cost_estimate=pl.CostEstimate(flops=flops, bytes_accessed=moved, transcendentals=0),
    )
    return lambda *operands: built(*[place(i, x) for i, x in enumerate(operands)], *deps)


def after(x, *deps):
    any_space = pl.BlockSpec(memory_space=pl.ANY)
    return pl.pallas_call(
        lambda *refs: None,
        in_specs=[any_space] * (1 + len(deps)),
        out_specs=any_space,
        out_shape=sds(x.shape, x.dtype),
        input_output_aliases={0: 0},
        compiler_params=pltpu.CompilerParams(vmem_limit_bytes=1024 * 1024),
    )(hold(x), *deps)


def await_all(x, *deps):
    any_space = pl.BlockSpec(memory_space=pl.ANY)
    return pl.pallas_call(
        lambda *refs: None,
        in_specs=[any_space] * (1 + len(deps)),
        out_specs=any_space,
        out_shape=jax.ShapeDtypeStruct(x.shape, x.dtype),
        input_output_aliases={0: 0},
        compiler_params=pltpu.CompilerParams(vmem_limit_bytes=1024 * 1024),
    )(x, *deps)


def hold(x):
    return pltpu.with_memory_space_constraint(x, pltpu.HBM)


def corner(x):
    return x[(0,) * (x.ndim - 2)][:8, :128]


def whole(*shape):
    return pl.BlockSpec(shape, lambda *_: (0,) * len(shape))


def sds(shape, dtype):
    return pltpu.HBM(shape, dtype)


def low_half(shape):
    return lax.broadcasted_iota(jnp.int32, shape, len(shape) - 1) < HEAD


def swap_halves(u):
    lane = lax.broadcasted_iota(jnp.int32, u.shape, 1)
    return jnp.where(lane % HEAD < HEAD // 2, pltpu.roll(u, 96, 1), pltpu.roll(u, 32, 1))


def pre_kernel(blk, tok, gain, wq, wk, wv, cos, sin, h_ref, send):
    @pl.when(pl.program_id(0) == 0)
    def _():
        x = tok[...].astype(F32)
        inverse = lax.rsqrt(jnp.mean(x * x, axis=-1, keepdims=True) + EPS)
        h_ref[...] = (x * inverse * gain[...]).astype(BF16)

    h = h_ref[...]
    c = jnp.concatenate([cos[...], cos[...]], 0)
    s = jnp.concatenate([sin[...], sin[...]], 0)

    def rope(u):
        return u * c + swap_halves(u) * s

    q = dot(h, wq[...])
    k = rope(dot(h, wk[...]))
    v = dot(h, wv[...])
    low = low_half(k.shape)
    pairs = (
        jnp.where(low, k, pltpu.roll(v, HEAD, 1)).astype(BF16),
        jnp.where(low, pltpu.roll(k, HEAD, 1), v).astype(BF16),
    )
    for j in range(2):
        qj = (rope(q[:, j * 128 : (j + 1) * 128]).astype(BF16).astype(F32) * SCALE).astype(BF16)
        for t in range(2):
            for half in range(2):
                first = t * 64 + half * 32
                send[half, j, t, 0:32, :] = qj[first : first + 32]
                send[half, j, t, 32:96, :] = pairs[j][t * 64 : t * 64 + 64]


def pre(blk, tok, gain, w_qkv, cos, sin, deps):
    places = pl.BlockSpec((64, 128), lambda m, blk: (blk[0], 0))
    return call(
        pre_kernel,
        (4,),
        [
            whole(128, 1024),
            whole(1, 1024),
            pl.BlockSpec((1024, 256), lambda m, blk: (0, m)),
            pl.BlockSpec((1024, 128), lambda m, blk: (0, 8 + m)),
            pl.BlockSpec((1024, 128), lambda m, blk: (0, 12 + m)),
            places,
            places,
        ],
        [whole(128, 1024), pl.BlockSpec((2, 2, 2, 96, 128), lambda m, blk: (0, m, 0, 0, 0))],
        [sds((128, 1024), BF16), sds((2, 8, 2, 96, 128), BF16)],
        flops=2 * 128 * 1024 * 2048,
        moved=5 << 20,
        scalars=1,
        deps=deps,
    )(blk, tok, gain, w_qkv, w_qkv, w_qkv, cos, sin)


def plan_kernel(routes, gates, pos_ref, gate_ref, out):
    named = jnp.concatenate([routes[0], routes[1]], 1).astype(F32)
    weights = jnp.concatenate([gates[0], gates[1]], 1)
    experts = lax.broadcasted_iota(jnp.int32, (32, 128), 0).astype(F32)
    chosen = jnp.zeros((32, 128), F32)
    gate = jnp.zeros((32, 128), F32)
    for k in range(TOP):
        match = named[k : k + 1] == experts
        chosen = jnp.where(match, 1.0, chosen)
        gate = jnp.where(match, weights[k : k + 1], gate)
    row = lax.broadcasted_iota(jnp.int32, (128, 128), 0)
    before = jnp.where(row < lax.broadcasted_iota(jnp.int32, (128, 128), 1), 1.0, 0.0)
    rank = dot(chosen.astype(BF16), before.astype(BF16))
    pos = jnp.where(chosen > 0.0, rank, -1.0)
    pos_ref[...] = pos.astype(jnp.int32)
    gate_ref[...] = gate
    high = gate.astype(BF16).astype(F32)
    rest = gate - high
    for j in range(8):
        part = slice(4 * j, 4 * j + 4)
        tile = jnp.concatenate([pos[part], high[part], rest[part], jnp.zeros((4, 128), F32)], 0)
        out[:, j * 128 : (j + 1) * 128] = tile.astype(BF16)


def plan(routes, gates):
    return call(
        plan_kernel,
        (1,),
        [whole(2, 8, 64), whole(2, 8, 64)],
        [whole(32, 128), whole(32, 128), whole(16, 1024)],
        [sds((32, 128), jnp.int32), sds((32, 128), F32), sds((16, 1024), BF16)],
        moved=1 << 17,
    )(routes, gates)


def pack_kernel(dz, info, dz_far, info_far, out):
    out[0, 0:128, :] = dz[...]
    out[0, 128:144, :] = info[...]
    out[1, 0:128, :] = dz_far[...]
    out[1, 128:144, :] = info_far[...]


def pack(dz, info, dz_far, info_far, deps):
    return call(
        pack_kernel,
        (1,),
        [whole(128, 1024), whole(16, 1024), whole(128, 1024), whole(16, 1024)],
        whole(2, 144, 1024),
        sds((2, 144, 1024), BF16),
        moved=1 << 20,
        moving=(2, 3),
        deps=deps,
    )(dz, info, dz_far, info_far)


def split_queries(q):
    qf = q.astype(F32)
    low = low_half(qf.shape)
    first = jnp.where(low, qf, 0.0)
    second = jnp.where(low, pltpu.roll(qf, HEAD, 1), 0.0)
    return jnp.concatenate([first, second], 0).astype(BF16)


def limits(tile, info):
    place = lax.broadcasted_iota(jnp.int32, (1, 512), 1) % 256
    position = (tile * 8 + place // 32) * 64 + info[1] * 32 + place % 32
    return jnp.minimum(position, info[0] - 1)


def load_pairs(x_ref, kv, kvt):
    kv[...] = x_ref[:, 32:96, :].reshape(2048, 128)
    for c in range(8):
        rows = slice(c * 256, (c + 1) * 256)
        kvt[:, rows] = kv[rows, :].astype(F32).T.astype(BF16)


def attend_kernel(info, x_ref, o_ref, ot_ref, lse_ref, kv, kvt):
    load_pairs(x_ref, kv, kvt)
    for tile in range(4):
        q2 = split_queries(x_ref[tile * 8 : (tile + 1) * 8, 0:32, :].reshape(256, 128))
        limit = limits(tile, info)
        keys = (tile + 1) * 512
        s = dot(kv[0:keys, :], q2, NT)
        place = lax.broadcasted_iota(jnp.int32, (keys, 1), 0)
        s = jnp.where(place <= limit, s, -1e30)
        top = jnp.max(s, axis=0, keepdims=True)
        p = jnp.exp(s - top)
        total = jnp.sum(p, axis=0, keepdims=True)
        out = dot(kvt[64:128, 0:keys], p.astype(BF16)) / total
        ot_ref[tile] = out
        lse_ref[tile] = jnp.broadcast_to(top + jnp.log(total), (8, 512))
        both = jnp.concatenate([out[:, :256], out[:, 256:]], 0).T
        o_ref[tile * 8 : (tile + 1) * 8] = both.astype(BF16).reshape(8, 32, 128)


def attend(info, arrived, deps):
    return call(
        attend_kernel,
        (1,),
        [pl.BlockSpec(memory_space=pltpu.SMEM), whole(32, 96, 128)],
        [whole(32, 32, 128), whole(4, 64, 512), whole(4, 8, 512)],
        [sds((32, 32, 128), BF16), sds((4, 64, 512), F32), sds((4, 8, 512), F32)],
        [pltpu.VMEM((2048, 128), BF16), pltpu.VMEM((128, 2048), BF16)],
        flops=4 * 2048 * 1280 * 128,
        moved=2 << 20,
        deps=deps,
        moving=(1,),
    )(info, arrived)


def attend_back_kernel(
    info, x_ref, do_ref, ot_ref, lse_ref, cos, sin, out_ref, gain_ref, kv, kvt, total
):
    load_pairs(x_ref, kv, kvt)
    total[...] = jnp.zeros_like(total)
    for tile in range(4):
        q2 = split_queries(x_ref[tile * 8 : (tile + 1) * 8, 0:32, :].reshape(256, 128))
        grad = do_ref[tile * 8 : (tile + 1) * 8, 0:32, :].reshape(256, 128).astype(F32)
        low = low_half(grad.shape)
        do2 = jnp.concatenate(
            [jnp.where(low, 0.0, pltpu.roll(grad, HEAD, 1)), jnp.where(low, 0.0, grad)], 0
        ).astype(BF16)
        grad_t = grad.T
        grad_t = jnp.concatenate([grad_t[:64], grad_t[64:]], 1)
        inner = jnp.sum(grad_t * ot_ref[tile], axis=0, keepdims=True)
        lse = lse_ref[tile][0:1]
        limit = limits(tile, info)

        def step(c, acc):
            at = pl.ds(pl.multiple_of(c * 256, 256), 256)
            part = kv[at, :]
            s = dot(part, q2, NT)
            place = c * 256 + lax.broadcasted_iota(jnp.int32, (256, 1), 0)
            p = jnp.exp(jnp.where(place <= limit, s, -1e30) - lse)
            ds = (p * (dot(part, do2, NT) - inner)).astype(BF16)
            total[at, :] += dot(ds, q2) + dot(p.astype(BF16), do2)
            return acc + dot(kvt[0:64, at], ds)

        acc = lax.fori_loop(0, 2 * tile + 2, step, jnp.zeros((64, 512), F32))
        dq = jnp.concatenate([acc[:, :256], acc[:, 256:]], 0).T
        at = (slice(tile * 8, tile * 8 + 8), pl.ds(pl.multiple_of(info[1] * 32, 32), 32))
        c, s = cos[at].reshape(256, 128), sin[at].reshape(256, 128)
        dq = ((dq * c - swap_halves(dq) * s) * SCALE).astype(BF16)
        out_ref[tile * 8 : (tile + 1) * 8, 0:32, :] = dq.reshape(8, 32, 128)
    for tile in range(4):
        blocks = slice(tile * 8, tile * 8 + 8)
        part = total[tile * 512 : (tile + 1) * 512, :]
        turned = part * cos[blocks].reshape(512, 128) - swap_halves(part) * sin[
            blocks
        ].reshape(512, 128)
        part = jnp.where(low_half(part.shape), turned, part)
        out_ref[blocks, 32:96, :] = part.astype(BF16).reshape(8, 64, 128)
    gains = jnp.sum(do_ref[:, 32:48, :].astype(F32), axis=0)
    gain_ref[...] = gains[:8] + gains[8:]


def attend_back(info, arrived, grad, ot, lse, cos, sin, deps):
    return call(
        attend_back_kernel,
        (1,),
        [
            pl.BlockSpec(memory_space=pltpu.SMEM),
            whole(32, 96, 128),
            whole(32, 48, 128),
            whole(4, 64, 512),
            whole(4, 8, 512),
            whole(32, 64, 128),
            whole(32, 64, 128),
        ],
        [whole(32, 96, 128), whole(8, 128)],
        [sds((32, 96, 128), BF16), sds((8, 128), F32)],
        [pltpu.VMEM((2048, 128), BF16), pltpu.VMEM((128, 2048), BF16), pltpu.VMEM((2048, 128), F32)],
        flops=10 * 2048 * 1280 * 128,
        moved=3 << 20,
        deps=deps,
        moving=(1, 2,),
    )(info, arrived, grad, ot, lse, cos.reshape(32, 64, 128), sin.reshape(32, 64, 128))


def placement(pos):
    shape = (pos.shape[0], 48, 128)
    slots = lax.broadcasted_iota(jnp.int32, shape, 1)
    return (pos[...][:, None, :] == slots).reshape(shape[0] * 48, 128)


def gated(pos, gate):
    placed = placement(pos)
    weight = jnp.broadcast_to(gate[...][:, None, :], (pos.shape[0], 48, 128))
    weight = jnp.where(placed, weight.reshape(placed.shape), 0.0)
    high = weight.astype(BF16)
    return high, (weight - high.astype(F32)).astype(BF16)


PLACE = pl.BlockSpec((16, 128), lambda e: (e, 0))
SLOTS = pl.BlockSpec((16, 48, 1024), lambda e: (e, 0, 0))


def mid_kernel(recv, w0, w1, w2, w3, tok, gain, pos, o_ref, y_ref, out, h2):
    @pl.when(pl.program_id(0) == 0)
    def _():
        for s in range(2):
            for half in range(2):
                first = s * 64 + half * 32
                for m in range(8):
                    o_ref[first : first + 32, m * 128 : (m + 1) * 128] = recv[half, m, s]
        o = o_ref[...]
        branch = jnp.concatenate([dot(o, w[...]) for w in (w0, w1, w2, w3)], 1)
        y = tok[...].astype(F32) + branch
        y_ref[...] = y
        inverse = lax.rsqrt(jnp.mean(y * y, axis=-1, keepdims=True) + EPS)
        h2[...] = (y * inverse * gain[...]).astype(BF16)

    placed = placement(pos).astype(F32).astype(BF16)
    out[...] = dot(placed, h2[...]).astype(BF16).reshape(out.shape)


def mid(recv, w_out, tok, gain, pos, deps):
    return call(
        mid_kernel,
        (2,),
        [
            whole(2, 8, 2, 32, 128),
            *[pl.BlockSpec((1024, 256), lambda e, j=j: (0, j)) for j in range(4)],
            whole(128, 1024),
            whole(1, 1024),
            PLACE,
        ],
        [whole(128, 1024), whole(128, 1024), SLOTS],
        [sds((128, 1024), BF16), sds((128, 1024), F32), sds((32, 48, 1024), BF16)],
        [pltpu.VMEM((128, 1024), BF16)],
        flops=2 * 128 * 1024 * 1024 + 2 * 1536 * 128 * 1024,
        moved=6 << 20,
        moving=(0,),
        deps=deps,
    )(recv, w_out, w_out, w_out, w_out, tok, gain, pos)


def expert_kernel(which, x_ref, info, dz, g0, g1, u0, u1, d0, d1, dx2, da_ref, deo_ref, hid_ref):
    slots = lax.broadcasted_iota(jnp.int32, (48, 128), 0).astype(F32)
    rows16 = lax.broadcasted_iota(jnp.int32, (16, 128), 0)
    blank = jnp.zeros((48, 128), F32)
    mine = which[0] % 4
    for pair in range(PLACES):
        parts, weights = [], []
        for j in range(2):
            tile = info[pair, j].astype(F32)

            def pick(k):
                return jnp.sum(jnp.where(rows16 == mine + 4 * k, tile, 0.0), axis=0, keepdims=True)

            hot = jnp.where(slots == pick(0), 1.0, 0.0)
            weights.append(jnp.sum(hot * (pick(1) + pick(2)), axis=1, keepdims=True))
            parts.append(jnp.concatenate([hot, blank] if j == 0 else [blank, hot], 1))
        rows = dot(jnp.concatenate(parts, 0).astype(BF16), dz[pair].reshape(256, 1024))
        rows = (rows * jnp.concatenate(weights, 0)).astype(BF16)
        for j in range(2):
            first = pl.multiple_of(pair * 96 + (which[1] ^ j) * 48, 48)
            deo_ref[pl.ds(first, 48), :] = rows[j * 48 : (j + 1) * 48]
    x, deo = x_ref[...], deo_ref[...]
    for part, (wg, wu) in enumerate(((g0, u0), (g1, u1))):
        at = slice(part * 256, part * 256 + 256)
        late = slice(part * 256 + FF_EXP, part * 256 + FF_EXP + 256)
        gate, up = dot(x, wg[...]), dot(x, wu[...])
        dhid = dot(deo[:, :512], d0[at, :], NT) + dot(deo[:, 512:], d1[at, :], NT)
        sig = jax.nn.sigmoid(gate)
        act = gate * sig
        hid_ref[:, at] = (act * up).astype(BF16)
        da_ref[:, at] = (dhid * up * sig * (1.0 + gate * (1.0 - sig))).astype(BF16)
        da_ref[:, late] = (dhid * act).astype(BF16)
    total = dot(da_ref[:, 0:256], g0[...], NT) + dot(da_ref[:, 256:512], g1[...], NT)
    total += dot(da_ref[:, 512:768], u0[...], NT) + dot(da_ref[:, 768:1024], u1[...], NT)
    dx2[...] = total.astype(BF16)


PLACES = 4


def expert(which, x, dz_all, wgu, wdn, deps):
    count = PLACES * 96
    rows = pl.BlockSpec((count, 1024), lambda i, which: (i, 0))
    return call(
        expert_kernel,
        (16 // PLACES,),
        [
            rows,
            pl.BlockSpec((PLACES, 2, 16, 128), lambda i, which: (i, 0, 8, which[0] // 4)),
            pl.BlockSpec((PLACES, 2, 128, 1024), lambda i, which: (i, 0, 0, 0)),
            *[pl.BlockSpec((1024, 256), lambda i, which, j=j: (0, j)) for j in range(4)],
            *[pl.BlockSpec((512, 512), lambda i, which, j=j: (0, j)) for j in range(2)],
        ],
        [rows, rows, rows, pl.BlockSpec((count, 512), lambda i, which: (i, 0))],
        [*[sds((1536, 1024), BF16)] * 3, sds((1536, 512), BF16)],
        mb=32,
        flops=2 * 1536 * 1024 * 2816,
        moved=26 << 20,
        scalars=1,
        moving=(1,),
        deps=deps,
    )(which, x, dz_all, dz_all, wgu, wgu, wgu, wgu, wdn, wdn)


def expert_out_kernel(hid, d0, d1, eo):
    eo[:, 0:48, :512] = dot(hid[...], d0[...]).astype(BF16).reshape(8, 48, 512)
    eo[:, 0:48, 512:] = dot(hid[...], d1[...]).astype(BF16).reshape(8, 48, 512)


def expert_out(hid, wdn):
    return call(
        expert_out_kernel,
        (4,),
        [
            pl.BlockSpec((384, 512), lambda i: (i, 0)),
            *[pl.BlockSpec((512, 512), lambda i, j=j: (0, j)) for j in range(2)],
        ],
        pl.BlockSpec((8, 64, 1024), lambda i: (i, 0, 0)),
        sds((32, 64, 1024), BF16),
        flops=2 * 1536 * 1024 * 512,
        moved=7 << 20,
    )(hid, wdn, wdn)


def expert_grad_kernel(core, x_ref, da, hid, deo, own, other):
    step = pl.program_id(0)

    for first, out in ((0, own), (3, other)):

        @pl.when((step >= first) & (step < first + 2))
        def _():
            out[...] = dot(x_ref[...], da[...], TN).astype(BF16)

        @pl.when(step == first + 2)
        def _():
            out[...] = dot(hid[...], deo[...], TN).astype(BF16)


def expert_grad(core, x, da, hid, deo):
    def half(i, core):
        return jnp.where(i < 3, core[0], 1 - core[0])

    return call(
        expert_grad_kernel,
        (6,),
        [
            pl.BlockSpec((1536, 256), lambda i, c: (0, half(i, c) * 2 + jnp.minimum(i % 3, 1))),
            whole(1536, 1024),
            pl.BlockSpec((1536, 256), lambda i, c: (0, half(i, c))),
            whole(1536, 1024),
        ],
        [
            pl.BlockSpec((256, 1024), lambda i, c: (jnp.minimum(i, 2), 0)),
            pl.BlockSpec((256, 1024), lambda i, c: (jnp.maximum(i - 3, 0), 0)),
        ],
        [sds((768, 1024), BF16)] * 2,
        flops=2 * 1536 * 1024 * 1536,
        moved=16 << 20,
        scalars=1,
        moving=(1,),
    )(core, x, da, hid, deo)


def final_expert_kernel(core, own, other, gate_up, down):
    step = pl.program_id(0)
    half = jnp.where(step < 4, step // 2, step - 4)

    def write(out):
        @pl.when(half == core[0])
        def _():
            out[...] = own[...].astype(F32)

        @pl.when(half != core[0])
        def _():
            out[...] = other[...].astype(F32)

    @pl.when(step < 4)
    def _():
        write(gate_up)

    @pl.when(step >= 4)
    def _():
        write(down)


def final_expert(core, own, other):
    part = pl.BlockSpec((256, 1024), lambda i: (jnp.where(i < 4, i % 2, 2), 0))
    return call(
        final_expert_kernel,
        (6,),
        [pl.BlockSpec(memory_space=pltpu.SMEM), part, part],
        [
            pl.BlockSpec((256, 1024), lambda i: (jnp.minimum(i, 3), 0)),
            pl.BlockSpec((256, 1024), lambda i: (jnp.maximum(i - 4, 0), 0)),
        ],
        [sds((1024, 1024), F32), sds((512, 1024), F32)],
        moved=9 << 20,
        moving=(1, 2,),
    )(core, own, other)


def norm_back(incoming, gain, vectors):
    inverse = lax.rsqrt(jnp.mean(vectors * vectors, axis=-1, keepdims=True) + EPS)
    scaled = vectors * inverse
    weighted = incoming * gain
    mean = jnp.mean(weighted * scaled, axis=-1, keepdims=True)
    return inverse * (weighted - scaled * mean), scaled


def mid_back_kernel(
    core, back, pos, y, gain, dz, w0, w1, w2, w3, dy_ref, own, other, send
):
    placed = placement(pos).astype(F32).astype(BF16)
    dh2 = dot(placed, back[...].reshape(1536, 1024), TN)
    dv, scaled = norm_back(dh2, gain[...], y[...])
    gains = jnp.sum(dh2 * scaled, axis=0, keepdims=True)
    row = lax.broadcasted_iota(jnp.int32, (8, 128), 0)
    tile = jnp.zeros((8, 128), F32)
    for r in range(8):
        tile = jnp.where(row == r, gains[:, r * 128 : (r + 1) * 128], tile)
    high = tile.astype(BF16).astype(F32)
    extra = jnp.concatenate([high, tile - high], 0).astype(BF16)
    dy = dz[...].astype(F32) + dv
    dy_ref[...] = dy
    dbr = dy.astype(BF16)

    @pl.when(core[0] == 0)
    def _():
        own[...] = dbr[:, :512]
        other[...] = dbr[:, 512:]

    @pl.when(core[0] == 1)
    def _():
        own[...] = dbr[:, 512:]
        other[...] = dbr[:, :512]

    do = jnp.concatenate([dot(dbr, w[...], NT) for w in (w0, w1, w2, w3)], 1).astype(BF16)
    for s in range(2):
        for half in range(2):
            first = s * 64 + half * 32
            for m in range(8):
                send[half, m, s, 0:32, :] = do[first : first + 32, m * 128 : (m + 1) * 128]
                send[half, m, s, 32:48, :] = extra


def mid_back(core, back, pos, y, gain, dz, w_out, deps):
    return call(
        mid_back_kernel,
        (1,),
        [
            pl.BlockSpec(memory_space=pltpu.SMEM),
            whole(32, 48, 1024),
            whole(32, 128),
            whole(128, 1024),
            whole(1, 1024),
            whole(128, 1024),
            *[pl.BlockSpec((256, 1024), lambda e, j=j: (j, 0)) for j in range(4)],
        ],
        [whole(128, 1024), whole(128, 512), whole(128, 512), whole(2, 8, 2, 48, 128)],
        [
            sds((128, 1024), F32),
            sds((128, 512), BF16),
            sds((128, 512), BF16),
            sds((2, 8, 2, 48, 128), BF16),
        ],
        flops=2 * 128 * 1024 * 1024 + 2 * 1536 * 128 * 1024,
        moved=6 << 20,
        deps=deps,
        moving=(1,),
    )(core, back, pos, y, gain, dz, w_out, w_out, w_out, w_out)


def combine_kernel(back, pos, gate, y, out):
    high, rest = gated(pos, gate)
    rows = back[...].reshape(1536, 1024)
    out[...] = (y[...] + dot(high, rows, TN) + dot(rest, rows, TN)).astype(BF16)


def combine(back, pos, gate, y):
    return call(
        combine_kernel,
        (1,),
        [
            pl.BlockSpec((32, 48, 1024), lambda _: (0, 0, 0)),
            whole(32, 128),
            whole(32, 128),
            whole(128, 1024),
        ],
        whole(128, 1024),
        sds((128, 1024), BF16),
        flops=4 * 1536 * 128 * 1024,
        moved=4 << 20,
        moving=(0,),
    )(back, pos, gate, y)


def last_kernel(recv, w0, w1, w2, w3, tok, gain, dy, grad_tokens, dproj):
    low = low_half((64, 128))
    for t in range(2):
        rows = slice(t * 64, t * 64 + 64)
        for mm in range(4):
            both = []
            for j in range(2):
                m = 2 * mm + j
                dq = jnp.concatenate([recv[0, m, t, 0:32, :], recv[1, m, t, 0:32, :]], 0)
                dproj[rows, m * 128 : (m + 1) * 128] = dq
                both.append(
                    recv[0, m, t, 32:96, :].astype(F32) + recv[1, m, t, 32:96, :].astype(F32)
                )
            dk = jnp.where(low, both[0], pltpu.roll(both[1], HEAD, 1))
            dv = jnp.where(low, pltpu.roll(both[0], HEAD, 1), both[1])
            dproj[rows, 1024 + mm * 128 : 1152 + mm * 128] = dk.astype(BF16)
            dproj[rows, 1536 + mm * 128 : 1664 + mm * 128] = dv.astype(BF16)
    d = dproj[...]
    dh = jnp.concatenate([dot(d, w[...], NT) for w in (w0, w1, w2, w3)], 1)
    dv, _ = norm_back(dh, gain[...], tok[...].astype(F32))
    grad_tokens[...] = dy[...] + dv


def last(recv, w_qkv, tok, gain, dy, deps):
    return call(
        last_kernel,
        (1,),
        [
            whole(2, 8, 2, 96, 128),
            *[pl.BlockSpec((256, 2048), lambda _, j=j: (j, 0)) for j in range(4)],
            whole(128, 1024),
            whole(1, 1024),
            whole(128, 1024),
        ],
        whole(128, 1024),
        sds((128, 1024), F32),
        [pltpu.VMEM((128, 2048), BF16)],
        flops=2 * 128 * 1024 * 2048,
        moved=6 << 20,
        deps=deps,
        moving=(0,),
    )(recv, w_qkv, w_qkv, w_qkv, w_qkv, tok, gain, dy)


def qkv_grad_kernel(place, h_all, d_ref, gains, out, rows, acc):
    step = pl.program_id(0)
    for pair in range(4):
        for zh in range(2):
            first = (pair * 2 + zh) * 64
            rows[first : first + 64, :] = h_all[pair, place[1] ^ zh]
    dq = d_ref[:, 0:32, :]
    none = jnp.zeros_like(dq)
    dq = jnp.where(place[0] == 0, jnp.concatenate([dq, none], 1), jnp.concatenate([none, dq], 1))
    both = jnp.concatenate([dq.reshape(512, 128), d_ref[:, 32:96, :].reshape(512, 128)], 1)
    product = dot(rows[...], both, TN)

    @pl.when(step == 0)
    def _():
        acc[...] = product

    @pl.when((step > 0) & (step < 3))
    def _():
        acc[...] += product

    @pl.when(step == 3)
    def _():
        out[:, 0:64, :] = (acc[...] + product).astype(BF16).reshape(16, 64, 256)
        high = gains[...].astype(BF16).astype(F32)
        tile = jnp.concatenate([high, gains[...] - high], 1)
        tile = jnp.concatenate([tile, jnp.zeros_like(tile)], 0).astype(BF16)
        out[:, 64:80, :] = jnp.broadcast_to(tile[None], (16, 16, 256))


def qkv_grad(place, h_all, dqkv, gains):
    return call(
        qkv_grad_kernel,
        (4,),
        [
            pl.BlockSpec((4, 2, 64, 1024), lambda i, place: (i, 0, 0, 0)),
            pl.BlockSpec((8, 96, 128), lambda i, place: (i, 0, 0)),
            whole(8, 128),
        ],
        whole(16, 80, 256),
        sds((16, 80, 256), BF16),
        [pltpu.VMEM((512, 1024), BF16), pltpu.VMEM((1024, 256), F32)],
        flops=2 * 2048 * 1024 * 256,
        moved=6 << 20,
        scalars=1,
    )(place, h_all, dqkv, gains)


def out_grad_kernel(left, left2, right, right2, _, out):
    a = jnp.concatenate([left[...], left2[...]], 0)
    b = jnp.concatenate([right[...], right2[...]], 0)
    product = dot(a, b, TN).astype(BF16).reshape(8, 2, 16, 512)
    out[:, :, :512] = product[:, 0]
    out[:, :, 512:] = product[:, 1]


def out_grad(left, left2, right, right2, eo):
    thin = pl.BlockSpec((128, 256), lambda i: (0, i))
    return call(
        out_grad_kernel,
        (4,),
        [thin, thin, whole(128, 512), whole(128, 512), pl.BlockSpec(memory_space=pl.ANY)],
        pl.BlockSpec((8, 16, 1024), lambda i: (i, 3, 0)),
        sds((32, 64, 1024), BF16),
        flops=2 * 256 * 1024 * 512,
        moved=3 << 20,
        aliases={4: 0},
        moving=(1, 3),
    )(left, left2, right, right2, eo)


def out_sum_kernel(pieces, out):
    out[...] = jnp.sum(pieces[...].astype(F32), axis=0).astype(BF16)


def out_sum(pieces):
    return call(
        out_sum_kernel,
        (1,),
        [pl.BlockSpec((32, 16, 1024), lambda i: (0, 3, 0))],
        whole(16, 1024),
        sds((16, 1024), BF16),
        moved=1 << 20,
        moving=(0,),
    )(pieces)


def add_pieces_kernel(which, qkv, out_w, out_w2, out, gains):
    total = jnp.sum(qkv[:, 0:64, :].astype(F32), axis=0).astype(BF16)
    out[:, 0:64, :] = jnp.broadcast_to(total[None], (32, 64, 256))
    other = (out_w[...].astype(F32) + out_w2[...].astype(F32)).astype(BF16)
    other = jnp.where(which[0] == 0, other[:, :512], other[:, 512:])
    out[:, 64:80, :] = jnp.broadcast_to(other[None, :, :256], (32, 16, 256))
    out[:, 80:96, :] = jnp.broadcast_to(other[None, :, 256:], (32, 16, 256))
    parts = [qkv[row, 64:80, :].astype(F32)[:8] for row in (0, 4, 8, 12)]
    parts = [part[:, :128] + part[:, 128:] for part in parts]
    gains[...] = parts[0] + parts[1] + parts[2] + parts[3]


def add_pieces(which, qkv, out_w, out_w2, deps):
    return call(
        add_pieces_kernel,
        (2,),
        [
            pl.BlockSpec(memory_space=pltpu.SMEM),
            whole(16, 80, 256),
            whole(16, 1024),
            whole(16, 1024),
        ],
        [pl.BlockSpec((32, 96, 256), lambda i: (i, 0, 0)), whole(8, 128)],
        [sds((64, 96, 256), BF16), sds((8, 128), F32)],
        moved=5 << 20,
        moving=(1, 3),
        deps=deps,
    )(which, qkv, out_w, out_w2)


def row_sums(product):
    total = jnp.sum(product, axis=-1, keepdims=True)
    return jnp.broadcast_to(total, (128, 128)).T[0:1]


def final_kernel(which, part, w_qkv, gain, *refs):
    out, out_w, gain_ref = refs[-3:]
    step = pl.program_id(0)
    low = low_half((64, 128))
    for zh in range(2):
        rows = slice(zh * 64, zh * 64 + 64)
        for mm in range(4):
            both = []
            for j in range(2):
                m = 2 * mm + j
                out[rows, m * 128 : (m + 1) * 128] = part[0, 0, m, zh, 0:64, 0:128].astype(F32)
                both.append(part[0, 0, m, zh, 0:64, 128:256].astype(F32))
            out[rows, 1024 + mm * 128 : 1152 + mm * 128] = jnp.where(
                low, both[0], pltpu.roll(both[1], HEAD, 1)
            )
            out[rows, 1536 + mm * 128 : 1664 + mm * 128] = jnp.where(
                low, pltpu.roll(both[0], HEAD, 1), both[1]
            )
        for m in range(8):
            out_w[0, m, zh, 0, :, 0:256] = part[0, 0, m, zh, 64:80, :].astype(F32)
            out_w[0, m, zh, 0, :, 256:512] = part[0, 0, m, zh, 80:96, :].astype(F32)

    @pl.when(step == 0)
    def _():
        gain_ref[...] = gain[...] if len(refs) == 3 else refs[0][...]

    at = pl.ds(step // 2 * 4 + which[0] * 2 + step % 2, 1)
    sums = row_sums(out[...] * w_qkv[...].astype(F32))
    gain_ref[at, :] = sums / gain[at, :]


def final(which, part, w_qkv, gain, before=()):
    def rows(i, which):
        return (i // 2 * 4 + which[0] * 2 + i % 2, 0)

    wide = pl.BlockSpec((128, 2048), rows)
    any_space = pl.BlockSpec(memory_space=pl.ANY)
    return call(
        final_kernel,
        (4,),
        [
            pl.BlockSpec((1, 1, 8, 2, 96, 256), lambda i, which: (i // 2, i % 2, 0, 0, 0, 0)),
            wide,
            whole(8, 128),
            *([whole(8, 128), any_space, any_space] if before else []),
        ],
        [
            wide,
            pl.BlockSpec(
                (1, 8, 2, 1, 16, 512), lambda i, which: (i % 2, 0, 0, i // 2, 0, which[0])
            ),
            whole(8, 128),
        ],
        [sds((1024, 2048), F32), sds((2, 8, 2, 2, 16, 1024), F32), sds((8, 128), F32)],
        moved=16 << 20,
        scalars=1,
        aliases={5: 0, 6: 1} if before else None,
        moving=(1,),
    )(which, part.reshape(2, 2, 8, 2, 96, 256), w_qkv, gain, *before)


def exchange(x):
    return lax.all_to_all(x, BLK, 0, 0, tiled=True)


def add_rounded(a, b):
    return (a.astype(F32) + b.astype(F32)).astype(BF16)


def among_experts(x):
    return lax.all_to_all(x, CHIPS, 0, 0, tiled=True, axis_index_groups=EXPERT_GROUPS)


def among_chips(x):
    return lax.all_to_all(x, CHIPS, 0, 0, tiled=True)


def shards(
    tokens, lengths, routes, gates, gain_attn, w_qkv, w_out, gain_moe, w_gate_up, w_down, cotangent
):
    core = lax.axis_index("core")
    blk = lax.axis_index(BLK)
    xh, zh = lax.axis_index("xh"), lax.axis_index("zh")
    tok = tokens.reshape(128, 1024)
    dz = cotangent.reshape(128, 1024)
    wgu = w_gate_up.reshape(1024, 1024)
    wdn = w_down.reshape(512, 1024)
    gain_a = gain_attn.reshape(1, 1024)
    gain_m = gain_moe.reshape(1, 1024)

    cos, sin = map(jnp.asarray, rope_tables())
    zl = lax.axis_index("zl").astype(jnp.int32).reshape(1)
    which = core.astype(jnp.int32).reshape(1)
    info = jnp.stack([lax.dynamic_index_in_dim(lengths, zh, 0, False), xh]).astype(jnp.int32)

    def to_partner(part):
        return lax.ppermute(part, "core", SWAP)

    dz_far = lax.ppermute(dz, ("zl", "zh"), Z_PAIRS)
    pos, gate, chosen = plan(routes.transpose(0, 2, 1), gates.transpose(0, 2, 1))
    chosen_far = lax.ppermute(chosen, ("zl", "zh"), Z_PAIRS)
    h, send = pre(
        blk.astype(jnp.int32).reshape(1), tok, gain_a, w_qkv, cos, sin, [hold(chosen)]
    )
    planned = pack(dz, chosen, dz_far, chosen_far, [hold(send)])
    dz_all = lax.all_gather(planned, PLANE).reshape(16, 2, 144, 1024)
    arrived = exchange(send.reshape(32, 96, 128))
    o_part, ot, lse = attend(info, arrived, [corner(planned)])
    h_both = h.reshape(2, 64, 1024)
    h_mine = lax.dynamic_index_in_dim(h_both, zh, 0, keepdims=False)
    h_far = lax.ppermute(lax.dynamic_index_in_dim(h_both, 1 - zh, 0, keepdims=False), "zh", SWAP)
    h_near = jnp.stack([after(h_mine, hold(o_part)), h_far])
    o_recv = exchange(o_part).reshape(2, 8, 2, 32, 128)
    o, y, rows = mid(o_recv, w_out, tok, gain_m, pos, [corner(h_near[1])])
    o_other = to_partner(o)
    x = among_experts(rows).reshape(1536, 1024)
    place = jnp.stack([blk, zh]).astype(jnp.int32)
    dx2, da, deo, hid = expert(place, x, dz_all, wgu, wdn, [corner(o_other)])
    dx2_back = among_experts(dx2.reshape(32, 48, 1024))
    experts_own, experts_send = expert_grad(which, x, da, hid, deo)
    dy, dbr_own, dbr_send, do = mid_back(
        which, dx2_back, pos, y, gain_m, dz, w_out, [hold(experts_send)]
    )
    experts_own = add_rounded(experts_own, to_partner(experts_send))
    experts_far = lax.ppermute(experts_own, "zl", SWAP)
    h_near = after(h_near, hold(da))
    h_all = lax.all_gather(h_near, PLANE).reshape(16, 2, 64, 1024)


    do_recv = exchange(do.reshape(32, 48, 128))
    eo = expert_out(hid, wdn)
    eo = out_grad(o, o_other, dbr_own, to_partner(dbr_send), eo)
    eo_back = among_experts(after(eo, do_recv))
    mixed = combine(eo_back, pos, gate, y)
    out_part = out_sum(eo_back)
    out_far = lax.ppermute(out_part, "zl", SWAP)
    dqkv, gains = attend_back(info, arrived, do_recv, ot, lse, cos, sin, [])
    place = jnp.stack([xh, zh]).astype(jnp.int32)
    qkv_partial = qkv_grad(place, h_all, dqkv, gains)
    experts_own = add_rounded(after(experts_own, hold(qkv_partial)), experts_far)
    qkv_partial = after(qkv_partial, eo_back, corner(experts_own))
    qkv_pieces = lax.all_to_all(qkv_partial, SAME_COLUMNS, 0, 0, tiled=True)
    experts_other = to_partner(experts_own)
    grad_gate_up, grad_down = final_expert(which, experts_own, experts_other)
    copies, gains = add_pieces(zl, qkv_pieces, out_part, out_far, [])
    own = await_all(among_chips(copies), hold(mixed), hold(grad_gate_up))
    dqkv_recv = exchange(after(dqkv, corner(own))).reshape(2, 8, 2, 96, 128)
    rows = final(which, own, w_qkv, gain_attn.reshape(8, 128))
    grad_qkv, grad_out, grad_gain_attn = final(
        1 - which, to_partner(own), w_qkv, gain_attn.reshape(8, 128), (rows[2], rows[0], rows[1])
    )
    grad_tokens = last(dqkv_recv, w_qkv, tok, gain_a, dy, [hold(grad_qkv)])

    return (
        mixed.reshape(2, 64, 1024),
        grad_tokens.reshape(2, 64, 1024),
        grad_gain_attn.reshape(1024),
        grad_qkv,
        grad_out.reshape(1024, 1024),
        gains.reshape(1024),
        grad_gate_up[None],
        grad_down[None],
    )


def solution(mesh):
    split = Mesh(mesh.devices.reshape(2, 2, 2, 2, 4, 2), AXES)
    rows = P(ROWS, BLK, None)
    return jax.shard_map(
        shards,
        mesh=split,
        in_specs=(
            rows,
            P(ROWS),
            rows,
            rows,
            P(),
            P(),
            P(),
            P(),
            P(BLK, None, None),
            P(BLK, None, None),
            rows,
        ),
        out_specs=(
            rows,
            rows,
            P(),
            P(),
            P(),
            P(),
            P(BLK, None, None),
            P(BLK, None, None),
        ),
        check_vma=False,
    )
```

```python
import jax
import jax.numpy as jnp
import numpy as np
from jax import lax
from jax.experimental import pallas as pl
from jax.experimental.pallas import tpu as pltpu
from jax.sharding import Mesh
from jax.sharding import PartitionSpec as P

HEADS = 16
KV_HEADS = 8
HEAD = 64
FF_EXP = 512
TOP = 8
MOST = 24
EPS = 1e-06
ROPE_BASE = 10000.0
SCALE = HEAD ** (-0.5)

ROWS = ("zl", "core")
PLANE = ("xh", "xl", "y")
BLK = ("xh", "xl", "y", "zh")
CHIPS = ("zl", "xh", "xl", "y", "zh")
AXES = ("zl", "core", "xh", "xl", "y", "zh")
SAME_COLUMNS = ("zl", "core", "xh", "zh")
SWAP = [(0, 1), (1, 0)]
EXPERT_GROUPS = [
    [(parity ^ zh) * 32 + xy * 2 + zh for xy in range(16) for zh in range(2)] for parity in range(2)
]
Z_PAIRS = [(i, 3 - i) for i in range(4)]
F32 = jnp.float32
BF16 = jnp.bfloat16
NT = (((1,), (1,)), ((), ()))
TN = (((0,), (0,)), ((), ()))


def rope_tables():
    lane = np.arange(128) % HEAD
    frequency = (ROPE_BASE ** (-(lane % 32) / 32.0)).astype(np.float32)
    angles = np.arange(2048, dtype=np.float32)[:, None] * frequency[None, :]
    sign = np.where(lane < 32, -1.0, 1.0)
    cosine = np.cos(angles.astype(np.float64)).astype(np.float32)
    return cosine, (np.sin(angles.astype(np.float64)) * sign).astype(np.float32)


def dot(left, right, dims=(((1,), (0,)), ((), ()))):
    return lax.dot_general(left, right, dims, preferred_element_type=F32)


def call(
    kernel,
    grid,
    in_specs,
    out_specs,
    out_shape,
    scratch=(),
    mb=24,
    flops=0,
    moved=0,
    deps=(),
    scalars=0,
    aliases=None,
    moving=(),
):
    count = len(in_specs) + scalars

    def place(i, x):
        small = i < scalars or in_specs[i - scalars].memory_space == pltpu.SMEM
        return x if small or i in moving else hold(x)

    def body(*refs):
        kernel(*refs[:count], *refs[count + len(deps) :])

    built = pl.pallas_call(
        body,
        grid_spec=pltpu.PrefetchScalarGridSpec(
            num_scalar_prefetch=scalars,
            grid=grid,
            in_specs=[*in_specs, *[pl.BlockSpec(memory_space=pl.ANY)] * len(deps)],
            out_specs=out_specs,
            scratch_shapes=list(scratch),
        ),
        out_shape=out_shape,
        input_output_aliases=aliases or {},
        compiler_params=pltpu.CompilerParams(vmem_limit_bytes=mb * 1024 * 1024),
        cost_estimate=pl.CostEstimate(flops=flops, bytes_accessed=moved, transcendentals=0),
    )
    return lambda *operands: built(*[place(i, x) for i, x in enumerate(operands)], *deps)


def after(x, *deps):
    any_space = pl.BlockSpec(memory_space=pl.ANY)
    return pl.pallas_call(
        lambda *refs: None,
        in_specs=[any_space] * (1 + len(deps)),
        out_specs=any_space,
        out_shape=sds(x.shape, x.dtype),
        input_output_aliases={0: 0},
        compiler_params=pltpu.CompilerParams(vmem_limit_bytes=1024 * 1024),
    )(hold(x), *deps)


def await_all(x, *deps):
    any_space = pl.BlockSpec(memory_space=pl.ANY)
    return pl.pallas_call(
        lambda *refs: None,
        in_specs=[any_space] * (1 + len(deps)),
        out_specs=any_space,
        out_shape=jax.ShapeDtypeStruct(x.shape, x.dtype),
        input_output_aliases={0: 0},
        compiler_params=pltpu.CompilerParams(vmem_limit_bytes=1024 * 1024),
    )(x, *deps)


def hold(x):
    return pltpu.with_memory_space_constraint(x, pltpu.HBM)


def corner(x):
    return x[(0,) * (x.ndim - 2)][:8, :128]


def whole(*shape):
    return pl.BlockSpec(shape, lambda *_: (0,) * len(shape))


def sds(shape, dtype):
    return pltpu.HBM(shape, dtype)


def low_half(shape):
    return lax.broadcasted_iota(jnp.int32, shape, len(shape) - 1) < HEAD


def swap_halves(u):
    lane = lax.broadcasted_iota(jnp.int32, u.shape, 1)
    return jnp.where(lane % HEAD < HEAD // 2, pltpu.roll(u, 96, 1), pltpu.roll(u, 32, 1))


def pre_kernel(blk, tok, gain, wq, wk, wv, cos, sin, h_ref, send):
    @pl.when(pl.program_id(0) == 0)
    def _():
        x = tok[...].astype(F32)
        inverse = lax.rsqrt(jnp.mean(x * x, axis=-1, keepdims=True) + EPS)
        h_ref[...] = (x * inverse * gain[...]).astype(BF16)

    h = h_ref[...]
    c = jnp.concatenate([cos[...], cos[...]], 0)
    s = jnp.concatenate([sin[...], sin[...]], 0)

    def rope(u):
        return u * c + swap_halves(u) * s

    q = dot(h, wq[...])
    k = rope(dot(h, wk[...]))
    v = dot(h, wv[...])
    low = low_half(k.shape)
    pairs = (
        jnp.where(low, k, pltpu.roll(v, HEAD, 1)).astype(BF16),
        jnp.where(low, pltpu.roll(k, HEAD, 1), v).astype(BF16),
    )
    for j in range(2):
        qj = (rope(q[:, j * 128 : (j + 1) * 128]).astype(BF16).astype(F32) * SCALE).astype(BF16)
        for t in range(2):
            for half in range(2):
                first = t * 64 + half * 32
                send[half, j, t, 0:32, :] = qj[first : first + 32]
                send[half, j, t, 32:96, :] = pairs[j][t * 64 : t * 64 + 64]


def pre(blk, tok, gain, w_qkv, cos, sin, deps):
    places = pl.BlockSpec((64, 128), lambda m, blk: (blk[0], 0))
    return call(
        pre_kernel,
        (4,),
        [
            whole(128, 1024),
            whole(1, 1024),
            pl.BlockSpec((1024, 256), lambda m, blk: (0, m)),
            pl.BlockSpec((1024, 128), lambda m, blk: (0, 8 + m)),
            pl.BlockSpec((1024, 128), lambda m, blk: (0, 12 + m)),
            places,
            places,
        ],
        [whole(128, 1024), pl.BlockSpec((2, 2, 2, 96, 128), lambda m, blk: (0, m, 0, 0, 0))],
        [sds((128, 1024), BF16), sds((2, 8, 2, 96, 128), BF16)],
        flops=2 * 128 * 1024 * 2048,
        moved=5 << 20,
        scalars=1,
        deps=deps,
    )(blk, tok, gain, w_qkv, w_qkv, w_qkv, cos, sin)


def plan_kernel(routes, gates, pos_ref, gate_ref, out):
    named = jnp.concatenate([routes[0], routes[1]], 1).astype(F32)
    weights = jnp.concatenate([gates[0], gates[1]], 1)
    experts = lax.broadcasted_iota(jnp.int32, (32, 128), 0).astype(F32)
    chosen = jnp.zeros((32, 128), F32)
    gate = jnp.zeros((32, 128), F32)
    for k in range(TOP):
        match = named[k : k + 1] == experts
        chosen = jnp.where(match, 1.0, chosen)
        gate = jnp.where(match, weights[k : k + 1], gate)
    row = lax.broadcasted_iota(jnp.int32, (128, 128), 0)
    before = jnp.where(row < lax.broadcasted_iota(jnp.int32, (128, 128), 1), 1.0, 0.0)
    rank = dot(chosen.astype(BF16), before.astype(BF16))
    pos = jnp.where(chosen > 0.0, rank, -1.0)
    pos_ref[...] = pos.astype(jnp.int32)
    gate_ref[...] = gate
    high = gate.astype(BF16).astype(F32)
    rest = gate - high
    for j in range(8):
        part = slice(4 * j, 4 * j + 4)
        tile = jnp.concatenate([pos[part], high[part], rest[part], jnp.zeros((4, 128), F32)], 0)
        out[:, j * 128 : (j + 1) * 128] = tile.astype(BF16)


def plan(routes, gates):
    return call(
        plan_kernel,
        (1,),
        [whole(2, 8, 64), whole(2, 8, 64)],
        [whole(32, 128), whole(32, 128), whole(16, 1024)],
        [sds((32, 128), jnp.int32), sds((32, 128), F32), sds((16, 1024), BF16)],
        moved=1 << 17,
    )(routes, gates)


def pack_kernel(dz, info, dz_far, info_far, out):
    out[0, 0:128, :] = dz[...]
    out[0, 128:144, :] = info[...]
    out[1, 0:128, :] = dz_far[...]
    out[1, 128:144, :] = info_far[...]


def pack(dz, info, dz_far, info_far, deps):
    return call(
        pack_kernel,
        (1,),
        [whole(128, 1024), whole(16, 1024), whole(128, 1024), whole(16, 1024)],
        whole(2, 144, 1024),
        sds((2, 144, 1024), BF16),
        moved=1 << 20,
        moving=(2, 3),
        deps=deps,
    )(dz, info, dz_far, info_far)


def split_queries(q):
    qf = q.astype(F32)
    low = low_half(qf.shape)
    first = jnp.where(low, qf, 0.0)
    second = jnp.where(low, pltpu.roll(qf, HEAD, 1), 0.0)
    return jnp.concatenate([first, second], 0).astype(BF16)


def limits(tile, info):
    place = lax.broadcasted_iota(jnp.int32, (1, 512), 1) % 256
    position = (tile * 8 + place // 32) * 64 + info[1] * 32 + place % 32
    return jnp.minimum(position, info[0] - 1)


def load_pairs(x_ref, kv, kvt):
    kv[...] = x_ref[:, 32:96, :].reshape(2048, 128)
    for c in range(8):
        rows = slice(c * 256, (c + 1) * 256)
        kvt[:, rows] = kv[rows, :].astype(F32).T.astype(BF16)


def attend_kernel(info, x_ref, o_ref, ot_ref, lse_ref, kv, kvt):
    load_pairs(x_ref, kv, kvt)
    for tile in range(4):
        q2 = split_queries(x_ref[tile * 8 : (tile + 1) * 8, 0:32, :].reshape(256, 128))
        limit = limits(tile, info)
        keys = (tile + 1) * 512
        s = dot(kv[0:keys, :], q2, NT)
        place = lax.broadcasted_iota(jnp.int32, (keys, 1), 0)
        s = jnp.where(place <= limit, s, -1e30)
        top = jnp.max(s, axis=0, keepdims=True)
        p = jnp.exp(s - top)
        total = jnp.sum(p, axis=0, keepdims=True)
        out = dot(kvt[64:128, 0:keys], p.astype(BF16)) / total
        ot_ref[tile] = out
        lse_ref[tile] = jnp.broadcast_to(top + jnp.log(total), (8, 512))
        both = jnp.concatenate([out[:, :256], out[:, 256:]], 0).T
        o_ref[tile * 8 : (tile + 1) * 8] = both.astype(BF16).reshape(8, 32, 128)


def attend(info, arrived, deps):
    return call(
        attend_kernel,
        (1,),
        [pl.BlockSpec(memory_space=pltpu.SMEM), whole(32, 96, 128)],
        [whole(32, 32, 128), whole(4, 64, 512), whole(4, 8, 512)],
        [sds((32, 32, 128), BF16), sds((4, 64, 512), F32), sds((4, 8, 512), F32)],
        [pltpu.VMEM((2048, 128), BF16), pltpu.VMEM((128, 2048), BF16)],
        flops=4 * 2048 * 1280 * 128,
        moved=2 << 20,
        deps=deps,
        moving=(1,),
    )(info, arrived)


def attend_back_kernel(
    info, x_ref, do_ref, ot_ref, lse_ref, cos, sin, out_ref, gain_ref, kv, kvt, total
):
    load_pairs(x_ref, kv, kvt)
    total[...] = jnp.zeros_like(total)
    for tile in range(4):
        q2 = split_queries(x_ref[tile * 8 : (tile + 1) * 8, 0:32, :].reshape(256, 128))
        grad = do_ref[tile * 8 : (tile + 1) * 8, 0:32, :].reshape(256, 128).astype(F32)
        low = low_half(grad.shape)
        do2 = jnp.concatenate(
            [jnp.where(low, 0.0, pltpu.roll(grad, HEAD, 1)), jnp.where(low, 0.0, grad)], 0
        ).astype(BF16)
        grad_t = grad.T
        grad_t = jnp.concatenate([grad_t[:64], grad_t[64:]], 1)
        inner = jnp.sum(grad_t * ot_ref[tile], axis=0, keepdims=True)
        lse = lse_ref[tile][0:1]
        limit = limits(tile, info)

        def step(c, acc):
            at = pl.ds(pl.multiple_of(c * 256, 256), 256)
            part = kv[at, :]
            s = dot(part, q2, NT)
            place = c * 256 + lax.broadcasted_iota(jnp.int32, (256, 1), 0)
            p = jnp.exp(jnp.where(place <= limit, s, -1e30) - lse)
            ds = (p * (dot(part, do2, NT) - inner)).astype(BF16)
            total[at, :] += dot(ds, q2) + dot(p.astype(BF16), do2)
            return acc + dot(kvt[0:64, at], ds)

        acc = lax.fori_loop(0, 2 * tile + 2, step, jnp.zeros((64, 512), F32))
        dq = jnp.concatenate([acc[:, :256], acc[:, 256:]], 0).T
        at = (slice(tile * 8, tile * 8 + 8), pl.ds(pl.multiple_of(info[1] * 32, 32), 32))
        c, s = cos[at].reshape(256, 128), sin[at].reshape(256, 128)
        dq = ((dq * c - swap_halves(dq) * s) * SCALE).astype(BF16)
        out_ref[tile * 8 : (tile + 1) * 8, 0:32, :] = dq.reshape(8, 32, 128)
    for tile in range(4):
        blocks = slice(tile * 8, tile * 8 + 8)
        part = total[tile * 512 : (tile + 1) * 512, :]
        turned = part * cos[blocks].reshape(512, 128) - swap_halves(part) * sin[
            blocks
        ].reshape(512, 128)
        part = jnp.where(low_half(part.shape), turned, part)
        out_ref[blocks, 32:96, :] = part.astype(BF16).reshape(8, 64, 128)
    gains = jnp.sum(do_ref[:, 32:48, :].astype(F32), axis=0)
    gain_ref[...] = gains[:8] + gains[8:]


def attend_back(info, arrived, grad, ot, lse, cos, sin, deps):
    return call(
        attend_back_kernel,
        (1,),
        [
            pl.BlockSpec(memory_space=pltpu.SMEM),
            whole(32, 96, 128),
            whole(32, 48, 128),
            whole(4, 64, 512),
            whole(4, 8, 512),
            whole(32, 64, 128),
            whole(32, 64, 128),
        ],
        [whole(32, 96, 128), whole(8, 128)],
        [sds((32, 96, 128), BF16), sds((8, 128), F32)],
        [pltpu.VMEM((2048, 128), BF16), pltpu.VMEM((128, 2048), BF16), pltpu.VMEM((2048, 128), F32)],
        flops=10 * 2048 * 1280 * 128,
        moved=3 << 20,
        deps=deps,
        moving=(1, 2,),
    )(info, arrived, grad, ot, lse, cos.reshape(32, 64, 128), sin.reshape(32, 64, 128))


def placement(pos):
    shape = (pos.shape[0], 48, 128)
    slots = lax.broadcasted_iota(jnp.int32, shape, 1)
    return (pos[...][:, None, :] == slots).reshape(shape[0] * 48, 128)


def gated(pos, gate):
    placed = placement(pos)
    weight = jnp.broadcast_to(gate[...][:, None, :], (pos.shape[0], 48, 128))
    weight = jnp.where(placed, weight.reshape(placed.shape), 0.0)
    high = weight.astype(BF16)
    return high, (weight - high.astype(F32)).astype(BF16)


PLACE = pl.BlockSpec((16, 128), lambda e: (e, 0))
SLOTS = pl.BlockSpec((16, 48, 1024), lambda e: (e, 0, 0))


def mid_kernel(recv, w0, w1, w2, w3, tok, gain, pos, o_ref, y_ref, out, h2):
    @pl.when(pl.program_id(0) == 0)
    def _():
        for s in range(2):
            for half in range(2):
                first = s * 64 + half * 32
                for m in range(8):
                    o_ref[first : first + 32, m * 128 : (m + 1) * 128] = recv[half, m, s]
        o = o_ref[...]
        branch = jnp.concatenate([dot(o, w[...]) for w in (w0, w1, w2, w3)], 1)
        y = tok[...].astype(F32) + branch
        y_ref[...] = y
        inverse = lax.rsqrt(jnp.mean(y * y, axis=-1, keepdims=True) + EPS)
        h2[...] = (y * inverse * gain[...]).astype(BF16)

    placed = placement(pos).astype(F32).astype(BF16)
    out[...] = dot(placed, h2[...]).astype(BF16).reshape(out.shape)


def mid(recv, w_out, tok, gain, pos, deps):
    return call(
        mid_kernel,
        (2,),
        [
            whole(2, 8, 2, 32, 128),
            *[pl.BlockSpec((1024, 256), lambda e, j=j: (0, j)) for j in range(4)],
            whole(128, 1024),
            whole(1, 1024),
            PLACE,
        ],
        [whole(128, 1024), whole(128, 1024), SLOTS],
        [sds((128, 1024), BF16), sds((128, 1024), F32), sds((32, 48, 1024), BF16)],
        [pltpu.VMEM((128, 1024), BF16)],
        flops=2 * 128 * 1024 * 1024 + 2 * 1536 * 128 * 1024,
        moved=6 << 20,
        moving=(0,),
        deps=deps,
    )(recv, w_out, w_out, w_out, w_out, tok, gain, pos)


def expert_kernel(which, x_ref, info, dz, g0, g1, u0, u1, d0, d1, dx2, da_ref, deo_ref, hid_ref):
    slots = lax.broadcasted_iota(jnp.int32, (48, 128), 0).astype(F32)
    rows16 = lax.broadcasted_iota(jnp.int32, (16, 128), 0)
    blank = jnp.zeros((48, 128), F32)
    mine = which[0] % 4
    for pair in range(PLACES):
        parts, weights = [], []
        for j in range(2):
            tile = info[pair, j].astype(F32)

            def pick(k):
                return jnp.sum(jnp.where(rows16 == mine + 4 * k, tile, 0.0), axis=0, keepdims=True)

            hot = jnp.where(slots == pick(0), 1.0, 0.0)
            weights.append(jnp.sum(hot * (pick(1) + pick(2)), axis=1, keepdims=True))
            parts.append(jnp.concatenate([hot, blank] if j == 0 else [blank, hot], 1))
        rows = dot(jnp.concatenate(parts, 0).astype(BF16), dz[pair].reshape(256, 1024))
        rows = (rows * jnp.concatenate(weights, 0)).astype(BF16)
        for j in range(2):
            first = pl.multiple_of(pair * 96 + (which[1] ^ j) * 48, 48)
            deo_ref[pl.ds(first, 48), :] = rows[j * 48 : (j + 1) * 48]
    x, deo = x_ref[...], deo_ref[...]
    for part, (wg, wu) in enumerate(((g0, u0), (g1, u1))):
        at = slice(part * 256, part * 256 + 256)
        late = slice(part * 256 + FF_EXP, part * 256 + FF_EXP + 256)
        gate, up = dot(x, wg[...]), dot(x, wu[...])
        dhid = dot(deo[:, :512], d0[at, :], NT) + dot(deo[:, 512:], d1[at, :], NT)
        sig = jax.nn.sigmoid(gate)
        act = gate * sig
        hid_ref[:, at] = (act * up).astype(BF16)
        da_ref[:, at] = (dhid * up * sig * (1.0 + gate * (1.0 - sig))).astype(BF16)
        da_ref[:, late] = (dhid * act).astype(BF16)
    total = dot(da_ref[:, 0:256], g0[...], NT) + dot(da_ref[:, 256:512], g1[...], NT)
    total += dot(da_ref[:, 512:768], u0[...], NT) + dot(da_ref[:, 768:1024], u1[...], NT)
    dx2[...] = total.astype(BF16)


PLACES = 4


def expert(which, x, dz_all, wgu, wdn, deps):
    count = PLACES * 96
    rows = pl.BlockSpec((count, 1024), lambda i, which: (i, 0))
    return call(
        expert_kernel,
        (16 // PLACES,),
        [
            rows,
            pl.BlockSpec((PLACES, 2, 16, 128), lambda i, which: (i, 0, 8, which[0] // 4)),
            pl.BlockSpec((PLACES, 2, 128, 1024), lambda i, which: (i, 0, 0, 0)),
            *[pl.BlockSpec((1024, 256), lambda i, which, j=j: (0, j)) for j in range(4)],
            *[pl.BlockSpec((512, 512), lambda i, which, j=j: (0, j)) for j in range(2)],
        ],
        [rows, rows, rows, pl.BlockSpec((count, 512), lambda i, which: (i, 0))],
        [*[sds((1536, 1024), BF16)] * 3, sds((1536, 512), BF16)],
        mb=32,
        flops=2 * 1536 * 1024 * 2816,
        moved=26 << 20,
        scalars=1,
        moving=(1,),
        deps=deps,
    )(which, x, dz_all, dz_all, wgu, wgu, wgu, wgu, wdn, wdn)


def expert_out_kernel(which, info, hid, d0, d1, out):
    slots = lax.broadcasted_iota(jnp.int32, (48, 128), 0).astype(F32)
    rows16 = lax.broadcasted_iota(jnp.int32, (16, 128), 0)
    mine = which[0] % 4
    eo = jnp.concatenate([dot(hid[...], d0[...]), dot(hid[...], d1[...])], 1).astype(BF16)
    for place in range(4):
        for zh in range(2):
            tile = info[place, which[1] ^ zh].astype(F32)

            def pick(k):
                return jnp.sum(jnp.where(rows16 == mine + 4 * k, tile, 0.0), axis=0, keepdims=True)

            hot = jnp.where(slots == pick(0), 1.0, 0.0)
            gate = jnp.concatenate([hot * pick(1), hot * pick(2)], 0).astype(BF16)
            first = place * 96 + zh * 48
            rows = eo[first : first + 48]
            product = dot(gate, jnp.concatenate([rows, rows], 0), TN)
            out[place, which[1] ^ zh] = product.astype(BF16)


def expert_out(which, dz_all, hid, wdn):
    return call(
        expert_out_kernel,
        (4,),
        [
            pl.BlockSpec((4, 2, 16, 128), lambda i, which: (i, 0, 8, which[0] // 4)),
            pl.BlockSpec((384, 512), lambda i, which: (i, 0)),
            *[pl.BlockSpec((512, 512), lambda i, which, j=j: (0, j)) for j in range(2)],
        ],
        pl.BlockSpec((4, 2, 128, 1024), lambda i, which: (i, 0, 0, 0)),
        sds((16, 2, 128, 1024), BF16),
        flops=2 * 1536 * 1024 * 512 + 4 * 1536 * 128 * 1024,
        moved=12 << 20,
        scalars=1,
    )(which, dz_all, hid, wdn, wdn)


def expert_grad_kernel(core, x_ref, da, hid, deo, own, other):
    step = pl.program_id(0)

    for first, out in ((0, own), (3, other)):

        @pl.when((step >= first) & (step < first + 2))
        def _():
            out[...] = dot(x_ref[...], da[...], TN).astype(BF16)

        @pl.when(step == first + 2)
        def _():
            out[...] = dot(hid[...], deo[...], TN).astype(BF16)


def expert_grad(core, x, da, hid, deo):
    def half(i, core):
        return jnp.where(i < 3, core[0], 1 - core[0])

    return call(
        expert_grad_kernel,
        (6,),
        [
            pl.BlockSpec((1536, 256), lambda i, c: (0, half(i, c) * 2 + jnp.minimum(i % 3, 1))),
            whole(1536, 1024),
            pl.BlockSpec((1536, 256), lambda i, c: (0, half(i, c))),
            whole(1536, 1024),
        ],
        [
            pl.BlockSpec((256, 1024), lambda i, c: (jnp.minimum(i, 2), 0)),
            pl.BlockSpec((256, 1024), lambda i, c: (jnp.maximum(i - 3, 0), 0)),
        ],
        [sds((768, 1024), BF16)] * 2,
        flops=2 * 1536 * 1024 * 1536,
        moved=16 << 20,
        scalars=1,
        moving=(1,),
    )(core, x, da, hid, deo)


def final_expert_kernel(core, own, other, gate_up, down):
    step = pl.program_id(0)
    half = jnp.where(step < 4, step // 2, step - 4)

    def write(out):
        @pl.when(half == core[0])
        def _():
            out[...] = own[...].astype(F32)

        @pl.when(half != core[0])
        def _():
            out[...] = other[...].astype(F32)

    @pl.when(step < 4)
    def _():
        write(gate_up)

    @pl.when(step >= 4)
    def _():
        write(down)


def final_expert(core, own, other):
    part = pl.BlockSpec((256, 1024), lambda i: (jnp.where(i < 4, i % 2, 2), 0))
    return call(
        final_expert_kernel,
        (6,),
        [pl.BlockSpec(memory_space=pltpu.SMEM), part, part],
        [
            pl.BlockSpec((256, 1024), lambda i: (jnp.minimum(i, 3), 0)),
            pl.BlockSpec((256, 1024), lambda i: (jnp.maximum(i - 4, 0), 0)),
        ],
        [sds((1024, 1024), F32), sds((512, 1024), F32)],
        moved=9 << 20,
        moving=(1, 2,),
    )(core, own, other)


def norm_back(incoming, gain, vectors):
    inverse = lax.rsqrt(jnp.mean(vectors * vectors, axis=-1, keepdims=True) + EPS)
    scaled = vectors * inverse
    weighted = incoming * gain
    mean = jnp.mean(weighted * scaled, axis=-1, keepdims=True)
    return inverse * (weighted - scaled * mean), scaled


def mid_back_kernel(
    core, back, pos, y, gain, dz, w0, w1, w2, w3, dy_ref, own, other, send
):
    placed = placement(pos).astype(F32).astype(BF16)
    dh2 = dot(placed, back[...].reshape(1536, 1024), TN)
    dv, scaled = norm_back(dh2, gain[...], y[...])
    gains = jnp.sum(dh2 * scaled, axis=0, keepdims=True)
    row = lax.broadcasted_iota(jnp.int32, (8, 128), 0)
    tile = jnp.zeros((8, 128), F32)
    for r in range(8):
        tile = jnp.where(row == r, gains[:, r * 128 : (r + 1) * 128], tile)
    high = tile.astype(BF16).astype(F32)
    extra = jnp.concatenate([high, tile - high], 0).astype(BF16)
    dy = dz[...].astype(F32) + dv
    dy_ref[...] = dy
    dbr = dy.astype(BF16)

    @pl.when(core[0] == 0)
    def _():
        own[...] = dbr[:, :512]
        other[...] = dbr[:, 512:]

    @pl.when(core[0] == 1)
    def _():
        own[...] = dbr[:, 512:]
        other[...] = dbr[:, :512]

    do = jnp.concatenate([dot(dbr, w[...], NT) for w in (w0, w1, w2, w3)], 1).astype(BF16)
    for s in range(2):
        for half in range(2):
            first = s * 64 + half * 32
            for m in range(8):
                send[half, m, s, 0:32, :] = do[first : first + 32, m * 128 : (m + 1) * 128]
                send[half, m, s, 32:48, :] = extra


def mid_back(core, back, pos, y, gain, dz, w_out, deps):
    return call(
        mid_back_kernel,
        (1,),
        [
            pl.BlockSpec(memory_space=pltpu.SMEM),
            whole(32, 48, 1024),
            whole(32, 128),
            whole(128, 1024),
            whole(1, 1024),
            whole(128, 1024),
            *[pl.BlockSpec((256, 1024), lambda e, j=j: (j, 0)) for j in range(4)],
        ],
        [whole(128, 1024), whole(128, 512), whole(128, 512), whole(2, 8, 2, 48, 128)],
        [
            sds((128, 1024), F32),
            sds((128, 512), BF16),
            sds((128, 512), BF16),
            sds((2, 8, 2, 48, 128), BF16),
        ],
        flops=2 * 128 * 1024 * 1024 + 2 * 1536 * 128 * 1024,
        moved=6 << 20,
        deps=deps,
        moving=(1,),
    )(core, back, pos, y, gain, dz, w_out, w_out, w_out, w_out)


def last_kernel(
    recv, w0, w1, w2, w3, tok, gain, dy, y, near, far, grad_tokens, mixed, dproj
):
    mixed[...] = (y[...] + near[0].astype(F32) + far[...].astype(F32)).astype(BF16)
    low = low_half((64, 128))
    for t in range(2):
        rows = slice(t * 64, t * 64 + 64)
        for mm in range(4):
            both = []
            for j in range(2):
                m = 2 * mm + j
                dq = jnp.concatenate([recv[0, m, t, 0:32, :], recv[1, m, t, 0:32, :]], 0)
                dproj[rows, m * 128 : (m + 1) * 128] = dq
                both.append(
                    recv[0, m, t, 32:96, :].astype(F32) + recv[1, m, t, 32:96, :].astype(F32)
                )
            dk = jnp.where(low, both[0], pltpu.roll(both[1], HEAD, 1))
            dv = jnp.where(low, pltpu.roll(both[0], HEAD, 1), both[1])
            dproj[rows, 1024 + mm * 128 : 1152 + mm * 128] = dk.astype(BF16)
            dproj[rows, 1536 + mm * 128 : 1664 + mm * 128] = dv.astype(BF16)
    d = dproj[...]
    dh = jnp.concatenate([dot(d, w[...], NT) for w in (w0, w1, w2, w3)], 1)
    dv, _ = norm_back(dh, gain[...], tok[...].astype(F32))
    grad_tokens[...] = dy[...] + dv


def last(recv, w_qkv, tok, gain, dy, y, sums, far, deps):
    return call(
        last_kernel,
        (1,),
        [
            whole(2, 8, 2, 96, 128),
            *[pl.BlockSpec((256, 2048), lambda _, j=j: (j, 0)) for j in range(4)],
            whole(128, 1024),
            whole(1, 1024),
            whole(128, 1024),
            whole(128, 1024),
            pl.BlockSpec((1, 128, 1024), lambda _: (0, 0, 0)),
            whole(128, 1024),
        ],
        [whole(128, 1024), whole(128, 1024)],
        [sds((128, 1024), F32), sds((128, 1024), BF16)],
        [pltpu.VMEM((128, 2048), BF16)],
        flops=2 * 128 * 1024 * 2048,
        moved=6 << 20,
        deps=deps,
        moving=(0, 9, 10),
    )(recv, w_qkv, w_qkv, w_qkv, w_qkv, tok, gain, dy, y, sums, far)


def qkv_grad_kernel(place, h_all, d_ref, gains, out, rows, acc):
    step = pl.program_id(0)
    for pair in range(4):
        for zh in range(2):
            first = (pair * 2 + zh) * 64
            rows[first : first + 64, :] = h_all[pair, place[1] ^ zh]
    dq = d_ref[:, 0:32, :]
    none = jnp.zeros_like(dq)
    dq = jnp.where(place[0] == 0, jnp.concatenate([dq, none], 1), jnp.concatenate([none, dq], 1))
    both = jnp.concatenate([dq.reshape(512, 128), d_ref[:, 32:96, :].reshape(512, 128)], 1)
    product = dot(rows[...], both, TN)

    @pl.when(step == 0)
    def _():
        acc[...] = product

    @pl.when((step > 0) & (step < 3))
    def _():
        acc[...] += product

    @pl.when(step == 3)
    def _():
        out[:, 0:64, :] = (acc[...] + product).astype(BF16).reshape(16, 64, 256)
        high = gains[...].astype(BF16).astype(F32)
        tile = jnp.concatenate([high, gains[...] - high], 1)
        tile = jnp.concatenate([tile, jnp.zeros_like(tile)], 0).astype(BF16)
        out[:, 64:80, :] = jnp.broadcast_to(tile[None], (16, 16, 256))


def qkv_grad(place, h_all, dqkv, gains):
    return call(
        qkv_grad_kernel,
        (4,),
        [
            pl.BlockSpec((4, 2, 64, 1024), lambda i, place: (i, 0, 0, 0)),
            pl.BlockSpec((8, 96, 128), lambda i, place: (i, 0, 0)),
            whole(8, 128),
        ],
        whole(16, 80, 256),
        sds((16, 80, 256), BF16),
        [pltpu.VMEM((512, 1024), BF16), pltpu.VMEM((1024, 256), F32)],
        flops=2 * 2048 * 1024 * 256,
        moved=6 << 20,
        scalars=1,
    )(place, h_all, dqkv, gains)


def out_grad_kernel(left, left2, right, right2, out):
    a = jnp.concatenate([left[...], left2[...]], 0)
    b = jnp.concatenate([right[...], right2[...]], 0)
    out[...] = dot(a, b, TN).astype(BF16)


def out_grad(left, left2, right, right2):
    thin = pl.BlockSpec((128, 256), lambda i: (0, i))
    return call(
        out_grad_kernel,
        (4,),
        [thin, thin, whole(128, 512), whole(128, 512)],
        pl.BlockSpec((256, 512), lambda i: (i, 0)),
        sds((1024, 512), BF16),
        flops=2 * 256 * 1024 * 512,
        moved=3 << 20,
        moving=(1, 3),
    )(left, left2, right, right2)


def add_pieces_kernel(qkv, out_w, out, gains):
    total = jnp.sum(qkv[:, 0:64, :].astype(F32), axis=0).astype(BF16)
    out[:, 0:64, :] = jnp.broadcast_to(total[None], (32, 64, 256))
    other = jnp.sum(out_w[...].astype(F32), axis=0).astype(BF16)
    out[:, 64:80, :] = jnp.broadcast_to(other[None, :, :256], (32, 16, 256))
    out[:, 80:96, :] = jnp.broadcast_to(other[None, :, 256:], (32, 16, 256))
    parts = [qkv[row, 64:80, :].astype(F32)[:8] for row in (0, 4, 8, 12)]
    parts = [part[:, :128] + part[:, 128:] for part in parts]
    gains[...] = parts[0] + parts[1] + parts[2] + parts[3]


def add_pieces(qkv, out_w, deps):
    return call(
        add_pieces_kernel,
        (2,),
        [whole(16, 80, 256), whole(64, 16, 512)],
        [pl.BlockSpec((32, 96, 256), lambda i: (i, 0, 0)), whole(8, 128)],
        [sds((64, 96, 256), BF16), sds((8, 128), F32)],
        moved=5 << 20,
        moving=(0, 1),
        deps=deps,
    )(qkv, out_w)


def row_sums(product):
    total = jnp.sum(product, axis=-1, keepdims=True)
    return jnp.broadcast_to(total, (128, 128)).T[0:1]


def final_kernel(which, part, w_qkv, gain, *refs):
    out, out_w, gain_ref = refs[-3:]
    step = pl.program_id(0)
    low = low_half((64, 128))
    for zh in range(2):
        rows = slice(zh * 64, zh * 64 + 64)
        for mm in range(4):
            both = []
            for j in range(2):
                m = 2 * mm + j
                out[rows, m * 128 : (m + 1) * 128] = part[0, 0, m, zh, 0:64, 0:128].astype(F32)
                both.append(part[0, 0, m, zh, 0:64, 128:256].astype(F32))
            out[rows, 1024 + mm * 128 : 1152 + mm * 128] = jnp.where(
                low, both[0], pltpu.roll(both[1], HEAD, 1)
            )
            out[rows, 1536 + mm * 128 : 1664 + mm * 128] = jnp.where(
                low, pltpu.roll(both[0], HEAD, 1), both[1]
            )
        for m in range(8):
            out_w[0, m, zh, :, 0:256] = part[0, 0, m, zh, 64:80, :].astype(F32)
            out_w[0, m, zh, :, 256:512] = part[0, 0, m, zh, 80:96, :].astype(F32)

    @pl.when(step == 0)
    def _():
        gain_ref[...] = gain[...] if len(refs) == 3 else refs[0][...]

    at = pl.ds(step // 2 * 4 + which[0] * 2 + step % 2, 1)
    sums = row_sums(out[...] * w_qkv[...].astype(F32))
    gain_ref[at, :] = sums / gain[at, :]


def final(which, part, w_qkv, gain, before=()):
    def rows(i, which):
        return (i // 2 * 4 + which[0] * 2 + i % 2, 0)

    wide = pl.BlockSpec((128, 2048), rows)
    any_space = pl.BlockSpec(memory_space=pl.ANY)
    return call(
        final_kernel,
        (4,),
        [
            pl.BlockSpec((1, 1, 8, 2, 96, 256), lambda i, which: (i // 2, i % 2, 0, 0, 0, 0)),
            wide,
            whole(8, 128),
            *([whole(8, 128), any_space, any_space] if before else []),
        ],
        [
            wide,
            pl.BlockSpec((1, 8, 2, 16, 512), lambda i, which: (i, 0, 0, 0, which[0])),
            whole(8, 128),
        ],
        [sds((1024, 2048), F32), sds((4, 8, 2, 16, 1024), F32), sds((8, 128), F32)],
        moved=16 << 20,
        scalars=1,
        aliases={5: 0, 6: 1} if before else None,
        moving=(1,),
    )(which, part.reshape(2, 2, 8, 2, 96, 256), w_qkv, gain, *before)


def exchange(x):
    return lax.all_to_all(x, BLK, 0, 0, tiled=True)


def add_rounded(a, b):
    return (a.astype(F32) + b.astype(F32)).astype(BF16)


def among_experts(x):
    return lax.all_to_all(x, CHIPS, 0, 0, tiled=True, axis_index_groups=EXPERT_GROUPS)


def among_chips(x):
    return lax.all_to_all(x, CHIPS, 0, 0, tiled=True)


def shards(
    tokens, lengths, routes, gates, gain_attn, w_qkv, w_out, gain_moe, w_gate_up, w_down, cotangent
):
    core = lax.axis_index("core")
    blk = lax.axis_index(BLK)
    xh, zh = lax.axis_index("xh"), lax.axis_index("zh")
    tok = tokens.reshape(128, 1024)
    dz = cotangent.reshape(128, 1024)
    wgu = w_gate_up.reshape(1024, 1024)
    wdn = w_down.reshape(512, 1024)
    gain_a = gain_attn.reshape(1, 1024)
    gain_m = gain_moe.reshape(1, 1024)

    cos, sin = map(jnp.asarray, rope_tables())
    zl = lax.axis_index("zl").astype(jnp.int32).reshape(1)
    which = core.astype(jnp.int32).reshape(1)
    info = jnp.stack([lax.dynamic_index_in_dim(lengths, zh, 0, False), xh]).astype(jnp.int32)

    def to_partner(part):
        return lax.ppermute(part, "core", SWAP)

    dz_far = lax.ppermute(dz, ("zl", "zh"), Z_PAIRS)
    pos, gate, chosen = plan(routes.transpose(0, 2, 1), gates.transpose(0, 2, 1))
    chosen_far = lax.ppermute(chosen, ("zl", "zh"), Z_PAIRS)
    h, send = pre(
        blk.astype(jnp.int32).reshape(1), tok, gain_a, w_qkv, cos, sin, [hold(chosen)]
    )
    planned = pack(dz, chosen, dz_far, chosen_far, [hold(send)])
    dz_all = lax.all_gather(planned, PLANE).reshape(16, 2, 144, 1024)
    arrived = exchange(send.reshape(32, 96, 128))
    o_part, ot, lse = attend(info, arrived, [corner(planned)])
    h_both = h.reshape(2, 64, 1024)
    h_mine = lax.dynamic_index_in_dim(h_both, zh, 0, keepdims=False)
    h_far = lax.ppermute(lax.dynamic_index_in_dim(h_both, 1 - zh, 0, keepdims=False), "zh", SWAP)
    h_near = jnp.stack([after(h_mine, hold(o_part)), h_far])
    o_recv = exchange(o_part).reshape(2, 8, 2, 32, 128)
    o, y, rows = mid(o_recv, w_out, tok, gain_m, pos, [corner(h_near[1])])
    o_other = to_partner(o)
    x = among_experts(rows).reshape(1536, 1024)

    place = jnp.stack([blk, zh]).astype(jnp.int32)
    dx2, da, deo, hid = expert(place, x, dz_all, wgu, wdn, [corner(o_other)])
    h_near = after(h_near, hold(da))
    h_all = lax.all_gather(h_near, PLANE).reshape(16, 2, 64, 1024)

    dx2_back = among_experts(dx2.reshape(32, 48, 1024))
    outputs = expert_out(place, dz_all, hid, wdn)
    experts_own, experts_send = expert_grad(which, x, da, hid, deo)
    experts_own = add_rounded(experts_own, to_partner(experts_send))
    dy, dbr_own, dbr_send, do = mid_back(
        which, dx2_back, pos, y, gain_m, dz, w_out, [corner(experts_own), hold(outputs)]
    )

    sums = after(outputs.reshape(4096, 1024), hold(dbr_own))
    sums = lax.psum_scatter(sums, PLANE, tiled=True).reshape(2, 128, 1024)
    far = lax.ppermute(sums[1], ("zl", "zh"), Z_PAIRS)


    do_recv = exchange(do.reshape(32, 48, 128))
    out_partial = out_grad(o, o_other, dbr_own, to_partner(dbr_send))
    out_sent = after(out_partial.reshape(64, 16, 512), do_recv)
    experts_own = after(experts_own, hold(out_sent))
    experts_far = lax.ppermute(experts_own, "zl", SWAP)
    out_pieces = among_chips(out_sent)
    dqkv, gains = attend_back(info, arrived, do_recv, ot, lse, cos, sin, [hold(out_sent)])

    place = jnp.stack([xh, zh]).astype(jnp.int32)
    qkv_partial = qkv_grad(place, h_all, dqkv, gains)
    experts_own = add_rounded(after(experts_own, hold(qkv_partial)), experts_far)
    qkv_pieces = lax.all_to_all(
        after(qkv_partial, out_pieces), SAME_COLUMNS, 0, 0, tiled=True
    )
    experts_other = to_partner(experts_own)
    grad_gate_up, grad_down = final_expert(which, experts_own, experts_other)
    copies, gains = add_pieces(qkv_pieces, out_pieces, [corner(experts_own)])
    own = await_all(among_chips(copies), hold(grad_gate_up))
    dqkv_recv = exchange(after(dqkv, corner(own))).reshape(2, 8, 2, 96, 128)
    rows = final(which, own, w_qkv, gain_attn.reshape(8, 128))
    grad_qkv, grad_out, grad_gain_attn = final(
        1 - which, to_partner(own), w_qkv, gain_attn.reshape(8, 128), (rows[2], rows[0], rows[1])
    )
    grad_tokens, mixed = last(
        dqkv_recv, w_qkv, tok, gain_a, dy, y, sums, far, [hold(grad_qkv)]
    )
    return (
        mixed.reshape(2, 64, 1024),
        grad_tokens.reshape(2, 64, 1024),
        grad_gain_attn.reshape(1024),
        grad_qkv,
        grad_out.reshape(1024, 1024),
        gains.reshape(1024),
        grad_gate_up[None],
        grad_down[None],
    )


def solution(mesh):
    split = Mesh(mesh.devices.reshape(2, 2, 2, 2, 4, 2), AXES)
    rows = P(ROWS, BLK, None)
    return jax.shard_map(
        shards,
        mesh=split,
        in_specs=(
            rows,
            P(ROWS),
            rows,
            rows,
            P(),
            P(),
            P(),
            P(),
            P(BLK, None, None),
            P(BLK, None, None),
            rows,
        ),
        out_specs=(
            rows,
            rows,
            P(),
            P(),
            P(),
            P(),
            P(BLK, None, None),
            P(BLK, None, None),
        ),
        check_vma=False,
    )
```

```python
import jax
import jax.numpy as jnp
import numpy as np
from jax import lax
from jax.experimental import pallas as pl
from jax.experimental.pallas import tpu as pltpu
from jax.sharding import Mesh
from jax.sharding import PartitionSpec as P

HEADS = 16
KV_HEADS = 8
HEAD = 64
FF_EXP = 512
TOP = 8
MOST = 24
EPS = 1e-06
ROPE_BASE = 10000.0
SCALE = HEAD ** (-0.5)

ROWS = ("zl", "core")
PLANE = ("xh", "xl", "y")
BLK = ("xh", "xl", "y", "zh")
CHIPS = ("zl", "xh", "xl", "y", "zh")
AXES = ("zl", "core", "xh", "xl", "y", "zh")
SAME_COLUMNS = ("zl", "core", "xh", "zh")
SWAP = [(0, 1), (1, 0)]
EXPERT_GROUPS = [
    [(parity ^ zh) * 32 + xy * 2 + zh for xy in range(16) for zh in range(2)] for parity in range(2)
]
Z_PAIRS = [(i, 3 - i) for i in range(4)]
F32 = jnp.float32
BF16 = jnp.bfloat16
NT = (((1,), (1,)), ((), ()))
TN = (((0,), (0,)), ((), ()))


def rope_tables():
    lane = np.arange(128) % HEAD
    frequency = (ROPE_BASE ** (-(lane % 32) / 32.0)).astype(np.float32)
    angles = np.arange(2048, dtype=np.float32)[:, None] * frequency[None, :]
    sign = np.where(lane < 32, -1.0, 1.0)
    cosine = np.cos(angles.astype(np.float64)).astype(np.float32)
    return cosine, (np.sin(angles.astype(np.float64)) * sign).astype(np.float32)


def dot(left, right, dims=(((1,), (0,)), ((), ()))):
    return lax.dot_general(left, right, dims, preferred_element_type=F32)


def call(
    kernel,
    grid,
    in_specs,
    out_specs,
    out_shape,
    scratch=(),
    mb=24,
    flops=0,
    moved=0,
    deps=(),
    scalars=0,
    aliases=None,
    moving=(),
):
    count = len(in_specs) + scalars

    def place(i, x):
        small = i < scalars or in_specs[i - scalars].memory_space == pltpu.SMEM
        return x if small or i in moving else hold(x)

    def body(*refs):
        kernel(*refs[:count], *refs[count + len(deps) :])

    built = pl.pallas_call(
        body,
        grid_spec=pltpu.PrefetchScalarGridSpec(
            num_scalar_prefetch=scalars,
            grid=grid,
            in_specs=[*in_specs, *[pl.BlockSpec(memory_space=pl.ANY)] * len(deps)],
            out_specs=out_specs,
            scratch_shapes=list(scratch),
        ),
        out_shape=out_shape,
        input_output_aliases=aliases or {},
        compiler_params=pltpu.CompilerParams(vmem_limit_bytes=mb * 1024 * 1024),
        cost_estimate=pl.CostEstimate(flops=flops, bytes_accessed=moved, transcendentals=0),
    )
    return lambda *operands: built(*[place(i, x) for i, x in enumerate(operands)], *deps)


def after(x, *deps):
    any_space = pl.BlockSpec(memory_space=pl.ANY)
    return pl.pallas_call(
        lambda *refs: None,
        in_specs=[any_space] * (1 + len(deps)),
        out_specs=any_space,
        out_shape=sds(x.shape, x.dtype),
        input_output_aliases={0: 0},
        compiler_params=pltpu.CompilerParams(vmem_limit_bytes=1024 * 1024),
    )(hold(x), *deps)


def await_all(x, *deps):
    any_space = pl.BlockSpec(memory_space=pl.ANY)
    return pl.pallas_call(
        lambda *refs: None,
        in_specs=[any_space] * (1 + len(deps)),
        out_specs=any_space,
        out_shape=jax.ShapeDtypeStruct(x.shape, x.dtype),
        input_output_aliases={0: 0},
        compiler_params=pltpu.CompilerParams(vmem_limit_bytes=1024 * 1024),
    )(x, *deps)


def hold(x):
    return pltpu.with_memory_space_constraint(x, pltpu.HBM)


def corner(x):
    return x[(0,) * (x.ndim - 2)][:8, :128]


def whole(*shape):
    return pl.BlockSpec(shape, lambda *_: (0,) * len(shape))


def sds(shape, dtype):
    return pltpu.HBM(shape, dtype)


def low_half(shape):
    return lax.broadcasted_iota(jnp.int32, shape, len(shape) - 1) < HEAD


def swap_halves(u):
    lane = lax.broadcasted_iota(jnp.int32, u.shape, 1)
    return jnp.where(lane % HEAD < HEAD // 2, pltpu.roll(u, 96, 1), pltpu.roll(u, 32, 1))


def pre_kernel(blk, tok, gain, wq, wk, wv, cos, sin, h_ref, send):
    @pl.when(pl.program_id(0) == 0)
    def _():
        x = tok[...].astype(F32)
        inverse = lax.rsqrt(jnp.mean(x * x, axis=-1, keepdims=True) + EPS)
        h_ref[...] = (x * inverse * gain[...]).astype(BF16)

    h = h_ref[...]
    c = jnp.concatenate([cos[...], cos[...]], 0)
    s = jnp.concatenate([sin[...], sin[...]], 0)

    def rope(u):
        return u * c + swap_halves(u) * s

    q = dot(h, wq[...])
    k = rope(dot(h, wk[...]))
    v = dot(h, wv[...])
    low = low_half(k.shape)
    pairs = (
        jnp.where(low, k, pltpu.roll(v, HEAD, 1)).astype(BF16),
        jnp.where(low, pltpu.roll(k, HEAD, 1), v).astype(BF16),
    )
    for j in range(2):
        qj = (rope(q[:, j * 128 : (j + 1) * 128]).astype(BF16).astype(F32) * SCALE).astype(BF16)
        for t in range(2):
            for half in range(2):
                first = t * 64 + half * 32
                send[half, j, t, 0:32, :] = qj[first : first + 32]
                send[half, j, t, 32:96, :] = pairs[j][t * 64 : t * 64 + 64]


def pre(blk, tok, gain, w_qkv, cos, sin, deps):
    places = pl.BlockSpec((64, 128), lambda m, blk: (blk[0], 0))
    return call(
        pre_kernel,
        (4,),
        [
            whole(128, 1024),
            whole(1, 1024),
            pl.BlockSpec((1024, 256), lambda m, blk: (0, m)),
            pl.BlockSpec((1024, 128), lambda m, blk: (0, 8 + m)),
            pl.BlockSpec((1024, 128), lambda m, blk: (0, 12 + m)),
            places,
            places,
        ],
        [whole(128, 1024), pl.BlockSpec((2, 2, 2, 96, 128), lambda m, blk: (0, m, 0, 0, 0))],
        [sds((128, 1024), BF16), sds((2, 8, 2, 96, 128), BF16)],
        flops=2 * 128 * 1024 * 2048,
        moved=5 << 20,
        scalars=1,
        deps=deps,
    )(blk, tok, gain, w_qkv, w_qkv, w_qkv, cos, sin)


def plan_kernel(routes, gates, pos_ref, gate_ref, out):
    named = jnp.concatenate([routes[0], routes[1]], 1).astype(F32)
    weights = jnp.concatenate([gates[0], gates[1]], 1)
    experts = lax.broadcasted_iota(jnp.int32, (32, 128), 0).astype(F32)
    chosen = jnp.zeros((32, 128), F32)
    gate = jnp.zeros((32, 128), F32)
    for k in range(TOP):
        match = named[k : k + 1] == experts
        chosen = jnp.where(match, 1.0, chosen)
        gate = jnp.where(match, weights[k : k + 1], gate)
    row = lax.broadcasted_iota(jnp.int32, (128, 128), 0)
    before = jnp.where(row < lax.broadcasted_iota(jnp.int32, (128, 128), 1), 1.0, 0.0)
    rank = dot(chosen.astype(BF16), before.astype(BF16))
    pos = jnp.where(chosen > 0.0, rank, -1.0)
    pos_ref[...] = pos.astype(jnp.int32)
    gate_ref[...] = gate
    high = gate.astype(BF16).astype(F32)
    rest = gate - high
    for j in range(8):
        part = slice(4 * j, 4 * j + 4)
        tile = jnp.concatenate([pos[part], high[part], rest[part], jnp.zeros((4, 128), F32)], 0)
        out[:, j * 128 : (j + 1) * 128] = tile.astype(BF16)


def plan(routes, gates):
    return call(
        plan_kernel,
        (1,),
        [whole(2, 8, 64), whole(2, 8, 64)],
        [whole(32, 128), whole(32, 128), whole(16, 1024)],
        [sds((32, 128), jnp.int32), sds((32, 128), F32), sds((16, 1024), BF16)],
        moved=1 << 17,
    )(routes, gates)


def pack_kernel(dz, info, dz_far, info_far, out):
    out[0, 0:128, :] = dz[...]
    out[0, 128:144, :] = info[...]
    out[1, 0:128, :] = dz_far[...]
    out[1, 128:144, :] = info_far[...]


def pack(dz, info, dz_far, info_far, deps):
    return call(
        pack_kernel,
        (1,),
        [whole(128, 1024), whole(16, 1024), whole(128, 1024), whole(16, 1024)],
        whole(2, 144, 1024),
        sds((2, 144, 1024), BF16),
        moved=1 << 20,
        moving=(2, 3),
        deps=deps,
    )(dz, info, dz_far, info_far)


def split_queries(q):
    qf = q.astype(F32)
    low = low_half(qf.shape)
    first = jnp.where(low, qf, 0.0)
    second = jnp.where(low, pltpu.roll(qf, HEAD, 1), 0.0)
    return jnp.concatenate([first, second], 0).astype(BF16)


def limits(tile, info):
    place = lax.broadcasted_iota(jnp.int32, (1, 512), 1) % 256
    position = (tile * 8 + place // 32) * 64 + info[1] * 32 + place % 32
    return jnp.minimum(position, info[0] - 1)


def load_pairs(x_ref, kv, kvt):
    kv[...] = x_ref[:, 32:96, :].reshape(2048, 128)
    for c in range(8):
        rows = slice(c * 256, (c + 1) * 256)
        kvt[:, rows] = kv[rows, :].astype(F32).T.astype(BF16)


def attend_kernel(info, x_ref, o_ref, ot_ref, lse_ref, kv, kvt):
    load_pairs(x_ref, kv, kvt)
    for tile in range(4):
        q2 = split_queries(x_ref[tile * 8 : (tile + 1) * 8, 0:32, :].reshape(256, 128))
        limit = limits(tile, info)
        keys = (tile + 1) * 512
        s = dot(kv[0:keys, :], q2, NT)
        place = lax.broadcasted_iota(jnp.int32, (keys, 1), 0)
        s = jnp.where(place <= limit, s, -1e30)
        top = jnp.max(s, axis=0, keepdims=True)
        p = jnp.exp(s - top)
        total = jnp.sum(p, axis=0, keepdims=True)
        out = dot(kvt[64:128, 0:keys], p.astype(BF16)) / total
        ot_ref[tile] = out
        lse_ref[tile] = jnp.broadcast_to(top + jnp.log(total), (8, 512))
        both = jnp.concatenate([out[:, :256], out[:, 256:]], 0).T
        o_ref[tile * 8 : (tile + 1) * 8] = both.astype(BF16).reshape(8, 32, 128)


def attend(info, arrived, deps):
    return call(
        attend_kernel,
        (1,),
        [pl.BlockSpec(memory_space=pltpu.SMEM), whole(32, 96, 128)],
        [whole(32, 32, 128), whole(4, 64, 512), whole(4, 8, 512)],
        [sds((32, 32, 128), BF16), sds((4, 64, 512), F32), sds((4, 8, 512), F32)],
        [pltpu.VMEM((2048, 128), BF16), pltpu.VMEM((128, 2048), BF16)],
        flops=4 * 2048 * 1280 * 128,
        moved=2 << 20,
        deps=deps,
        moving=(1,),
    )(info, arrived)


def attend_back_kernel(
    info, x_ref, do_ref, ot_ref, lse_ref, cos, sin, out_ref, gain_ref, kv, kvt, total
):
    load_pairs(x_ref, kv, kvt)
    total[...] = jnp.zeros_like(total)
    for tile in range(4):
        q2 = split_queries(x_ref[tile * 8 : (tile + 1) * 8, 0:32, :].reshape(256, 128))
        grad = do_ref[tile * 8 : (tile + 1) * 8, 0:32, :].reshape(256, 128).astype(F32)
        low = low_half(grad.shape)
        do2 = jnp.concatenate(
            [jnp.where(low, 0.0, pltpu.roll(grad, HEAD, 1)), jnp.where(low, 0.0, grad)], 0
        ).astype(BF16)
        grad_t = grad.T
        grad_t = jnp.concatenate([grad_t[:64], grad_t[64:]], 1)
        inner = jnp.sum(grad_t * ot_ref[tile], axis=0, keepdims=True)
        lse = lse_ref[tile][0:1]
        limit = limits(tile, info)

        def step(c, acc):
            at = pl.ds(pl.multiple_of(c * 256, 256), 256)
            part = kv[at, :]
            s = dot(part, q2, NT)
            place = c * 256 + lax.broadcasted_iota(jnp.int32, (256, 1), 0)
            p = jnp.exp(jnp.where(place <= limit, s, -1e30) - lse)
            ds = (p * (dot(part, do2, NT) - inner)).astype(BF16)
            total[at, :] += dot(ds, q2) + dot(p.astype(BF16), do2)
            return acc + dot(kvt[0:64, at], ds)

        acc = lax.fori_loop(0, 2 * tile + 2, step, jnp.zeros((64, 512), F32))
        dq = jnp.concatenate([acc[:, :256], acc[:, 256:]], 0).T
        at = (slice(tile * 8, tile * 8 + 8), pl.ds(pl.multiple_of(info[1] * 32, 32), 32))
        c, s = cos[at].reshape(256, 128), sin[at].reshape(256, 128)
        dq = ((dq * c - swap_halves(dq) * s) * SCALE).astype(BF16)
        out_ref[tile * 8 : (tile + 1) * 8, 0:32, :] = dq.reshape(8, 32, 128)
    for tile in range(4):
        blocks = slice(tile * 8, tile * 8 + 8)
        part = total[tile * 512 : (tile + 1) * 512, :]
        turned = part * cos[blocks].reshape(512, 128) - swap_halves(part) * sin[
            blocks
        ].reshape(512, 128)
        part = jnp.where(low_half(part.shape), turned, part)
        out_ref[blocks, 32:96, :] = part.astype(BF16).reshape(8, 64, 128)
    gains = jnp.sum(do_ref[:, 32:48, :].astype(F32), axis=0)
    gain_ref[...] = gains[:8] + gains[8:]


def attend_back(info, arrived, grad, ot, lse, cos, sin, deps):
    return call(
        attend_back_kernel,
        (1,),
        [
            pl.BlockSpec(memory_space=pltpu.SMEM),
            whole(32, 96, 128),
            whole(32, 48, 128),
            whole(4, 64, 512),
            whole(4, 8, 512),
            whole(32, 64, 128),
            whole(32, 64, 128),
        ],
        [whole(32, 96, 128), whole(8, 128)],
        [sds((32, 96, 128), BF16), sds((8, 128), F32)],
        [pltpu.VMEM((2048, 128), BF16), pltpu.VMEM((128, 2048), BF16), pltpu.VMEM((2048, 128), F32)],
        flops=10 * 2048 * 1280 * 128,
        moved=3 << 20,
        deps=deps,
        moving=(1, 2,),
    )(info, arrived, grad, ot, lse, cos.reshape(32, 64, 128), sin.reshape(32, 64, 128))


def placement(pos):
    shape = (pos.shape[0], 48, 128)
    slots = lax.broadcasted_iota(jnp.int32, shape, 1)
    return (pos[...][:, None, :] == slots).reshape(shape[0] * 48, 128)


def gated(pos, gate):
    placed = placement(pos)
    weight = jnp.broadcast_to(gate[...][:, None, :], (pos.shape[0], 48, 128))
    weight = jnp.where(placed, weight.reshape(placed.shape), 0.0)
    high = weight.astype(BF16)
    return high, (weight - high.astype(F32)).astype(BF16)


PLACE = pl.BlockSpec((16, 128), lambda e: (e, 0))
SLOTS = pl.BlockSpec((16, 48, 1024), lambda e: (e, 0, 0))


def mid_kernel(recv, w0, w1, w2, w3, tok, gain, pos, o_ref, y_ref, out, h2):
    @pl.when(pl.program_id(0) == 0)
    def _():
        for s in range(2):
            for half in range(2):
                first = s * 64 + half * 32
                for m in range(8):
                    o_ref[first : first + 32, m * 128 : (m + 1) * 128] = recv[half, m, s]
        o = o_ref[...]
        branch = jnp.concatenate([dot(o, w[...]) for w in (w0, w1, w2, w3)], 1)
        y = tok[...].astype(F32) + branch
        y_ref[...] = y
        inverse = lax.rsqrt(jnp.mean(y * y, axis=-1, keepdims=True) + EPS)
        h2[...] = (y * inverse * gain[...]).astype(BF16)

    placed = placement(pos).astype(F32).astype(BF16)
    out[...] = dot(placed, h2[...]).astype(BF16).reshape(out.shape)


def mid(recv, w_out, tok, gain, pos, deps):
    return call(
        mid_kernel,
        (2,),
        [
            whole(2, 8, 2, 32, 128),
            *[pl.BlockSpec((1024, 256), lambda e, j=j: (0, j)) for j in range(4)],
            whole(128, 1024),
            whole(1, 1024),
            PLACE,
        ],
        [whole(128, 1024), whole(128, 1024), SLOTS],
        [sds((128, 1024), BF16), sds((128, 1024), F32), sds((32, 48, 1024), BF16)],
        [pltpu.VMEM((128, 1024), BF16)],
        flops=2 * 128 * 1024 * 1024 + 2 * 1536 * 128 * 1024,
        moved=6 << 20,
        moving=(0,),
        deps=deps,
    )(recv, w_out, w_out, w_out, w_out, tok, gain, pos)


def expert_kernel(which, x_ref, info, dz, g0, g1, u0, u1, d0, d1, dx2, da_ref, deo_ref, hid_ref):
    slots = lax.broadcasted_iota(jnp.int32, (48, 128), 0).astype(F32)
    rows16 = lax.broadcasted_iota(jnp.int32, (16, 128), 0)
    blank = jnp.zeros((48, 128), F32)
    mine = which[0] % 4
    for pair in range(PLACES):
        parts, weights = [], []
        for j in range(2):
            tile = info[pair, j].astype(F32)

            def pick(k):
                return jnp.sum(jnp.where(rows16 == mine + 4 * k, tile, 0.0), axis=0, keepdims=True)

            hot = jnp.where(slots == pick(0), 1.0, 0.0)
            weights.append(jnp.sum(hot * (pick(1) + pick(2)), axis=1, keepdims=True))
            parts.append(jnp.concatenate([hot, blank] if j == 0 else [blank, hot], 1))
        rows = dot(jnp.concatenate(parts, 0).astype(BF16), dz[pair].reshape(256, 1024))
        rows = (rows * jnp.concatenate(weights, 0)).astype(BF16)
        for j in range(2):
            first = pl.multiple_of(pair * 96 + (which[1] ^ j) * 48, 48)
            deo_ref[pl.ds(first, 48), :] = rows[j * 48 : (j + 1) * 48]
    x, deo = x_ref[...], deo_ref[...]
    for part, (wg, wu) in enumerate(((g0, u0), (g1, u1))):
        at = slice(part * 256, part * 256 + 256)
        late = slice(part * 256 + FF_EXP, part * 256 + FF_EXP + 256)
        gate, up = dot(x, wg[...]), dot(x, wu[...])
        dhid = dot(deo[:, :512], d0[at, :], NT) + dot(deo[:, 512:], d1[at, :], NT)
        sig = jax.nn.sigmoid(gate)
        act = gate * sig
        hid_ref[:, at] = (act * up).astype(BF16)
        da_ref[:, at] = (dhid * up * sig * (1.0 + gate * (1.0 - sig))).astype(BF16)
        da_ref[:, late] = (dhid * act).astype(BF16)
    total = dot(da_ref[:, 0:256], g0[...], NT) + dot(da_ref[:, 256:512], g1[...], NT)
    total += dot(da_ref[:, 512:768], u0[...], NT) + dot(da_ref[:, 768:1024], u1[...], NT)
    dx2[...] = total.astype(BF16)


PLACES = 4


def expert(which, x, dz_all, wgu, wdn, deps):
    count = PLACES * 96
    rows = pl.BlockSpec((count, 1024), lambda i, which: (i, 0))
    return call(
        expert_kernel,
        (16 // PLACES,),
        [
            rows,
            pl.BlockSpec((PLACES, 2, 16, 128), lambda i, which: (i, 0, 8, which[0] // 4)),
            pl.BlockSpec((PLACES, 2, 128, 1024), lambda i, which: (i, 0, 0, 0)),
            *[pl.BlockSpec((1024, 256), lambda i, which, j=j: (0, j)) for j in range(4)],
            *[pl.BlockSpec((512, 512), lambda i, which, j=j: (0, j)) for j in range(2)],
        ],
        [rows, rows, rows, pl.BlockSpec((count, 512), lambda i, which: (i, 0))],
        [*[sds((1536, 1024), BF16)] * 3, sds((1536, 512), BF16)],
        mb=32,
        flops=2 * 1536 * 1024 * 2816,
        moved=26 << 20,
        scalars=1,
        moving=(1,),
        deps=deps,
    )(which, x, dz_all, dz_all, wgu, wgu, wgu, wgu, wdn, wdn)


def expert_out_kernel(which, info, hid, d0, d1, out):
    slots = lax.broadcasted_iota(jnp.int32, (48, 128), 0).astype(F32)
    rows16 = lax.broadcasted_iota(jnp.int32, (16, 128), 0)
    mine = which[0] % 4
    eo = jnp.concatenate([dot(hid[...], d0[...]), dot(hid[...], d1[...])], 1).astype(BF16)
    for place in range(4):
        for zh in range(2):
            tile = info[place, which[1] ^ zh].astype(F32)

            def pick(k):
                return jnp.sum(jnp.where(rows16 == mine + 4 * k, tile, 0.0), axis=0, keepdims=True)

            hot = jnp.where(slots == pick(0), 1.0, 0.0)
            gate = jnp.concatenate([hot * pick(1), hot * pick(2)], 0).astype(BF16)
            first = place * 96 + zh * 48
            rows = eo[first : first + 48]
            product = dot(gate, jnp.concatenate([rows, rows], 0), TN)
            out[place, which[1] ^ zh] = product.astype(BF16)


def expert_out(which, dz_all, hid, wdn):
    return call(
        expert_out_kernel,
        (4,),
        [
            pl.BlockSpec((4, 2, 16, 128), lambda i, which: (i, 0, 8, which[0] // 4)),
            pl.BlockSpec((384, 512), lambda i, which: (i, 0)),
            *[pl.BlockSpec((512, 512), lambda i, which, j=j: (0, j)) for j in range(2)],
        ],
        pl.BlockSpec((4, 2, 128, 1024), lambda i, which: (i, 0, 0, 0)),
        sds((16, 2, 128, 1024), BF16),
        flops=2 * 1536 * 1024 * 512 + 4 * 1536 * 128 * 1024,
        moved=12 << 20,
        scalars=1,
    )(which, dz_all, hid, wdn, wdn)


def expert_grad_kernel(core, x_ref, da, hid, deo, own, other):
    step = pl.program_id(0)

    for first, out in ((0, own), (3, other)):

        @pl.when((step >= first) & (step < first + 2))
        def _():
            out[...] = dot(x_ref[...], da[...], TN).astype(BF16)

        @pl.when(step == first + 2)
        def _():
            out[...] = dot(hid[...], deo[...], TN).astype(BF16)


def expert_grad(core, x, da, hid, deo):
    def half(i, core):
        return jnp.where(i < 3, core[0], 1 - core[0])

    return call(
        expert_grad_kernel,
        (6,),
        [
            pl.BlockSpec((1536, 256), lambda i, c: (0, half(i, c) * 2 + jnp.minimum(i % 3, 1))),
            whole(1536, 1024),
            pl.BlockSpec((1536, 256), lambda i, c: (0, half(i, c))),
            whole(1536, 1024),
        ],
        [
            pl.BlockSpec((256, 1024), lambda i, c: (jnp.minimum(i, 2), 0)),
            pl.BlockSpec((256, 1024), lambda i, c: (jnp.maximum(i - 3, 0), 0)),
        ],
        [sds((768, 1024), BF16)] * 2,
        flops=2 * 1536 * 1024 * 1536,
        moved=16 << 20,
        scalars=1,
        moving=(1,),
    )(core, x, da, hid, deo)


def final_expert_kernel(core, own, other, gate_up, down):
    step = pl.program_id(0)
    half = jnp.where(step < 4, step // 2, step - 4)

    def write(out):
        @pl.when(half == core[0])
        def _():
            out[...] = own[...].astype(F32)

        @pl.when(half != core[0])
        def _():
            out[...] = other[...].astype(F32)

    @pl.when(step < 4)
    def _():
        write(gate_up)

    @pl.when(step >= 4)
    def _():
        write(down)


def final_expert(core, own, other):
    part = pl.BlockSpec((256, 1024), lambda i: (jnp.where(i < 4, i % 2, 2), 0))
    return call(
        final_expert_kernel,
        (6,),
        [pl.BlockSpec(memory_space=pltpu.SMEM), part, part],
        [
            pl.BlockSpec((256, 1024), lambda i: (jnp.minimum(i, 3), 0)),
            pl.BlockSpec((256, 1024), lambda i: (jnp.maximum(i - 4, 0), 0)),
        ],
        [sds((1024, 1024), F32), sds((512, 1024), F32)],
        moved=9 << 20,
        moving=(1, 2,),
    )(core, own, other)


def norm_back(incoming, gain, vectors):
    inverse = lax.rsqrt(jnp.mean(vectors * vectors, axis=-1, keepdims=True) + EPS)
    scaled = vectors * inverse
    weighted = incoming * gain
    mean = jnp.mean(weighted * scaled, axis=-1, keepdims=True)
    return inverse * (weighted - scaled * mean), scaled


def mid_back_kernel(
    core, back, pos, y, gain, dz, w0, w1, w2, w3, dy_ref, own, other, send
):
    placed = placement(pos).astype(F32).astype(BF16)
    dh2 = dot(placed, back[...].reshape(1536, 1024), TN)
    dv, scaled = norm_back(dh2, gain[...], y[...])
    gains = jnp.sum(dh2 * scaled, axis=0, keepdims=True)
    row = lax.broadcasted_iota(jnp.int32, (8, 128), 0)
    tile = jnp.zeros((8, 128), F32)
    for r in range(8):
        tile = jnp.where(row == r, gains[:, r * 128 : (r + 1) * 128], tile)
    high = tile.astype(BF16).astype(F32)
    extra = jnp.concatenate([high, tile - high], 0).astype(BF16)
    dy = dz[...].astype(F32) + dv
    dy_ref[...] = dy
    dbr = dy.astype(BF16)

    @pl.when(core[0] == 0)
    def _():
        own[...] = dbr[:, :512]
        other[...] = dbr[:, 512:]

    @pl.when(core[0] == 1)
    def _():
        own[...] = dbr[:, 512:]
        other[...] = dbr[:, :512]

    do = jnp.concatenate([dot(dbr, w[...], NT) for w in (w0, w1, w2, w3)], 1).astype(BF16)
    for s in range(2):
        for half in range(2):
            first = s * 64 + half * 32
            for m in range(8):
                send[half, m, s, 0:32, :] = do[first : first + 32, m * 128 : (m + 1) * 128]
                send[half, m, s, 32:48, :] = extra


def mid_back(core, back, pos, y, gain, dz, w_out, deps):
    return call(
        mid_back_kernel,
        (1,),
        [
            pl.BlockSpec(memory_space=pltpu.SMEM),
            whole(32, 48, 1024),
            whole(32, 128),
            whole(128, 1024),
            whole(1, 1024),
            whole(128, 1024),
            *[pl.BlockSpec((256, 1024), lambda e, j=j: (j, 0)) for j in range(4)],
        ],
        [whole(128, 1024), whole(128, 512), whole(128, 512), whole(2, 8, 2, 48, 128)],
        [
            sds((128, 1024), F32),
            sds((128, 512), BF16),
            sds((128, 512), BF16),
            sds((2, 8, 2, 48, 128), BF16),
        ],
        flops=2 * 128 * 1024 * 1024 + 2 * 1536 * 128 * 1024,
        moved=6 << 20,
        deps=deps,
        moving=(1,),
    )(core, back, pos, y, gain, dz, w_out, w_out, w_out, w_out)


def last_kernel(
    recv, w0, w1, w2, w3, tok, gain, dy, y, near, far, grad_tokens, mixed, dproj
):
    mixed[...] = (y[...] + near[0].astype(F32) + far[...].astype(F32)).astype(BF16)
    low = low_half((64, 128))
    for t in range(2):
        rows = slice(t * 64, t * 64 + 64)
        for mm in range(4):
            both = []
            for j in range(2):
                m = 2 * mm + j
                dq = jnp.concatenate([recv[0, m, t, 0:32, :], recv[1, m, t, 0:32, :]], 0)
                dproj[rows, m * 128 : (m + 1) * 128] = dq
                both.append(
                    recv[0, m, t, 32:96, :].astype(F32) + recv[1, m, t, 32:96, :].astype(F32)
                )
            dk = jnp.where(low, both[0], pltpu.roll(both[1], HEAD, 1))
            dv = jnp.where(low, pltpu.roll(both[0], HEAD, 1), both[1])
            dproj[rows, 1024 + mm * 128 : 1152 + mm * 128] = dk.astype(BF16)
            dproj[rows, 1536 + mm * 128 : 1664 + mm * 128] = dv.astype(BF16)
    d = dproj[...]
    dh = jnp.concatenate([dot(d, w[...], NT) for w in (w0, w1, w2, w3)], 1)
    dv, _ = norm_back(dh, gain[...], tok[...].astype(F32))
    grad_tokens[...] = dy[...] + dv


def last(recv, w_qkv, tok, gain, dy, y, sums, far, deps):
    return call(
        last_kernel,
        (1,),
        [
            whole(2, 8, 2, 96, 128),
            *[pl.BlockSpec((256, 2048), lambda _, j=j: (j, 0)) for j in range(4)],
            whole(128, 1024),
            whole(1, 1024),
            whole(128, 1024),
            whole(128, 1024),
            pl.BlockSpec((1, 128, 1024), lambda _: (0, 0, 0)),
            whole(128, 1024),
        ],
        [whole(128, 1024), whole(128, 1024)],
        [sds((128, 1024), F32), sds((128, 1024), BF16)],
        [pltpu.VMEM((128, 2048), BF16)],
        flops=2 * 128 * 1024 * 2048,
        moved=6 << 20,
        deps=deps,
        moving=(0, 9, 10),
    )(recv, w_qkv, w_qkv, w_qkv, w_qkv, tok, gain, dy, y, sums, far)


def qkv_grad_kernel(place, h_all, d_ref, gains, out, rows, acc):
    step = pl.program_id(0)
    for pair in range(4):
        for zh in range(2):
            first = (pair * 2 + zh) * 64
            rows[first : first + 64, :] = h_all[pair, place[1] ^ zh]
    dq = d_ref[:, 0:32, :]
    none = jnp.zeros_like(dq)
    dq = jnp.where(place[0] == 0, jnp.concatenate([dq, none], 1), jnp.concatenate([none, dq], 1))
    both = jnp.concatenate([dq.reshape(512, 128), d_ref[:, 32:96, :].reshape(512, 128)], 1)
    product = dot(rows[...], both, TN)

    @pl.when(step == 0)
    def _():
        acc[...] = product

    @pl.when((step > 0) & (step < 3))
    def _():
        acc[...] += product

    @pl.when(step == 3)
    def _():
        out[:, 0:64, :] = (acc[...] + product).astype(BF16).reshape(16, 64, 256)
        high = gains[...].astype(BF16).astype(F32)
        tile = jnp.concatenate([high, gains[...] - high], 1)
        tile = jnp.concatenate([tile, jnp.zeros_like(tile)], 0).astype(BF16)
        out[:, 64:80, :] = jnp.broadcast_to(tile[None], (16, 16, 256))


def qkv_grad(place, h_all, dqkv, gains):
    return call(
        qkv_grad_kernel,
        (4,),
        [
            pl.BlockSpec((4, 2, 64, 1024), lambda i, place: (i, 0, 0, 0)),
            pl.BlockSpec((8, 96, 128), lambda i, place: (i, 0, 0)),
            whole(8, 128),
        ],
        whole(16, 80, 256),
        sds((16, 80, 256), BF16),
        [pltpu.VMEM((512, 1024), BF16), pltpu.VMEM((1024, 256), F32)],
        flops=2 * 2048 * 1024 * 256,
        moved=6 << 20,
        scalars=1,
    )(place, h_all, dqkv, gains)


def out_grad_kernel(left, left2, right, right2, out):
    a = jnp.concatenate([left[...], left2[...]], 0)
    b = jnp.concatenate([right[...], right2[...]], 0)
    out[...] = dot(a, b, TN).astype(BF16)


def out_grad(left, left2, right, right2):
    thin = pl.BlockSpec((128, 256), lambda i: (0, i))
    return call(
        out_grad_kernel,
        (4,),
        [thin, thin, whole(128, 512), whole(128, 512)],
        pl.BlockSpec((256, 512), lambda i: (i, 0)),
        sds((1024, 512), BF16),
        flops=2 * 256 * 1024 * 512,
        moved=3 << 20,
        moving=(1, 3),
    )(left, left2, right, right2)


def add_pieces_kernel(qkv, out_w, out, gains):
    total = jnp.sum(qkv[:, 0:64, :].astype(F32), axis=0).astype(BF16)
    out[:, 0:64, :] = jnp.broadcast_to(total[None], (32, 64, 256))
    other = jnp.sum(out_w[...].astype(F32), axis=0).astype(BF16)
    out[:, 64:80, :] = jnp.broadcast_to(other[None, :, :256], (32, 16, 256))
    out[:, 80:96, :] = jnp.broadcast_to(other[None, :, 256:], (32, 16, 256))
    parts = [qkv[row, 64:80, :].astype(F32)[:8] for row in (0, 4, 8, 12)]
    parts = [part[:, :128] + part[:, 128:] for part in parts]
    gains[...] = parts[0] + parts[1] + parts[2] + parts[3]


def add_pieces(qkv, out_w, deps):
    return call(
        add_pieces_kernel,
        (2,),
        [whole(16, 80, 256), whole(64, 16, 512)],
        [pl.BlockSpec((32, 96, 256), lambda i: (i, 0, 0)), whole(8, 128)],
        [sds((64, 96, 256), BF16), sds((8, 128), F32)],
        moved=5 << 20,
        moving=(0, 1),
        deps=deps,
    )(qkv, out_w)


def row_sums(product):
    total = jnp.sum(product, axis=-1, keepdims=True)
    return jnp.broadcast_to(total, (128, 128)).T[0:1]


def final_kernel(which, part, w_qkv, gain, *refs):
    out, out_w, gain_ref = refs[-3:]
    step = pl.program_id(0)
    low = low_half((64, 128))
    for zh in range(2):
        rows = slice(zh * 64, zh * 64 + 64)
        for mm in range(4):
            both = []
            for j in range(2):
                m = 2 * mm + j
                out[rows, m * 128 : (m + 1) * 128] = part[0, 0, m, zh, 0:64, 0:128].astype(F32)
                both.append(part[0, 0, m, zh, 0:64, 128:256].astype(F32))
            out[rows, 1024 + mm * 128 : 1152 + mm * 128] = jnp.where(
                low, both[0], pltpu.roll(both[1], HEAD, 1)
            )
            out[rows, 1536 + mm * 128 : 1664 + mm * 128] = jnp.where(
                low, pltpu.roll(both[0], HEAD, 1), both[1]
            )
        for m in range(8):
            out_w[0, m, zh, :, 0:256] = part[0, 0, m, zh, 64:80, :].astype(F32)
            out_w[0, m, zh, :, 256:512] = part[0, 0, m, zh, 80:96, :].astype(F32)

    @pl.when(step == 0)
    def _():
        gain_ref[...] = gain[...] if len(refs) == 3 else refs[0][...]

    at = pl.ds(step // 2 * 4 + which[0] * 2 + step % 2, 1)
    sums = row_sums(out[...] * w_qkv[...].astype(F32))
    gain_ref[at, :] = sums / gain[at, :]


def final(which, part, w_qkv, gain, before=()):
    def rows(i, which):
        return (i // 2 * 4 + which[0] * 2 + i % 2, 0)

    wide = pl.BlockSpec((128, 2048), rows)
    any_space = pl.BlockSpec(memory_space=pl.ANY)
    return call(
        final_kernel,
        (4,),
        [
            pl.BlockSpec((1, 1, 8, 2, 96, 256), lambda i, which: (i // 2, i % 2, 0, 0, 0, 0)),
            wide,
            whole(8, 128),
            *([whole(8, 128), any_space, any_space] if before else []),
        ],
        [
            wide,
            pl.BlockSpec((1, 8, 2, 16, 512), lambda i, which: (i, 0, 0, 0, which[0])),
            whole(8, 128),
        ],
        [sds((1024, 2048), F32), sds((4, 8, 2, 16, 1024), F32), sds((8, 128), F32)],
        moved=16 << 20,
        scalars=1,
        aliases={5: 0, 6: 1} if before else None,
        moving=(1,),
    )(which, part.reshape(2, 2, 8, 2, 96, 256), w_qkv, gain, *before)


def exchange(x):
    return lax.all_to_all(x, BLK, 0, 0, tiled=True)


def add_rounded(a, b):
    return (a.astype(F32) + b.astype(F32)).astype(BF16)


def among_experts(x):
    return lax.all_to_all(x, CHIPS, 0, 0, tiled=True, axis_index_groups=EXPERT_GROUPS)


def among_chips(x):
    return lax.all_to_all(x, CHIPS, 0, 0, tiled=True)


def shards(
    tokens, lengths, routes, gates, gain_attn, w_qkv, w_out, gain_moe, w_gate_up, w_down, cotangent
):
    core = lax.axis_index("core")
    blk = lax.axis_index(BLK)
    xh, zh = lax.axis_index("xh"), lax.axis_index("zh")
    tok = tokens.reshape(128, 1024)
    dz = cotangent.reshape(128, 1024)
    wgu = w_gate_up.reshape(1024, 1024)
    wdn = w_down.reshape(512, 1024)
    gain_a = gain_attn.reshape(1, 1024)
    gain_m = gain_moe.reshape(1, 1024)

    cos, sin = map(jnp.asarray, rope_tables())
    zl = lax.axis_index("zl").astype(jnp.int32).reshape(1)
    which = core.astype(jnp.int32).reshape(1)
    info = jnp.stack([lax.dynamic_index_in_dim(lengths, zh, 0, False), xh]).astype(jnp.int32)

    def to_partner(part):
        return lax.ppermute(part, "core", SWAP)

    dz_far = lax.ppermute(dz, ("zl", "zh"), Z_PAIRS)
    pos, gate, chosen = plan(routes.transpose(0, 2, 1), gates.transpose(0, 2, 1))
    chosen_far = lax.ppermute(chosen, ("zl", "zh"), Z_PAIRS)
    h, send = pre(
        blk.astype(jnp.int32).reshape(1), tok, gain_a, w_qkv, cos, sin, [hold(chosen)]
    )
    planned = pack(dz, chosen, dz_far, chosen_far, [hold(send)])
    dz_all = lax.all_gather(planned, PLANE).reshape(16, 2, 144, 1024)
    arrived = exchange(send.reshape(32, 96, 128))
    o_part, ot, lse = attend(info, arrived, [corner(planned)])
    h_both = h.reshape(2, 64, 1024)
    h_mine = lax.dynamic_index_in_dim(h_both, zh, 0, keepdims=False)
    h_far = lax.ppermute(lax.dynamic_index_in_dim(h_both, 1 - zh, 0, keepdims=False), "zh", SWAP)
    h_near = jnp.stack([after(h_mine, hold(o_part)), h_far])
    o_recv = exchange(o_part).reshape(2, 8, 2, 32, 128)
    o, y, rows = mid(o_recv, w_out, tok, gain_m, pos, [corner(h_near[1])])
    o_other = to_partner(o)
    x = among_experts(rows).reshape(1536, 1024)

    place = jnp.stack([blk, zh]).astype(jnp.int32)
    dx2, da, deo, hid = expert(place, x, dz_all, wgu, wdn, [corner(o_other)])
    h_near = after(h_near, hold(da))
    h_all = lax.all_gather(h_near, PLANE).reshape(16, 2, 64, 1024)

    dx2_back = among_experts(dx2.reshape(32, 48, 1024))
    outputs = expert_out(place, dz_all, hid, wdn)
    experts_own, experts_send = expert_grad(which, x, da, hid, deo)
    experts_far = to_partner(experts_send)
    early = add_rounded(experts_own[:256], experts_far[:256])
    late = add_rounded(experts_own[256:], experts_far[256:])
    early = add_rounded(early, lax.ppermute(early, "zl", SWAP))
    dy, dbr_own, dbr_send, do = mid_back(
        which, dx2_back, pos, y, gain_m, dz, w_out, [corner(early), hold(outputs)]
    )

    sums = after(outputs.reshape(4096, 1024), hold(dbr_own))
    sums = lax.psum_scatter(sums, PLANE, tiled=True).reshape(2, 128, 1024)
    far = lax.ppermute(sums[1], ("zl", "zh"), Z_PAIRS)


    do_recv = exchange(do.reshape(32, 48, 128))
    out_partial = out_grad(o, o_other, dbr_own, to_partner(dbr_send))
    out_sent = after(out_partial.reshape(64, 16, 512), do_recv)
    late = after(late, hold(out_sent))
    late_far = lax.ppermute(late, "zl", SWAP)
    out_pieces = among_chips(out_sent)
    dqkv, gains = attend_back(info, arrived, do_recv, ot, lse, cos, sin, [hold(out_sent)])

    place = jnp.stack([xh, zh]).astype(jnp.int32)
    qkv_partial = qkv_grad(place, h_all, dqkv, gains)
    late = add_rounded(after(late, hold(qkv_partial)), late_far)
    experts_own = jnp.concatenate([early, late], 0)
    qkv_pieces = lax.all_to_all(
        after(qkv_partial, out_pieces), SAME_COLUMNS, 0, 0, tiled=True
    )
    experts_other = to_partner(experts_own)
    grad_gate_up, grad_down = final_expert(which, experts_own, experts_other)
    copies, gains = add_pieces(qkv_pieces, out_pieces, [corner(late)])
    own = await_all(among_chips(copies), hold(grad_gate_up))
    dqkv_recv = exchange(after(dqkv, corner(own))).reshape(2, 8, 2, 96, 128)
    rows = final(which, own, w_qkv, gain_attn.reshape(8, 128))
    grad_qkv, grad_out, grad_gain_attn = final(
        1 - which, to_partner(own), w_qkv, gain_attn.reshape(8, 128), (rows[2], rows[0], rows[1])
    )
    grad_tokens, mixed = last(
        dqkv_recv, w_qkv, tok, gain_a, dy, y, sums, far, [hold(grad_qkv)]
    )
    return (
        mixed.reshape(2, 64, 1024),
        grad_tokens.reshape(2, 64, 1024),
        grad_gain_attn.reshape(1024),
        grad_qkv,
        grad_out.reshape(1024, 1024),
        gains.reshape(1024),
        grad_gate_up[None],
        grad_down[None],
    )


def solution(mesh):
    split = Mesh(mesh.devices.reshape(2, 2, 2, 2, 4, 2), AXES)
    rows = P(ROWS, BLK, None)
    return jax.shard_map(
        shards,
        mesh=split,
        in_specs=(
            rows,
            P(ROWS),
            rows,
            rows,
            P(),
            P(),
            P(),
            P(),
            P(BLK, None, None),
            P(BLK, None, None),
            rows,
        ),
        out_specs=(
            rows,
            rows,
            P(),
            P(),
            P(),
            P(),
            P(BLK, None, None),
            P(BLK, None, None),
        ),
        check_vma=False,
    )
```

```python
import jax
import jax.numpy as jnp
import numpy as np
from jax import lax
from jax.experimental import pallas as pl
from jax.experimental.pallas import tpu as pltpu
from jax.sharding import Mesh
from jax.sharding import PartitionSpec as P

HEADS = 16
KV_HEADS = 8
HEAD = 64
FF_EXP = 512
TOP = 8
MOST = 24
EPS = 1e-06
ROPE_BASE = 10000.0
SCALE = HEAD ** (-0.5)

ROWS = ("zl", "core")
PLANE = ("xh", "xl", "y")
BLK = ("xh", "xl", "y", "zh")
CHIPS = ("zl", "xh", "xl", "y", "zh")
AXES = ("zl", "core", "xh", "xl", "y", "zh")
SAME_COLUMNS = ("zl", "core", "xh", "zh")
SWAP = [(0, 1), (1, 0)]
EXPERT_GROUPS = [
    [(parity ^ zh) * 32 + xy * 2 + zh for xy in range(16) for zh in range(2)] for parity in range(2)
]
Z_PAIRS = [(i, 3 - i) for i in range(4)]
F32 = jnp.float32
BF16 = jnp.bfloat16
NT = (((1,), (1,)), ((), ()))
TN = (((0,), (0,)), ((), ()))


def rope_tables():
    lane = np.arange(128) % HEAD
    frequency = (ROPE_BASE ** (-(lane % 32) / 32.0)).astype(np.float32)
    angles = np.arange(2048, dtype=np.float32)[:, None] * frequency[None, :]
    sign = np.where(lane < 32, -1.0, 1.0)
    cosine = np.cos(angles.astype(np.float64)).astype(np.float32)
    return cosine, (np.sin(angles.astype(np.float64)) * sign).astype(np.float32)


def dot(left, right, dims=(((1,), (0,)), ((), ()))):
    return lax.dot_general(left, right, dims, preferred_element_type=F32)


def call(
    kernel,
    grid,
    in_specs,
    out_specs,
    out_shape,
    scratch=(),
    mb=24,
    flops=0,
    moved=0,
    deps=(),
    scalars=0,
    aliases=None,
    moving=(),
):
    count = len(in_specs) + scalars

    def place(i, x):
        small = i < scalars or in_specs[i - scalars].memory_space == pltpu.SMEM
        return x if small or i in moving else hold(x)

    def body(*refs):
        kernel(*refs[:count], *refs[count + len(deps) :])

    built = pl.pallas_call(
        body,
        grid_spec=pltpu.PrefetchScalarGridSpec(
            num_scalar_prefetch=scalars,
            grid=grid,
            in_specs=[*in_specs, *[pl.BlockSpec(memory_space=pl.ANY)] * len(deps)],
            out_specs=out_specs,
            scratch_shapes=list(scratch),
        ),
        out_shape=out_shape,
        input_output_aliases=aliases or {},
        compiler_params=pltpu.CompilerParams(vmem_limit_bytes=mb * 1024 * 1024),
        cost_estimate=pl.CostEstimate(flops=flops, bytes_accessed=moved, transcendentals=0),
    )
    return lambda *operands: built(*[place(i, x) for i, x in enumerate(operands)], *deps)


def after(x, *deps):
    any_space = pl.BlockSpec(memory_space=pl.ANY)
    return pl.pallas_call(
        lambda *refs: None,
        in_specs=[any_space] * (1 + len(deps)),
        out_specs=any_space,
        out_shape=sds(x.shape, x.dtype),
        input_output_aliases={0: 0},
        compiler_params=pltpu.CompilerParams(vmem_limit_bytes=1024 * 1024),
    )(hold(x), *deps)


def await_all(x, *deps):
    any_space = pl.BlockSpec(memory_space=pl.ANY)
    return pl.pallas_call(
        lambda *refs: None,
        in_specs=[any_space] * (1 + len(deps)),
        out_specs=any_space,
        out_shape=jax.ShapeDtypeStruct(x.shape, x.dtype),
        input_output_aliases={0: 0},
        compiler_params=pltpu.CompilerParams(vmem_limit_bytes=1024 * 1024),
    )(x, *deps)


def hold(x):
    return pltpu.with_memory_space_constraint(x, pltpu.HBM)


def corner(x):
    return x[(0,) * (x.ndim - 2)][:8, :128]


def whole(*shape):
    return pl.BlockSpec(shape, lambda *_: (0,) * len(shape))


def sds(shape, dtype):
    return pltpu.HBM(shape, dtype)


def low_half(shape):
    return lax.broadcasted_iota(jnp.int32, shape, len(shape) - 1) < HEAD


def swap_halves(u):
    lane = lax.broadcasted_iota(jnp.int32, u.shape, 1)
    return jnp.where(lane % HEAD < HEAD // 2, pltpu.roll(u, 96, 1), pltpu.roll(u, 32, 1))


def pre_kernel(blk, tok, gain, wq, wk, wv, cos, sin, h_ref, send):
    @pl.when(pl.program_id(0) == 0)
    def _():
        x = tok[...].astype(F32)
        inverse = lax.rsqrt(jnp.mean(x * x, axis=-1, keepdims=True) + EPS)
        h_ref[...] = (x * inverse * gain[...]).astype(BF16)

    h = h_ref[...]
    c = jnp.concatenate([cos[...], cos[...]], 0)
    s = jnp.concatenate([sin[...], sin[...]], 0)

    def rope(u):
        return u * c + swap_halves(u) * s

    q = dot(h, wq[...])
    k = rope(dot(h, wk[...]))
    v = dot(h, wv[...])
    low = low_half(k.shape)
    pairs = (
        jnp.where(low, k, pltpu.roll(v, HEAD, 1)).astype(BF16),
        jnp.where(low, pltpu.roll(k, HEAD, 1), v).astype(BF16),
    )
    for j in range(2):
        qj = (rope(q[:, j * 128 : (j + 1) * 128]).astype(BF16).astype(F32) * SCALE).astype(BF16)
        for t in range(2):
            for half in range(2):
                first = t * 64 + half * 32
                send[half, j, t, 0:32, :] = qj[first : first + 32]
                send[half, j, t, 32:96, :] = pairs[j][t * 64 : t * 64 + 64]


def pre(blk, tok, gain, w_qkv, cos, sin, deps):
    places = pl.BlockSpec((64, 128), lambda m, blk: (blk[0], 0))
    return call(
        pre_kernel,
        (4,),
        [
            whole(128, 1024),
            whole(1, 1024),
            pl.BlockSpec((1024, 256), lambda m, blk: (0, m)),
            pl.BlockSpec((1024, 128), lambda m, blk: (0, 8 + m)),
            pl.BlockSpec((1024, 128), lambda m, blk: (0, 12 + m)),
            places,
            places,
        ],
        [whole(128, 1024), pl.BlockSpec((2, 2, 2, 96, 128), lambda m, blk: (0, m, 0, 0, 0))],
        [sds((128, 1024), BF16), sds((2, 8, 2, 96, 128), BF16)],
        flops=2 * 128 * 1024 * 2048,
        moved=5 << 20,
        scalars=1,
        deps=deps,
    )(blk, tok, gain, w_qkv, w_qkv, w_qkv, cos, sin)


def plan_kernel(routes, gates, pos_ref, gate_ref, out):
    named = jnp.concatenate([routes[0], routes[1]], 1).astype(F32)
    weights = jnp.concatenate([gates[0], gates[1]], 1)
    experts = lax.broadcasted_iota(jnp.int32, (32, 128), 0).astype(F32)
    chosen = jnp.zeros((32, 128), F32)
    gate = jnp.zeros((32, 128), F32)
    for k in range(TOP):
        match = named[k : k + 1] == experts
        chosen = jnp.where(match, 1.0, chosen)
        gate = jnp.where(match, weights[k : k + 1], gate)
    row = lax.broadcasted_iota(jnp.int32, (128, 128), 0)
    before = jnp.where(row < lax.broadcasted_iota(jnp.int32, (128, 128), 1), 1.0, 0.0)
    rank = dot(chosen.astype(BF16), before.astype(BF16))
    pos = jnp.where(chosen > 0.0, rank, -1.0)
    pos_ref[...] = pos.astype(jnp.int32)
    gate_ref[...] = gate
    high = gate.astype(BF16).astype(F32)
    rest = gate - high
    for j in range(8):
        part = slice(4 * j, 4 * j + 4)
        tile = jnp.concatenate([pos[part], high[part], rest[part], jnp.zeros((4, 128), F32)], 0)
        out[:, j * 128 : (j + 1) * 128] = tile.astype(BF16)


def plan(routes, gates):
    return call(
        plan_kernel,
        (1,),
        [whole(2, 8, 64), whole(2, 8, 64)],
        [whole(32, 128), whole(32, 128), whole(16, 1024)],
        [sds((32, 128), jnp.int32), sds((32, 128), F32), sds((16, 1024), BF16)],
        moved=1 << 17,
    )(routes, gates)


def pack_kernel(dz, info, dz_far, info_far, out):
    out[0, 0:128, :] = dz[...]
    out[0, 128:144, :] = info[...]
    out[1, 0:128, :] = dz_far[...]
    out[1, 128:144, :] = info_far[...]


def pack(dz, info, dz_far, info_far, deps):
    return call(
        pack_kernel,
        (1,),
        [whole(128, 1024), whole(16, 1024), whole(128, 1024), whole(16, 1024)],
        whole(2, 144, 1024),
        sds((2, 144, 1024), BF16),
        moved=1 << 20,
        moving=(2, 3),
        deps=deps,
    )(dz, info, dz_far, info_far)


def split_queries(q):
    qf = q.astype(F32)
    low = low_half(qf.shape)
    first = jnp.where(low, qf, 0.0)
    second = jnp.where(low, pltpu.roll(qf, HEAD, 1), 0.0)
    return jnp.concatenate([first, second], 0).astype(BF16)


def limits(tile, info):
    place = lax.broadcasted_iota(jnp.int32, (1, 512), 1) % 256
    position = (tile * 8 + place // 32) * 64 + info[1] * 32 + place % 32
    return jnp.minimum(position, info[0] - 1)


def load_pairs(x_ref, kv, kvt):
    kv[...] = x_ref[:, 32:96, :].reshape(2048, 128)
    for c in range(8):
        rows = slice(c * 256, (c + 1) * 256)
        kvt[:, rows] = kv[rows, :].astype(F32).T.astype(BF16)


def attend_kernel(info, x_ref, o_ref, ot_ref, lse_ref, kv, kvt):
    load_pairs(x_ref, kv, kvt)
    for tile in range(4):
        q2 = split_queries(x_ref[tile * 8 : (tile + 1) * 8, 0:32, :].reshape(256, 128))
        limit = limits(tile, info)
        keys = (tile + 1) * 512
        s = dot(kv[0:keys, :], q2, NT)
        place = lax.broadcasted_iota(jnp.int32, (keys, 1), 0)
        s = jnp.where(place <= limit, s, -1e30)
        top = jnp.max(s, axis=0, keepdims=True)
        p = jnp.exp(s - top)
        total = jnp.sum(p, axis=0, keepdims=True)
        out = dot(kvt[64:128, 0:keys], p.astype(BF16)) / total
        ot_ref[tile] = out
        lse_ref[tile] = jnp.broadcast_to(top + jnp.log(total), (8, 512))
        both = jnp.concatenate([out[:, :256], out[:, 256:]], 0).T
        o_ref[tile * 8 : (tile + 1) * 8] = both.astype(BF16).reshape(8, 32, 128)


def attend(info, arrived, deps):
    return call(
        attend_kernel,
        (1,),
        [pl.BlockSpec(memory_space=pltpu.SMEM), whole(32, 96, 128)],
        [whole(32, 32, 128), whole(4, 64, 512), whole(4, 8, 512)],
        [sds((32, 32, 128), BF16), sds((4, 64, 512), F32), sds((4, 8, 512), F32)],
        [pltpu.VMEM((2048, 128), BF16), pltpu.VMEM((128, 2048), BF16)],
        flops=4 * 2048 * 1280 * 128,
        moved=2 << 20,
        deps=deps,
        moving=(1,),
    )(info, arrived)


def attend_back_kernel(
    info, x_ref, do_ref, ot_ref, lse_ref, cos, sin, out_ref, gain_ref, kv, kvt, total
):
    load_pairs(x_ref, kv, kvt)
    total[...] = jnp.zeros_like(total)
    for tile in range(4):
        q2 = split_queries(x_ref[tile * 8 : (tile + 1) * 8, 0:32, :].reshape(256, 128))
        grad = do_ref[tile * 8 : (tile + 1) * 8, 0:32, :].reshape(256, 128).astype(F32)
        low = low_half(grad.shape)
        do2 = jnp.concatenate(
            [jnp.where(low, 0.0, pltpu.roll(grad, HEAD, 1)), jnp.where(low, 0.0, grad)], 0
        ).astype(BF16)
        grad_t = grad.T
        grad_t = jnp.concatenate([grad_t[:64], grad_t[64:]], 1)
        inner = jnp.sum(grad_t * ot_ref[tile], axis=0, keepdims=True)
        lse = lse_ref[tile][0:1]
        limit = limits(tile, info)

        acc = jnp.zeros((64, 512), F32)
        for c in range(tile + 1):
            at = slice(c * 512, c * 512 + 512)
            part = kv[at, :]
            s = dot(part, q2, NT)
            place = c * 512 + lax.broadcasted_iota(jnp.int32, (512, 1), 0)
            p = jnp.exp(jnp.where(place <= limit, s, -1e30) - lse)
            ds = (p * (dot(part, do2, NT) - inner)).astype(BF16)
            total[at, :] += dot(ds, q2) + dot(p.astype(BF16), do2)
            acc = acc + dot(kvt[0:64, at], ds)
        dq = jnp.concatenate([acc[:, :256], acc[:, 256:]], 0).T
        at = (slice(tile * 8, tile * 8 + 8), pl.ds(pl.multiple_of(info[1] * 32, 32), 32))
        c, s = cos[at].reshape(256, 128), sin[at].reshape(256, 128)
        dq = ((dq * c - swap_halves(dq) * s) * SCALE).astype(BF16)
        out_ref[tile * 8 : (tile + 1) * 8, 0:32, :] = dq.reshape(8, 32, 128)
    for tile in range(4):
        blocks = slice(tile * 8, tile * 8 + 8)
        part = total[tile * 512 : (tile + 1) * 512, :]
        turned = part * cos[blocks].reshape(512, 128) - swap_halves(part) * sin[
            blocks
        ].reshape(512, 128)
        part = jnp.where(low_half(part.shape), turned, part)
        out_ref[blocks, 32:96, :] = part.astype(BF16).reshape(8, 64, 128)
    gains = jnp.sum(do_ref[:, 32:48, :].astype(F32), axis=0)
    gain_ref[...] = gains[:8] + gains[8:]


def attend_back(info, arrived, grad, ot, lse, cos, sin, deps):
    return call(
        attend_back_kernel,
        (1,),
        [
            pl.BlockSpec(memory_space=pltpu.SMEM),
            whole(32, 96, 128),
            whole(32, 48, 128),
            whole(4, 64, 512),
            whole(4, 8, 512),
            whole(32, 64, 128),
            whole(32, 64, 128),
        ],
        [whole(32, 96, 128), whole(8, 128)],
        [sds((32, 96, 128), BF16), sds((8, 128), F32)],
        [pltpu.VMEM((2048, 128), BF16), pltpu.VMEM((128, 2048), BF16), pltpu.VMEM((2048, 128), F32)],
        flops=10 * 2048 * 1280 * 128,
        moved=3 << 20,
        deps=deps,
        moving=(1, 2,),
    )(info, arrived, grad, ot, lse, cos.reshape(32, 64, 128), sin.reshape(32, 64, 128))


def placement(pos):
    shape = (pos.shape[0], 48, 128)
    slots = lax.broadcasted_iota(jnp.int32, shape, 1)
    return (pos[...][:, None, :] == slots).reshape(shape[0] * 48, 128)


def gated(pos, gate):
    placed = placement(pos)
    weight = jnp.broadcast_to(gate[...][:, None, :], (pos.shape[0], 48, 128))
    weight = jnp.where(placed, weight.reshape(placed.shape), 0.0)
    high = weight.astype(BF16)
    return high, (weight - high.astype(F32)).astype(BF16)


PLACE = pl.BlockSpec((16, 128), lambda e: (e, 0))
SLOTS = pl.BlockSpec((16, 48, 1024), lambda e: (e, 0, 0))


def mid_kernel(recv, w0, w1, w2, w3, tok, gain, pos, o_ref, y_ref, out, h2):
    @pl.when(pl.program_id(0) == 0)
    def _():
        for s in range(2):
            for half in range(2):
                first = s * 64 + half * 32
                for m in range(8):
                    o_ref[first : first + 32, m * 128 : (m + 1) * 128] = recv[half, m, s]
        o = o_ref[...]
        branch = jnp.concatenate([dot(o, w[...]) for w in (w0, w1, w2, w3)], 1)
        y = tok[...].astype(F32) + branch
        y_ref[...] = y
        inverse = lax.rsqrt(jnp.mean(y * y, axis=-1, keepdims=True) + EPS)
        h2[...] = (y * inverse * gain[...]).astype(BF16)

    placed = placement(pos).astype(F32).astype(BF16)
    out[...] = dot(placed, h2[...]).astype(BF16).reshape(out.shape)


def mid(recv, w_out, tok, gain, pos, deps):
    return call(
        mid_kernel,
        (2,),
        [
            whole(2, 8, 2, 32, 128),
            *[pl.BlockSpec((1024, 256), lambda e, j=j: (0, j)) for j in range(4)],
            whole(128, 1024),
            whole(1, 1024),
            PLACE,
        ],
        [whole(128, 1024), whole(128, 1024), SLOTS],
        [sds((128, 1024), BF16), sds((128, 1024), F32), sds((32, 48, 1024), BF16)],
        [pltpu.VMEM((128, 1024), BF16)],
        flops=2 * 128 * 1024 * 1024 + 2 * 1536 * 128 * 1024,
        moved=6 << 20,
        moving=(0,),
        deps=deps,
    )(recv, w_out, w_out, w_out, w_out, tok, gain, pos)


def expert_kernel(which, x_ref, info, dz, g0, g1, u0, u1, d0, d1, dx2, da_ref, deo_ref, hid_ref):
    slots = lax.broadcasted_iota(jnp.int32, (48, 128), 0).astype(F32)
    rows16 = lax.broadcasted_iota(jnp.int32, (16, 128), 0)
    blank = jnp.zeros((48, 128), F32)
    mine = which[0] % 4
    for pair in range(PLACES):
        parts, weights = [], []
        for j in range(2):
            tile = info[pair, j].astype(F32)

            def pick(k):
                return jnp.sum(jnp.where(rows16 == mine + 4 * k, tile, 0.0), axis=0, keepdims=True)

            hot = jnp.where(slots == pick(0), 1.0, 0.0)
            weights.append(jnp.sum(hot * (pick(1) + pick(2)), axis=1, keepdims=True))
            parts.append(jnp.concatenate([hot, blank] if j == 0 else [blank, hot], 1))
        rows = dot(jnp.concatenate(parts, 0).astype(BF16), dz[pair].reshape(256, 1024))
        rows = (rows * jnp.concatenate(weights, 0)).astype(BF16)
        for j in range(2):
            first = pl.multiple_of(pair * 96 + (which[1] ^ j) * 48, 48)
            deo_ref[pl.ds(first, 48), :] = rows[j * 48 : (j + 1) * 48]
    x, deo = x_ref[...], deo_ref[...]
    for part, (wg, wu) in enumerate(((g0, u0), (g1, u1))):
        at = slice(part * 256, part * 256 + 256)
        late = slice(part * 256 + FF_EXP, part * 256 + FF_EXP + 256)
        gate, up = dot(x, wg[...]), dot(x, wu[...])
        dhid = dot(deo[:, :512], d0[at, :], NT) + dot(deo[:, 512:], d1[at, :], NT)
        sig = jax.nn.sigmoid(gate)
        act = gate * sig
        hid_ref[:, at] = (act * up).astype(BF16)
        da_ref[:, at] = (dhid * up * sig * (1.0 + gate * (1.0 - sig))).astype(BF16)
        da_ref[:, late] = (dhid * act).astype(BF16)
    total = dot(da_ref[:, 0:256], g0[...], NT) + dot(da_ref[:, 256:512], g1[...], NT)
    total += dot(da_ref[:, 512:768], u0[...], NT) + dot(da_ref[:, 768:1024], u1[...], NT)
    dx2[...] = total.astype(BF16)


PLACES = 4


def expert(which, x, dz_all, wgu, wdn, deps):
    count = PLACES * 96
    rows = pl.BlockSpec((count, 1024), lambda i, which: (i, 0))
    return call(
        expert_kernel,
        (16 // PLACES,),
        [
            rows,
            pl.BlockSpec((PLACES, 2, 16, 128), lambda i, which: (i, 0, 8, which[0] // 4)),
            pl.BlockSpec((PLACES, 2, 128, 1024), lambda i, which: (i, 0, 0, 0)),
            *[pl.BlockSpec((1024, 256), lambda i, which, j=j: (0, j)) for j in range(4)],
            *[pl.BlockSpec((512, 512), lambda i, which, j=j: (0, j)) for j in range(2)],
        ],
        [rows, rows, rows, pl.BlockSpec((count, 512), lambda i, which: (i, 0))],
        [*[sds((1536, 1024), BF16)] * 3, sds((1536, 512), BF16)],
        mb=32,
        flops=2 * 1536 * 1024 * 2816,
        moved=26 << 20,
        scalars=1,
        moving=(1,),
        deps=deps,
    )(which, x, dz_all, dz_all, wgu, wgu, wgu, wgu, wdn, wdn)


def expert_out_kernel(which, info, hid, d0, d1, out):
    slots = lax.broadcasted_iota(jnp.int32, (48, 128), 0).astype(F32)
    rows16 = lax.broadcasted_iota(jnp.int32, (16, 128), 0)
    mine = which[0] % 4
    eo = jnp.concatenate([dot(hid[...], d0[...]), dot(hid[...], d1[...])], 1).astype(BF16)
    for place in range(4):
        for zh in range(2):
            tile = info[place, which[1] ^ zh].astype(F32)

            def pick(k):
                return jnp.sum(jnp.where(rows16 == mine + 4 * k, tile, 0.0), axis=0, keepdims=True)

            hot = jnp.where(slots == pick(0), 1.0, 0.0)
            gate = jnp.concatenate([hot * pick(1), hot * pick(2)], 0).astype(BF16)
            first = place * 96 + zh * 48
            rows = eo[first : first + 48]
            product = dot(gate, jnp.concatenate([rows, rows], 0), TN)
            out[place, which[1] ^ zh] = product.astype(BF16)


def expert_out(which, dz_all, hid, wdn):
    return call(
        expert_out_kernel,
        (4,),
        [
            pl.BlockSpec((4, 2, 16, 128), lambda i, which: (i, 0, 8, which[0] // 4)),
            pl.BlockSpec((384, 512), lambda i, which: (i, 0)),
            *[pl.BlockSpec((512, 512), lambda i, which, j=j: (0, j)) for j in range(2)],
        ],
        pl.BlockSpec((4, 2, 128, 1024), lambda i, which: (i, 0, 0, 0)),
        sds((16, 2, 128, 1024), BF16),
        flops=2 * 1536 * 1024 * 512 + 4 * 1536 * 128 * 1024,
        moved=12 << 20,
        scalars=1,
    )(which, dz_all, hid, wdn, wdn)


def expert_grad_kernel(core, x_ref, da, hid, deo, own, other):
    step = pl.program_id(0)

    for first, out in ((0, own), (3, other)):

        @pl.when((step >= first) & (step < first + 2))
        def _():
            out[...] = dot(x_ref[...], da[...], TN).astype(BF16)

        @pl.when(step == first + 2)
        def _():
            out[...] = dot(hid[...], deo[...], TN).astype(BF16)


def expert_grad(core, x, da, hid, deo):
    def half(i, core):
        return jnp.where(i < 3, core[0], 1 - core[0])

    return call(
        expert_grad_kernel,
        (6,),
        [
            pl.BlockSpec((1536, 256), lambda i, c: (0, half(i, c) * 2 + jnp.minimum(i % 3, 1))),
            whole(1536, 1024),
            pl.BlockSpec((1536, 256), lambda i, c: (0, half(i, c))),
            whole(1536, 1024),
        ],
        [
            pl.BlockSpec((256, 1024), lambda i, c: (jnp.minimum(i, 2), 0)),
            pl.BlockSpec((256, 1024), lambda i, c: (jnp.maximum(i - 3, 0), 0)),
        ],
        [sds((768, 1024), BF16)] * 2,
        flops=2 * 1536 * 1024 * 1536,
        moved=16 << 20,
        scalars=1,
        moving=(1,),
    )(core, x, da, hid, deo)


def final_expert_kernel(core, own, other, gate_up, down):
    step = pl.program_id(0)
    half = jnp.where(step < 4, step // 2, step - 4)

    def write(out):
        @pl.when(half == core[0])
        def _():
            out[...] = own[...].astype(F32)

        @pl.when(half != core[0])
        def _():
            out[...] = other[...].astype(F32)

    @pl.when(step < 4)
    def _():
        write(gate_up)

    @pl.when(step >= 4)
    def _():
        write(down)


def final_expert(core, own, other):
    part = pl.BlockSpec((256, 1024), lambda i: (jnp.where(i < 4, i % 2, 2), 0))
    return call(
        final_expert_kernel,
        (6,),
        [pl.BlockSpec(memory_space=pltpu.SMEM), part, part],
        [
            pl.BlockSpec((256, 1024), lambda i: (jnp.minimum(i, 3), 0)),
            pl.BlockSpec((256, 1024), lambda i: (jnp.maximum(i - 4, 0), 0)),
        ],
        [sds((1024, 1024), F32), sds((512, 1024), F32)],
        moved=9 << 20,
        moving=(1, 2,),
    )(core, own, other)


def norm_back(incoming, gain, vectors):
    inverse = lax.rsqrt(jnp.mean(vectors * vectors, axis=-1, keepdims=True) + EPS)
    scaled = vectors * inverse
    weighted = incoming * gain
    mean = jnp.mean(weighted * scaled, axis=-1, keepdims=True)
    return inverse * (weighted - scaled * mean), scaled


def mid_back_kernel(
    core, back, pos, y, gain, dz, w0, w1, w2, w3, dy_ref, own, other, send
):
    placed = placement(pos).astype(F32).astype(BF16)
    dh2 = dot(placed, back[...].reshape(1536, 1024), TN)
    dv, scaled = norm_back(dh2, gain[...], y[...])
    gains = jnp.sum(dh2 * scaled, axis=0, keepdims=True)
    row = lax.broadcasted_iota(jnp.int32, (8, 128), 0)
    tile = jnp.zeros((8, 128), F32)
    for r in range(8):
        tile = jnp.where(row == r, gains[:, r * 128 : (r + 1) * 128], tile)
    high = tile.astype(BF16).astype(F32)
    extra = jnp.concatenate([high, tile - high], 0).astype(BF16)
    dy = dz[...].astype(F32) + dv
    dy_ref[...] = dy
    dbr = dy.astype(BF16)

    @pl.when(core[0] == 0)
    def _():
        own[...] = dbr[:, :512]
        other[...] = dbr[:, 512:]

    @pl.when(core[0] == 1)
    def _():
        own[...] = dbr[:, 512:]
        other[...] = dbr[:, :512]

    do = jnp.concatenate([dot(dbr, w[...], NT) for w in (w0, w1, w2, w3)], 1).astype(BF16)
    for s in range(2):
        for half in range(2):
            first = s * 64 + half * 32
            for m in range(8):
                send[half, m, s, 0:32, :] = do[first : first + 32, m * 128 : (m + 1) * 128]
                send[half, m, s, 32:48, :] = extra


def mid_back(core, back, pos, y, gain, dz, w_out, deps):
    return call(
        mid_back_kernel,
        (1,),
        [
            pl.BlockSpec(memory_space=pltpu.SMEM),
            whole(32, 48, 1024),
            whole(32, 128),
            whole(128, 1024),
            whole(1, 1024),
            whole(128, 1024),
            *[pl.BlockSpec((256, 1024), lambda e, j=j: (j, 0)) for j in range(4)],
        ],
        [whole(128, 1024), whole(128, 512), whole(128, 512), whole(2, 8, 2, 48, 128)],
        [
            sds((128, 1024), F32),
            sds((128, 512), BF16),
            sds((128, 512), BF16),
            sds((2, 8, 2, 48, 128), BF16),
        ],
        flops=2 * 128 * 1024 * 1024 + 2 * 1536 * 128 * 1024,
        moved=6 << 20,
        deps=deps,
        moving=(1,),
    )(core, back, pos, y, gain, dz, w_out, w_out, w_out, w_out)


def last_kernel(
    recv, w0, w1, w2, w3, tok, gain, dy, y, near, far, grad_tokens, mixed, dproj
):
    mixed[...] = (y[...] + near[0].astype(F32) + far[...].astype(F32)).astype(BF16)
    low = low_half((64, 128))
    for t in range(2):
        rows = slice(t * 64, t * 64 + 64)
        for mm in range(4):
            both = []
            for j in range(2):
                m = 2 * mm + j
                dq = jnp.concatenate([recv[0, m, t, 0:32, :], recv[1, m, t, 0:32, :]], 0)
                dproj[rows, m * 128 : (m + 1) * 128] = dq
                both.append(
                    recv[0, m, t, 32:96, :].astype(F32) + recv[1, m, t, 32:96, :].astype(F32)
                )
            dk = jnp.where(low, both[0], pltpu.roll(both[1], HEAD, 1))
            dv = jnp.where(low, pltpu.roll(both[0], HEAD, 1), both[1])
            dproj[rows, 1024 + mm * 128 : 1152 + mm * 128] = dk.astype(BF16)
            dproj[rows, 1536 + mm * 128 : 1664 + mm * 128] = dv.astype(BF16)
    d = dproj[...]
    dh = jnp.concatenate([dot(d, w[...], NT) for w in (w0, w1, w2, w3)], 1)
    dv, _ = norm_back(dh, gain[...], tok[...].astype(F32))
    grad_tokens[...] = dy[...] + dv


def last(recv, w_qkv, tok, gain, dy, y, sums, far, deps):
    return call(
        last_kernel,
        (1,),
        [
            whole(2, 8, 2, 96, 128),
            *[pl.BlockSpec((256, 2048), lambda _, j=j: (j, 0)) for j in range(4)],
            whole(128, 1024),
            whole(1, 1024),
            whole(128, 1024),
            whole(128, 1024),
            pl.BlockSpec((1, 128, 1024), lambda _: (0, 0, 0)),
            whole(128, 1024),
        ],
        [whole(128, 1024), whole(128, 1024)],
        [sds((128, 1024), F32), sds((128, 1024), BF16)],
        [pltpu.VMEM((128, 2048), BF16)],
        flops=2 * 128 * 1024 * 2048,
        moved=6 << 20,
        deps=deps,
        moving=(0, 9, 10),
    )(recv, w_qkv, w_qkv, w_qkv, w_qkv, tok, gain, dy, y, sums, far)


def qkv_grad_kernel(place, h_all, d_ref, gains, out, rows, acc):
    step = pl.program_id(0)
    for pair in range(4):
        for zh in range(2):
            first = (pair * 2 + zh) * 64
            rows[first : first + 64, :] = h_all[pair, place[1] ^ zh]
    dq = d_ref[:, 0:32, :]
    none = jnp.zeros_like(dq)
    dq = jnp.where(place[0] == 0, jnp.concatenate([dq, none], 1), jnp.concatenate([none, dq], 1))
    both = jnp.concatenate([dq.reshape(512, 128), d_ref[:, 32:96, :].reshape(512, 128)], 1)
    product = dot(rows[...], both, TN)

    @pl.when(step == 0)
    def _():
        acc[...] = product

    @pl.when((step > 0) & (step < 3))
    def _():
        acc[...] += product

    @pl.when(step == 3)
    def _():
        out[:, 0:64, :] = (acc[...] + product).astype(BF16).reshape(16, 64, 256)
        high = gains[...].astype(BF16).astype(F32)
        tile = jnp.concatenate([high, gains[...] - high], 1)
        tile = jnp.concatenate([tile, jnp.zeros_like(tile)], 0).astype(BF16)
        out[:, 64:80, :] = jnp.broadcast_to(tile[None], (16, 16, 256))


def qkv_grad(place, h_all, dqkv, gains):
    return call(
        qkv_grad_kernel,
        (4,),
        [
            pl.BlockSpec((4, 2, 64, 1024), lambda i, place: (i, 0, 0, 0)),
            pl.BlockSpec((8, 96, 128), lambda i, place: (i, 0, 0)),
            whole(8, 128),
        ],
        whole(16, 80, 256),
        sds((16, 80, 256), BF16),
        [pltpu.VMEM((512, 1024), BF16), pltpu.VMEM((1024, 256), F32)],
        flops=2 * 2048 * 1024 * 256,
        moved=6 << 20,
        scalars=1,
    )(place, h_all, dqkv, gains)


def out_grad_kernel(left, left2, right, right2, out):
    a = jnp.concatenate([left[...], left2[...]], 0)
    b = jnp.concatenate([right[...], right2[...]], 0)
    out[...] = dot(a, b, TN).astype(BF16)


def out_grad(left, left2, right, right2):
    thin = pl.BlockSpec((128, 256), lambda i: (0, i))
    return call(
        out_grad_kernel,
        (4,),
        [thin, thin, whole(128, 512), whole(128, 512)],
        pl.BlockSpec((256, 512), lambda i: (i, 0)),
        sds((1024, 512), BF16),
        flops=2 * 256 * 1024 * 512,
        moved=3 << 20,
        moving=(1, 3),
    )(left, left2, right, right2)


def add_pieces_kernel(qkv, out_w, out, gains):
    total = jnp.sum(qkv[:, 0:64, :].astype(F32), axis=0).astype(BF16)
    out[:, 0:64, :] = jnp.broadcast_to(total[None], (32, 64, 256))
    other = jnp.sum(out_w[...].astype(F32), axis=0).astype(BF16)
    out[:, 64:80, :] = jnp.broadcast_to(other[None, :, :256], (32, 16, 256))
    out[:, 80:96, :] = jnp.broadcast_to(other[None, :, 256:], (32, 16, 256))
    parts = [qkv[row, 64:80, :].astype(F32)[:8] for row in (0, 4, 8, 12)]
    parts = [part[:, :128] + part[:, 128:] for part in parts]
    gains[...] = parts[0] + parts[1] + parts[2] + parts[3]


def add_pieces(qkv, out_w, deps):
    return call(
        add_pieces_kernel,
        (2,),
        [whole(16, 80, 256), whole(64, 16, 512)],
        [pl.BlockSpec((32, 96, 256), lambda i: (i, 0, 0)), whole(8, 128)],
        [sds((64, 96, 256), BF16), sds((8, 128), F32)],
        moved=5 << 20,
        moving=(0, 1),
        deps=deps,
    )(qkv, out_w)


def row_sums(product):
    total = jnp.sum(product, axis=-1, keepdims=True)
    return jnp.broadcast_to(total, (128, 128)).T[0:1]


def final_kernel(which, part, w_qkv, gain, *refs):
    out, out_w, gain_ref = refs[-3:]
    step = pl.program_id(0)
    low = low_half((64, 128))
    for zh in range(2):
        rows = slice(zh * 64, zh * 64 + 64)
        for mm in range(4):
            both = []
            for j in range(2):
                m = 2 * mm + j
                out[rows, m * 128 : (m + 1) * 128] = part[0, 0, m, zh, 0:64, 0:128].astype(F32)
                both.append(part[0, 0, m, zh, 0:64, 128:256].astype(F32))
            out[rows, 1024 + mm * 128 : 1152 + mm * 128] = jnp.where(
                low, both[0], pltpu.roll(both[1], HEAD, 1)
            )
            out[rows, 1536 + mm * 128 : 1664 + mm * 128] = jnp.where(
                low, pltpu.roll(both[0], HEAD, 1), both[1]
            )
        for m in range(8):
            out_w[0, m, zh, :, 0:256] = part[0, 0, m, zh, 64:80, :].astype(F32)
            out_w[0, m, zh, :, 256:512] = part[0, 0, m, zh, 80:96, :].astype(F32)

    @pl.when(step == 0)
    def _():
        gain_ref[...] = gain[...] if len(refs) == 3 else refs[0][...]

    at = pl.ds(step // 2 * 4 + which[0] * 2 + step % 2, 1)
    sums = row_sums(out[...] * w_qkv[...].astype(F32))
    gain_ref[at, :] = sums / gain[at, :]


def final(which, part, w_qkv, gain, before=()):
    def rows(i, which):
        return (i // 2 * 4 + which[0] * 2 + i % 2, 0)

    wide = pl.BlockSpec((128, 2048), rows)
    any_space = pl.BlockSpec(memory_space=pl.ANY)
    return call(
        final_kernel,
        (4,),
        [
            pl.BlockSpec((1, 1, 8, 2, 96, 256), lambda i, which: (i // 2, i % 2, 0, 0, 0, 0)),
            wide,
            whole(8, 128),
            *([whole(8, 128), any_space, any_space] if before else []),
        ],
        [
            wide,
            pl.BlockSpec((1, 8, 2, 16, 512), lambda i, which: (i, 0, 0, 0, which[0])),
            whole(8, 128),
        ],
        [sds((1024, 2048), F32), sds((4, 8, 2, 16, 1024), F32), sds((8, 128), F32)],
        moved=16 << 20,
        scalars=1,
        aliases={5: 0, 6: 1} if before else None,
        moving=(1,),
    )(which, part.reshape(2, 2, 8, 2, 96, 256), w_qkv, gain, *before)


def exchange(x):
    return lax.all_to_all(x, BLK, 0, 0, tiled=True)


def add_rounded(a, b):
    return (a.astype(F32) + b.astype(F32)).astype(BF16)


def among_experts(x):
    return lax.all_to_all(x, CHIPS, 0, 0, tiled=True, axis_index_groups=EXPERT_GROUPS)


def among_chips(x):
    return lax.all_to_all(x, CHIPS, 0, 0, tiled=True)


def shards(
    tokens, lengths, routes, gates, gain_attn, w_qkv, w_out, gain_moe, w_gate_up, w_down, cotangent
):
    core = lax.axis_index("core")
    blk = lax.axis_index(BLK)
    xh, zh = lax.axis_index("xh"), lax.axis_index("zh")
    tok = tokens.reshape(128, 1024)
    dz = cotangent.reshape(128, 1024)
    wgu = w_gate_up.reshape(1024, 1024)
    wdn = w_down.reshape(512, 1024)
    gain_a = gain_attn.reshape(1, 1024)
    gain_m = gain_moe.reshape(1, 1024)

    cos, sin = map(jnp.asarray, rope_tables())
    zl = lax.axis_index("zl").astype(jnp.int32).reshape(1)
    which = core.astype(jnp.int32).reshape(1)
    info = jnp.stack([lax.dynamic_index_in_dim(lengths, zh, 0, False), xh]).astype(jnp.int32)

    def to_partner(part):
        return lax.ppermute(part, "core", SWAP)

    dz_far = lax.ppermute(dz, ("zl", "zh"), Z_PAIRS)
    pos, gate, chosen = plan(routes.transpose(0, 2, 1), gates.transpose(0, 2, 1))
    chosen_far = lax.ppermute(chosen, ("zl", "zh"), Z_PAIRS)
    h, send = pre(
        blk.astype(jnp.int32).reshape(1), tok, gain_a, w_qkv, cos, sin, [hold(chosen)]
    )
    planned = pack(dz, chosen, dz_far, chosen_far, [hold(send)])
    dz_all = lax.all_gather(planned, PLANE).reshape(16, 2, 144, 1024)
    arrived = exchange(send.reshape(32, 96, 128))
    o_part, ot, lse = attend(info, arrived, [corner(planned)])
    h_both = h.reshape(2, 64, 1024)
    h_mine = lax.dynamic_index_in_dim(h_both, zh, 0, keepdims=False)
    h_far = lax.ppermute(lax.dynamic_index_in_dim(h_both, 1 - zh, 0, keepdims=False), "zh", SWAP)
    h_near = jnp.stack([after(h_mine, hold(o_part)), h_far])
    o_recv = exchange(o_part).reshape(2, 8, 2, 32, 128)
    o, y, rows = mid(o_recv, w_out, tok, gain_m, pos, [corner(h_near[1])])
    o_other = to_partner(o)
    x = among_experts(rows).reshape(1536, 1024)

    place = jnp.stack([blk, zh]).astype(jnp.int32)
    dx2, da, deo, hid = expert(place, x, dz_all, wgu, wdn, [corner(o_other)])
    h_near = after(h_near, hold(da))
    h_all = lax.all_gather(h_near, PLANE).reshape(16, 2, 64, 1024)

    dx2_back = among_experts(dx2.reshape(32, 48, 1024))
    outputs = expert_out(place, dz_all, hid, wdn)
    experts_own, experts_send = expert_grad(which, x, da, hid, deo)
    experts_far = to_partner(experts_send)
    early = add_rounded(experts_own[:256], experts_far[:256])
    late = add_rounded(experts_own[256:], experts_far[256:])
    early = add_rounded(early, lax.ppermute(early, "zl", SWAP))
    dy, dbr_own, dbr_send, do = mid_back(
        which, dx2_back, pos, y, gain_m, dz, w_out, [corner(early), hold(outputs)]
    )

    sums = after(outputs.reshape(4096, 1024), hold(dbr_own))
    sums = lax.psum_scatter(sums, PLANE, tiled=True).reshape(2, 128, 1024)


    do_recv = exchange(do.reshape(32, 48, 128))
    out_partial = out_grad(o, o_other, dbr_own, to_partner(dbr_send))
    out_sent = after(out_partial.reshape(64, 16, 512), do_recv)
    late = after(late, hold(out_sent))
    late_far = lax.ppermute(late, "zl", SWAP)
    out_pieces = among_chips(out_sent)
    dqkv, gains = attend_back(info, arrived, do_recv, ot, lse, cos, sin, [hold(out_sent)])

    place = jnp.stack([xh, zh]).astype(jnp.int32)
    qkv_partial = qkv_grad(place, h_all, dqkv, gains)
    late = add_rounded(after(late, hold(qkv_partial)), late_far)
    experts_own = jnp.concatenate([early, late], 0)
    qkv_pieces = lax.all_to_all(
        after(qkv_partial, out_pieces), SAME_COLUMNS, 0, 0, tiled=True
    )
    experts_other = to_partner(experts_own)
    grad_gate_up, grad_down = final_expert(which, experts_own, experts_other)
    copies, gains = add_pieces(qkv_pieces, out_pieces, [corner(late)])
    own = await_all(among_chips(copies), hold(grad_gate_up))
    dqkv_recv = exchange(after(dqkv, corner(own))).reshape(2, 8, 2, 96, 128)
    rows = final(which, own, w_qkv, gain_attn.reshape(8, 128))
    sums = await_all(sums, hold(rows[0]))
    far = lax.ppermute(sums[1], ("zl", "zh"), Z_PAIRS)
    grad_qkv, grad_out, grad_gain_attn = final(
        1 - which, to_partner(own), w_qkv, gain_attn.reshape(8, 128), (rows[2], rows[0], rows[1])
    )
    grad_tokens, mixed = last(
        dqkv_recv, w_qkv, tok, gain_a, dy, y, sums, far, [hold(grad_qkv)]
    )
    return (
        mixed.reshape(2, 64, 1024),
        grad_tokens.reshape(2, 64, 1024),
        grad_gain_attn.reshape(1024),
        grad_qkv,
        grad_out.reshape(1024, 1024),
        gains.reshape(1024),
        grad_gate_up[None],
        grad_down[None],
    )


def solution(mesh):
    split = Mesh(mesh.devices.reshape(2, 2, 2, 2, 4, 2), AXES)
    rows = P(ROWS, BLK, None)
    return jax.shard_map(
        shards,
        mesh=split,
        in_specs=(
            rows,
            P(ROWS),
            rows,
            rows,
            P(),
            P(),
            P(),
            P(),
            P(BLK, None, None),
            P(BLK, None, None),
            rows,
        ),
        out_specs=(
            rows,
            rows,
            P(),
            P(),
            P(),
            P(),
            P(BLK, None, None),
            P(BLK, None, None),
        ),
        check_vma=False,
    )
```
